128 devices in a mesh: lat: 16 (over x, z), wave: 8 (over y, core).
Axes of the slice: x: 4, y: 4, z: 4, core: 2. Of those that a mesh axis runs over, the one named last changes fastest.
Arguments:
- spectra: bfloat16 [16, 2, 640, 640], P('lat', None, 'wave'), may hold values from -6 to 6
- legendre: bfloat16 [640, 2560, 640], P('wave', 'lat'), may hold values from -0.25 to 0.25
- wave_order: int32 [640], replicated, may hold values from 0 to 639, as said below
- writer_order: int32 [16], replicated, may hold values from 0 to 15, each once
Outputs:
- coefficients: bfloat16 [16, 2560, 5120], P('wave', 'lat')
The draws below stay inside these ranges and needn't reach their ends.
Inputs may be any that keep to these rules, and one draw needn't show every extreme that they name: `wave_order`: a permutation of 0 to 639; for every q, slots 2q and 2q+1 hold wavenumbers m and 639-m with m < 320.
All inputs are finite; a program needn't handle non-finite values.
Results may differ from the reference program's by a relative error of at most 0.0056.
Values may be sent and summed in bfloat16 or wider, within the bound.
No kernel may reach another device: no remote copies, remote signals or barrier semaphores. Data moves between devices by JAX's collectives and lax.ppermute only.
A program may use at most 192 MiB of HBM per device.

```python
import math
import jax
import jax.numpy as jnp
from jax import lax

NLATG = 2560
NLON = 5120
M1 = 640
NN = 640
WL = 5
FL = 16


def draw_wave_order(key, part):
    lower = jax.random.permutation(key, M1 // 2).astype(jnp.int32)
    upper = (M1 - 1 - lower).astype(jnp.int32)
    return jnp.stack([lower, upper], axis=1).reshape(M1).astype(jnp.int32)


def shard_levels(stream_key, dims, split, least, high):
    factor_of, own = 1.0, jax.random.fold_in(stream_key, 6)
    for position, blocks in split:
        draws = jnp.exp(jax.random.uniform(jax.random.fold_in(own, position), (blocks,), jnp.float32, least / len(split), high / len(split)))
        factor_of = factor_of * jnp.repeat(draws, dims[position] // blocks).reshape([-1 if axis == position else 1 for axis in range(len(dims))])
    return factor_of


def scatter_about(own_key, shape, deviation, limit, split=(), kind=jnp.bfloat16):
    array = deviation * jax.random.normal(own_key, shape, jnp.float32)
    if split:
        array = array * shard_levels(own_key, shape, split, -0.22, 0.18)
    return jnp.clip(array, -limit, limit).astype(kind)


def setup_inputs(seed: int = 0) -> dict:
    keys = jax.random.split(jax.random.key(seed), 5)
    return {
        "spectra": scatter_about(keys[0], (FL, 2, M1, NN), 1.0, 6.0, ((0, 16), (2, 8))),
        "legendre": scatter_about(keys[1], (M1, NLATG, NN), NN ** -0.5, 0.25, ((0, 8), (1, 16))),
        "wave_order": draw_wave_order(jax.random.fold_in(keys[4], 71), 0),
        "writer_order": jax.random.permutation(keys[3], FL).astype(jnp.int32),
    }


LIFT_ALPHA = -1.586134342059924
LIFT_BETA = -0.052980118572961
LIFT_GAMMA = 0.882911075530934
LIFT_DELTA = 0.443506852043971
LIFT_KAPPA = 1.149604398860241

def trimmed(values, lower, upper, along):
    return lax.slice_in_dim(values, lower, values.shape[along] - upper, 1, along)

def lifting(extended, along):
    length = extended.shape[along]
    even_rows = lax.slice_in_dim(extended, 0, length, 2, along)
    odd_rows = lax.slice_in_dim(extended, 1, length, 2, along)
    first_d = trimmed(odd_rows, 0, 1, along) + LIFT_ALPHA * (trimmed(even_rows, 0, 1, along) + trimmed(even_rows, 1, 0, along))
    first_s = trimmed(even_rows, 1, 1, along) + LIFT_BETA * (trimmed(first_d, 0, 1, along) + trimmed(first_d, 1, 0, along))
    second_d = trimmed(first_d, 1, 1, along) + LIFT_GAMMA * (trimmed(first_s, 0, 1, along) + trimmed(first_s, 1, 0, along))
    second_s = trimmed(first_s, 1, 1, along) + LIFT_DELTA * (trimmed(second_d, 0, 1, along) + trimmed(second_d, 1, 0, along))
    return (second_s * LIFT_KAPPA, trimmed(second_d, 1, 0, along) / LIFT_KAPPA)

def pair_up(smooth, detail, along):
    stacked = jnp.stack([smooth, detail], axis=along + 1)
    shape = list(smooth.shape)
    shape[along] = shape[along] * 2
    return stacked.reshape(shape)

def analyze(values, along, levels, extend):
    if levels == 0:
        return values
    smooth, detail = lifting(extend(values), along)
    return pair_up(analyze(smooth, along, levels - 1, extend), detail, along)

def padding(values, along, mode_name):
    widths = [(0, 0)] * values.ndim
    widths[along] = (4, 4)
    return jnp.pad(values, widths, mode=mode_name)

def dft_table(slots, count_lon, count_waves):
    lon_index = jnp.arange(count_lon, dtype=jnp.int32)
    phase = slots[:, None] * lon_index[None, :] % count_lon
    angle = phase.astype(jnp.float32) * (2.0 * math.pi / count_lon)
    weight = jnp.where(slots == 0, 1.0, 2.0).astype(jnp.float32) / math.sqrt(2.0 * count_waves)
    table = jnp.concatenate([weight[:, None] * jnp.cos(angle), -weight[:, None] * jnp.sin(angle)], axis=0)
    return table.astype(jnp.bfloat16)

def reference(spectra, legendre, wave_order, writer_order):
    slots = wave_order.astype(jnp.int32)
    n_index = jnp.arange(NN, dtype=jnp.int32)
    keep = n_index[None, :] >= slots[:, None]
    masked = jnp.where(keep[None, None], spectra, jnp.zeros_like(spectra))

    def one_wave(index):
        coeffs = lax.dynamic_index_in_dim(masked, index, 2, keepdims=False).astype(jnp.float32)
        values = lax.dynamic_index_in_dim(legendre, index, 0, keepdims=False).astype(jnp.float32)
        return jnp.einsum('frn,ln->flr', coeffs, values)
    fourier = lax.map(one_wave, jnp.arange(M1, dtype=jnp.int32)).astype(jnp.bfloat16)
    fourier = jnp.transpose(fourier, (1, 2, 3, 0))
    table = dft_table(slots, NLON, M1).astype(jnp.float32)

    def one_field(index):
        source = lax.dynamic_index_in_dim(fourier, writer_order[index].astype(jnp.int32), 0, keepdims=False)
        rows = source.reshape(NLATG, 2 * M1).astype(jnp.float32)
        grid = jnp.dot(rows, table, preferred_element_type=jnp.float32)
        rowwise = analyze(grid, 1, WL, lambda values: padding(values, 1, 'wrap'))
        return analyze(rowwise, 0, WL, lambda values: padding(values, 0, 'reflect')).astype(jnp.bfloat16)
    return lax.map(one_field, jnp.arange(FL, dtype=jnp.int32))
```

```python
import math

import jax
import jax.numpy as jnp
import ml_dtypes
import numpy as np
from jax import lax
from jax.experimental import pallas as pl
from jax.experimental.pallas import tpu as pltpu
from jax.sharding import PartitionSpec as P

NLAT = 2560
NLON = 5120
NWAVE = 640
WL = 5
BANDS = 16
OWNERS = 8
BAND = NLAT // BANDS
SLOTS = NWAVE // OWNERS
PAIRS = SLOTS // 2
FIELDS = 16
BLOCKS = 6
LANE = 128
EDGE = 32
TILE = 512

LIFT_ALPHA = -1.586134342059924
LIFT_BETA = -0.052980118572961
LIFT_GAMMA = 0.882911075530934
LIFT_DELTA = 0.443506852043971
LIFT_KAPPA = 1.149604398860241


def analyze(values, levels, mode_name):
    if levels == 0:
        return values
    widths = [(4, 4)] + [(0, 0)] * (values.ndim - 1)
    extended = np.pad(values, widths, mode=mode_name)
    even, odd = extended[0::2], extended[1::2]
    first_d = odd[:-1] + LIFT_ALPHA * (even[:-1] + even[1:])
    first_s = even[1:-1] + LIFT_BETA * (first_d[:-1] + first_d[1:])
    second_d = first_d[1:-1] + LIFT_GAMMA * (first_s[:-1] + first_s[1:])
    second_s = first_s[1:-1] + LIFT_DELTA * (second_d[:-1] + second_d[1:])
    result = np.empty_like(values)
    result[0::2] = analyze(second_s * LIFT_KAPPA, levels - 1, mode_name)
    result[1::2] = second_d[1:] / LIFT_KAPPA
    return result


def longitude_matrix():
    waves = np.arange(NWAVE)
    phase = waves[:, None] * np.arange(NLON)[None, :] % NLON
    angle = phase * (2.0 * math.pi / NLON)
    weight = np.where(waves == 0, 1.0, 2.0)[:, None] / math.sqrt(2.0 * NWAVE)
    table = np.concatenate([weight * np.cos(angle), -weight * np.sin(angle)], axis=0)
    table = table.astype(np.float32).astype(ml_dtypes.bfloat16).astype(np.float64)
    return analyze(table.T, WL, "wrap").T.astype(np.float32).astype(ml_dtypes.bfloat16)


def latitude_matrices():
    whole = analyze(np.eye(NLAT), WL, "reflect")
    inner = whole[:, 7 * BAND : 8 * BAND]
    touched = np.nonzero((inner != 0).any(axis=1))[0]
    above = touched[touched < 7 * BAND] - 6 * BAND
    below = touched[touched >= 8 * BAND] - 8 * BAND
    out = np.zeros((3, 4, BAND, 4 * BAND + 8 * EDGE))
    for variant, band in enumerate((0, 7, BANDS - 1)):
        columns = whole[:, band * BAND : (band + 1) * BAND]
        own = columns[band * BAND : (band + 1) * BAND]
        for part in range(4):
            out[variant, part, :, part * BAND : (part + 1) * BAND] = own.T
            start = 4 * BAND + part * EDGE
            if band > 0:
                out[variant, part, :, start : start + len(above)] = columns[(band - 1) * BAND + above].T
            start += 4 * EDGE
            if band < BANDS - 1:
                out[variant, part, :, start : start + len(below)] = columns[(band + 1) * BAND + below].T
    place = np.zeros((2, 4 * EDGE, 4 * BAND))
    for part in range(4):
        place[0, part * EDGE + np.arange(len(above)), part * BAND + above] = 1.0
        place[1, part * EDGE + np.arange(len(below)), part * BAND + below] = 1.0
    return (
        out.astype(np.float32).astype(ml_dtypes.bfloat16),
        place.astype(ml_dtypes.bfloat16),
    )


def pack_kernel(order_ref, spectra_ref, real_ref, imag_ref, wide, low, high):
    first = lax.axis_index("wave") * SLOTS
    for pair in range(PAIRS):
        low[pl.ds(pair, 1), :] = jnp.full((1, LANE), order_ref[first + 2 * pair], jnp.int32)
        high[pl.ds(pair, 1), :] = jnp.full((1, LANE), order_ref[first + 2 * pair + 1], jnp.int32)
    waves_a, waves_b = low[...], high[...]
    lane = lax.broadcasted_iota(jnp.int32, (PAIRS, LANE), 1)
    for part, out in enumerate((real_ref, imag_ref)):
        for block in range(5):
            wide[block] = spectra_ref[0, part, :, block * LANE : (block + 1) * LANE].astype(jnp.float32)
        for block in range(BLOCKS):
            taken = jnp.zeros((PAIRS, LANE), jnp.float32)
            if block <= 4:
                values = wide[4 - block, pl.ds(1, PAIRS, stride=2), :]
                taken = jnp.where(lane + (4 - block) * LANE >= waves_b, values, taken)
            if block >= 1:
                values = wide[block - 1, pl.ds(0, PAIRS, stride=2), :]
                values = jnp.where(lane + (block - 1) * LANE >= waves_a, values, jnp.zeros_like(values))
                taken = jnp.where(waves_a < block * LANE, values, taken)
            out[:, block * LANE : (block + 1) * LANE] = taken.astype(jnp.bfloat16)


def legendre_kernel(order_ref, writer_ref, *refs):
    parts = refs[:8]
    legendre_ref, matrix_ref, own_ref, above_ref, below_ref = refs[8:13]
    held, spread, rows, matrix, sems, matrix_sem = refs[13:]
    first = lax.axis_index("wave") * SLOTS
    band = lax.axis_index("lat")
    variant = jnp.where(band == 0, 0, jnp.where(band == BANDS - 1, 2, 1))
    matrix_copy = pltpu.make_async_copy(matrix_ref.at[variant], matrix, matrix_sem)
    matrix_copy.start()

    def fetch(pair, carry):
        wave = order_ref[first + 2 * pair]
        for block in range(BLOCKS):
            from_a = wave < block * LANE
            slot = jnp.where(from_a, 2 * pair, 2 * pair + 1)
            source = jnp.where(from_a, block - 1, 4 - block)
            pltpu.make_async_copy(
                legendre_ref.at[slot, :, pl.ds(pl.multiple_of(source * LANE, LANE), LANE)],
                held.at[pair, :, pl.ds(block * LANE, LANE)],
                sems.at[pair],
            ).start()
        return carry

    lax.fori_loop(0, PAIRS, fetch, 0)

    band_x, band_z = band // 4, lax.rem(band, 4)
    steps = (0, 3, 1, 2)
    for outer in range(4):
        for inner in range(4):
            for part in range(2):
                along_x, along_z = (outer, inner) if part == 0 else (inner, outer)
                field = 4 * lax.rem(band_x + steps[along_x], 4) + lax.rem(band_z + steps[along_z], 4)
                start = pl.multiple_of((2 * field + part) * PAIRS, 8)
                for block in range(BLOCKS):
                    values = parts[4 * part + outer][inner, :, block * LANE : (block + 1) * LANE]
                    spread[block, pl.ds(start, PAIRS), :] = values.astype(jnp.float32)

    def contract(pair, carry):
        pltpu.make_async_copy(held.at[pair], held.at[pair], sems.at[pair]).wait()
        wave = order_ref[first + 2 * pair]
        lower, upper = [], []
        for block in range(BLOCKS):
            values = spread[block, pl.ds(pair, 2 * FIELDS, stride=PAIRS), :]
            from_a = wave < block * LANE
            lower.append(jnp.where(from_a, values, 0.0).astype(jnp.bfloat16))
            upper.append(jnp.where(from_a, 0.0, values).astype(jnp.bfloat16))
        left = jnp.concatenate(
            [jnp.concatenate(lower, axis=1), jnp.concatenate(upper, axis=1)], axis=0
        )
        sums = lax.dot_general(
            left, held[pair], (((1,), (1,)), ((), ())), preferred_element_type=jnp.float32
        )
        for which in range(2):
            piece = sums[which * 2 * FIELDS : (which + 1) * 2 * FIELDS]
            where = pl.ds(2 * pair + which, 2 * FIELDS, stride=SLOTS)
            rows[0, where, :] = piece[:, :LANE]
            rows[1, where, : BAND - LANE] = piece[:, LANE:]
        return carry

    lax.fori_loop(0, PAIRS, contract, 0)
    matrix_copy.wait()

    def lift(owner, carry):
        total = jnp.zeros((SLOTS, 4 * BAND + 8 * EDGE), jnp.float32)
        for part in range(4):
            field = writer_ref[2 * owner + part // 2]
            start = pl.multiple_of((2 * field + part % 2) * SLOTS, 8)
            left = jnp.concatenate(
                [rows[0, pl.ds(start, SLOTS), :], rows[1, pl.ds(start, SLOTS), : BAND - LANE]], axis=1
            ).astype(jnp.bfloat16)
            total += jnp.dot(left, matrix[part], preferred_element_type=jnp.float32)
        own_ref[owner] = total[:, : 4 * BAND]
        above_ref[owner] = total[:, 4 * BAND : 4 * BAND + 4 * EDGE].astype(jnp.bfloat16)
        below_ref[owner] = total[:, 4 * BAND + 4 * EDGE :].astype(jnp.bfloat16)
        return carry

    lax.fori_loop(0, OWNERS, lift, 0)


def join_kernel(own_ref, above_ref, below_ref, place_ref, out_ref):
    for owner in range(OWNERS):
        total = own_ref[owner]
        total += jnp.dot(above_ref[owner], place_ref[0], preferred_element_type=jnp.float32)
        total += jnp.dot(below_ref[owner], place_ref[1], preferred_element_type=jnp.float32)
        out_ref[owner] = total.astype(jnp.bfloat16)


def synthesis_kernel(order_ref, waves_ref, table_ref, out_ref, left):
    @pl.when(pl.program_id(0) == 0)
    def _():
        row = lax.broadcasted_iota(jnp.int32, (NWAVE, NWAVE), 0)
        chosen = jnp.where(row == order_ref[...], 1.0, 0.0).astype(jnp.bfloat16)
        ordered = jnp.dot(chosen, waves_ref[...], preferred_element_type=jnp.float32)
        turned = ordered.T.astype(jnp.bfloat16)
        for field in range(2):
            for part in range(2):
                left[field * BAND : (field + 1) * BAND, part * NWAVE : (part + 1) * NWAVE] = turned[
                    (2 * field + part) * BAND : (2 * field + part + 1) * BAND
                ]

    sums = jnp.dot(left[...], table_ref[...], preferred_element_type=jnp.float32)
    out_ref[0] = sums[:BAND].astype(jnp.bfloat16)
    out_ref[1] = sums[BAND:].astype(jnp.bfloat16)


def along_z(step):
    return [(4 * x + z, 4 * x + (z + step) % 4) for x in range(4) for z in range(4)]


def along_x(step):
    return [(4 * x + z, 4 * ((x + step) % 4) + z) for x in range(4) for z in range(4)]


def neighbour(step):
    return [(band, (band + step) % BANDS) for band in range(BANDS)]


SMEM = pl.BlockSpec(memory_space=pltpu.SMEM)
VMEM = pl.BlockSpec(memory_space=pltpu.VMEM)
ANY = pl.BlockSpec(memory_space=pl.ANY)


def make_on_device(table, matrices, place):
    def on_device(spectra, legendre, wave_order, writer_order):
        real, imag = pl.pallas_call(
            pack_kernel,
            out_shape=[jax.ShapeDtypeStruct((PAIRS, BLOCKS * LANE), jnp.bfloat16)] * 2,
            in_specs=[SMEM, VMEM],
            out_specs=[VMEM, VMEM],
            scratch_shapes=[
                pltpu.VMEM((5, SLOTS, LANE), jnp.float32),
                pltpu.VMEM((PAIRS, LANE), jnp.int32),
                pltpu.VMEM((PAIRS, LANE), jnp.int32),
            ],
            name="pack",
        )(wave_order, spectra)
        firsts = [[real], [imag]]
        for step in (1, 3, 2):
            firsts[0].append(lax.ppermute(real, "lat", along_z(step)))
            firsts[1].append(lax.ppermute(imag, "lat", along_x(step)))
        firsts = [jnp.stack(blocks) for blocks in firsts]
        seconds = [[firsts[0]], [firsts[1]]]
        for step in (1, 3, 2):
            seconds[0].append(lax.ppermute(firsts[0], "lat", along_x(step)))
            seconds[1].append(lax.ppermute(firsts[1], "lat", along_z(step)))

        width = 4 * BAND
        own, above, below = pl.pallas_call(
            legendre_kernel,
            out_shape=[
                jax.ShapeDtypeStruct((OWNERS, SLOTS, width), jnp.float32),
                jax.ShapeDtypeStruct((OWNERS, SLOTS, 4 * EDGE), jnp.bfloat16),
                jax.ShapeDtypeStruct((OWNERS, SLOTS, 4 * EDGE), jnp.bfloat16),
            ],
            in_specs=[SMEM, SMEM] + [VMEM] * 8 + [ANY, ANY],
            out_specs=[VMEM] * 3,
            scratch_shapes=[
                pltpu.VMEM((PAIRS, BAND, BLOCKS * LANE), jnp.bfloat16),
                pltpu.VMEM((BLOCKS, 2 * FIELDS * PAIRS, LANE), jnp.float32),
                pltpu.VMEM((2, 2 * FIELDS * SLOTS, LANE), jnp.float32),
                pltpu.VMEM((4, BAND, width + 8 * EDGE), jnp.bfloat16),
                pltpu.SemaphoreType.DMA((PAIRS,)),
                pltpu.SemaphoreType.DMA,
            ],
            compiler_params=pltpu.CompilerParams(vmem_limit_bytes=40 * 2**20),
            cost_estimate=pl.CostEstimate(flops=800_000_000, bytes_accessed=14_000_000, transcendentals=0),
            name="legendre",
        )(wave_order, writer_order, *seconds[0], *seconds[1], legendre, matrices)

        above = lax.ppermute(above, "lat", neighbour(-1))
        below = lax.ppermute(below, "lat", neighbour(1))
        joined = pl.pallas_call(
            join_kernel,
            out_shape=jax.ShapeDtypeStruct((OWNERS, SLOTS, width), jnp.bfloat16),
            in_specs=[VMEM] * 4,
            out_specs=VMEM,
            name="join",
        )(own, above, below, place)

        waves = lax.all_to_all(joined, "wave", split_axis=0, concat_axis=0, tiled=True)
        return pl.pallas_call(
            synthesis_kernel,
            grid=(NLON // TILE,),
            out_shape=jax.ShapeDtypeStruct((2, BAND, NLON), jnp.bfloat16),
            in_specs=[
                pl.BlockSpec((1, NWAVE), lambda j: (0, 0)),
                pl.BlockSpec((NWAVE, width), lambda j: (0, 0)),
                pl.BlockSpec((2 * NWAVE, TILE), lambda j: (0, j)),
            ],
            out_specs=pl.BlockSpec((2, BAND, TILE), lambda j: (0, 0, j)),
            scratch_shapes=[pltpu.VMEM((2 * BAND, 2 * NWAVE), jnp.bfloat16)],
            compiler_params=pltpu.CompilerParams(vmem_limit_bytes=40 * 2**20),
            cost_estimate=pl.CostEstimate(flops=4_400_000_000, bytes_accessed=18_000_000, transcendentals=0),
            name="synthesis",
        )(wave_order.reshape(1, NWAVE), waves.reshape(NWAVE, width), table)

    return on_device


def solution(mesh):
    table = longitude_matrix()
    matrices, place = latitude_matrices()
    return jax.shard_map(
        make_on_device(jnp.asarray(table), jnp.asarray(matrices), jnp.asarray(place)),
        mesh=mesh,
        in_specs=(P("lat", None, "wave", None), P("wave", "lat", None), P(), P()),
        out_specs=P("wave", "lat", None),
        check_vma=False,
    )
```

```python
import math

import jax
import jax.numpy as jnp
import ml_dtypes
import numpy as np
from jax import lax
from jax.experimental import pallas as pl
from jax.experimental.pallas import tpu as pltpu
from jax.sharding import PartitionSpec as P

NLAT = 2560
NLON = 5120
NWAVE = 640
WL = 5
BANDS = 16
OWNERS = 8
BAND = NLAT // BANDS
SLOTS = NWAVE // OWNERS
PAIRS = SLOTS // 2
FIELDS = 16
BLOCKS = 6
LANE = 128
HALVES = 2
PART_PAIRS = PAIRS // HALVES
PART_SLOTS = SLOTS // HALVES
RANK = 16
WIDTH = 4 * LANE + 4 * (BAND - LANE + 2 * RANK)
TILE = 512
GROUP = 4
SMALL_BYTES = 48 * 2**20
LARGE_BYTES = 52 * 2**20

LIFT_ALPHA = -1.586134342059924
LIFT_BETA = -0.052980118572961
LIFT_GAMMA = 0.882911075530934
LIFT_DELTA = 0.443506852043971
LIFT_KAPPA = 1.149604398860241


def analyze(values, levels, mode_name):
    if levels == 0:
        return values
    widths = [(4, 4)] + [(0, 0)] * (values.ndim - 1)
    extended = np.pad(values, widths, mode=mode_name)
    even, odd = extended[0::2], extended[1::2]
    first_d = odd[:-1] + LIFT_ALPHA * (even[:-1] + even[1:])
    first_s = even[1:-1] + LIFT_BETA * (first_d[:-1] + first_d[1:])
    second_d = first_d[1:-1] + LIFT_GAMMA * (first_s[:-1] + first_s[1:])
    second_s = first_s[1:-1] + LIFT_DELTA * (second_d[:-1] + second_d[1:])
    result = np.empty_like(values)
    result[0::2] = analyze(second_s * LIFT_KAPPA, levels - 1, mode_name)
    result[1::2] = second_d[1:] / LIFT_KAPPA
    return result


def longitude_matrix():
    waves = np.arange(NWAVE)
    phase = waves[:, None] * np.arange(NLON)[None, :] % NLON
    angle = phase * (2.0 * math.pi / NLON)
    weight = np.where(waves == 0, 1.0, 2.0)[:, None] / math.sqrt(2.0 * NWAVE)
    table = np.concatenate([weight * np.cos(angle), -weight * np.sin(angle)], axis=0)
    table = table.astype(np.float32).astype(ml_dtypes.bfloat16).astype(np.float64)
    return analyze(table.T, WL, "wrap").T.astype(np.float32).astype(ml_dtypes.bfloat16)


def latitude_matrices():
    whole = analyze(np.eye(NLAT), WL, "reflect")

    def block(row_band, column_band):
        return whole[row_band * BAND : (row_band + 1) * BAND, column_band * BAND : (column_band + 1) * BAND]

    assert all(np.abs(block(band - 1, band) - block(6, 7)).max() < 1e-12 for band in range(1, BANDS))
    assert all(np.abs(block(band, band - 1) - block(8, 7)).max() < 1e-12 for band in range(1, BANDS))
    inner = whole[:, 7 * BAND : 8 * BAND]
    assert np.abs(inner[: 6 * BAND]).max() == 0 and np.abs(inner[9 * BAND :]).max() == 0
    assert all(np.abs(block(band, band) - block(7, 7)).max() < 1e-12 for band in range(1, BANDS - 1))
    expand = np.zeros((BAND, 2 * RANK))
    project = np.zeros((BAND, 2 * RANK))
    for side, part in enumerate((block(6, 7), block(8, 7))):
        left, sizes, right = np.linalg.svd(part)
        rank = int((sizes > 1e-12).sum())
        assert rank <= RANK
        expand[:, side * RANK : side * RANK + rank] = left[:, :rank] * sizes[:rank]
        project[:, side * RANK : side * RANK + rank] = right[:rank].T
    out = np.zeros((3, BAND, 2 * LANE))
    for variant, band in enumerate((0, 7, BANDS - 1)):
        own = block(band, band).T
        tail = np.concatenate([own[:, LANE:], project], axis=1)
        out[variant] = np.concatenate([own[:, :LANE], tail, tail], axis=1)
    return (
        out.astype(np.float32).astype(ml_dtypes.bfloat16),
        expand.astype(np.float32).astype(ml_dtypes.bfloat16),
    )


def pack_kernel(order_ref, spectra_ref, *refs):
    outs, (wide, low, high, packed) = refs[:HALVES], refs[HALVES:]
    first = lax.axis_index("wave") * SLOTS
    for pair in range(PAIRS):
        low[pl.ds(pair, 1), :] = jnp.full((1, LANE), order_ref[first + 2 * pair], jnp.int32)
        high[pl.ds(pair, 1), :] = jnp.full((1, LANE), order_ref[first + 2 * pair + 1], jnp.int32)
    waves_a, waves_b = low[...], high[...]
    lane = lax.broadcasted_iota(jnp.int32, (PAIRS, LANE), 1)
    for part in range(2):
        for block in range(5):
            wide[block] = spectra_ref[0, part, :, block * LANE : (block + 1) * LANE].astype(jnp.float32)
        for block in range(BLOCKS):
            taken = jnp.zeros((PAIRS, LANE), jnp.float32)
            if block <= 4:
                values = wide[4 - block, pl.ds(1, PAIRS, stride=2), :]
                taken = jnp.where(lane + (4 - block) * LANE >= waves_b, values, taken)
            if block >= 1:
                values = wide[block - 1, pl.ds(0, PAIRS, stride=2), :]
                values = jnp.where(lane + (block - 1) * LANE >= waves_a, values, jnp.zeros_like(values))
                taken = jnp.where(waves_a < block * LANE, values, taken)
            for half in range(HALVES):
                packed[half, pl.ds(part * PART_PAIRS, PART_PAIRS), block * LANE : (block + 1) * LANE] = taken[
                    half * PART_PAIRS : (half + 1) * PART_PAIRS
                ]
    for half in range(HALVES):
        outs[half][...] = packed[half].astype(jnp.bfloat16)


def legendre_kernel(half, order_ref, writer_ref, *refs):
    parts = refs[:4]
    legendre_ref, matrix_ref, out_ref = refs[4:7]
    held, staged, spread, rows, results, matrix, sems, staged_sems, matrix_sem = refs[7:]
    base = half * PART_PAIRS
    first = lax.axis_index("wave") * SLOTS + 2 * base
    band = lax.axis_index("lat")
    variant = jnp.where(band == 0, 0, jnp.where(band == BANDS - 1, 2, 1))
    copies = [pltpu.make_async_copy(parts[i], staged.at[i], staged_sems.at[i]) for i in range(4)]
    for copy in copies:
        copy.start()

    def fetch(pair, carry):
        wave = order_ref[first + 2 * pair]
        for block in range(BLOCKS):
            from_a = wave < block * LANE
            slot = 2 * (base + pair) + jnp.where(from_a, 0, 1)
            source = jnp.where(from_a, block - 1, 4 - block)
            pltpu.make_async_copy(
                legendre_ref.at[slot, :, pl.ds(pl.multiple_of(source * LANE, LANE), LANE)],
                held.at[pair, :, pl.ds(block * LANE, LANE)],
                sems.at[pair],
            ).start()
        return carry

    lax.fori_loop(0, PART_PAIRS, fetch, 0)
    matrix_copy = pltpu.make_async_copy(matrix_ref.at[variant], matrix, matrix_sem)
    matrix_copy.start()

    band_x, band_z = band // 4, lax.rem(band, 4)
    steps = (0, 3, 1, 2)
    for outer in range(4):
        copies[outer].wait()
        for inner in range(4):
            along_x, along_z = (outer, inner) if half == 0 else (inner, outer)
            field = 4 * lax.rem(band_x + steps[along_x], 4) + lax.rem(band_z + steps[along_z], 4)
            start = pl.multiple_of(field * 2 * PART_PAIRS, 8)
            for block in range(BLOCKS):
                values = staged[outer, inner, :, block * LANE : (block + 1) * LANE]
                spread[block, pl.ds(start, 2 * PART_PAIRS), :] = values.astype(jnp.float32)

    def contract(group, carry):
        for member in range(GROUP):
            pair = group * GROUP + member
            pltpu.make_async_copy(held.at[pair], held.at[pair], sems.at[pair]).wait()
            wave = order_ref[first + 2 * pair]
            lower, upper = [], []
            for block in range(BLOCKS):
                values = spread[block, pl.ds(pair, 2 * FIELDS, stride=PART_PAIRS), :].astype(jnp.bfloat16)
                from_a = wave < block * LANE
                lower.append(jnp.where(from_a, values, jnp.zeros_like(values)))
                upper.append(jnp.where(from_a, jnp.zeros_like(values), values))
            left = jnp.concatenate(
                [jnp.concatenate(lower, axis=1), jnp.concatenate(upper, axis=1)], axis=0
            )
            sums = lax.dot_general(
                left, held[pair], (((1,), (1,)), ((), ())), preferred_element_type=jnp.float32
            )
            for which in range(2):
                piece = sums[which * 2 * FIELDS : (which + 1) * 2 * FIELDS]
                where = pl.ds(2 * pair + which, 2 * FIELDS, stride=PART_SLOTS)
                rows[0, where, :] = piece[:, :LANE]
                rows[1, where, : BAND - LANE] = piece[:, LANE:]
        return carry

    lax.fori_loop(0, PART_PAIRS // GROUP, contract, 0)
    matrix_copy.wait()

    chunk = 2 * FIELDS * PART_SLOTS // 4
    for index in range(4):
        picked = slice(index * chunk, (index + 1) * chunk)
        left = jnp.concatenate([rows[0, picked, :], rows[1, picked, : BAND - LANE]], axis=1).astype(jnp.bfloat16)
        sums = jnp.dot(left, matrix[...], preferred_element_type=jnp.float32)
        results[0, picked, :] = sums[:, :LANE]
        results[1, picked, :] = sums[:, LANE:]

    lane = lax.broadcasted_iota(jnp.int32, (PART_SLOTS, LANE), 1)
    for owner in range(OWNERS):
        for member in range(2):
            field = writer_ref[2 * owner + member]
            tails = []
            for part in range(2):
                start = pl.multiple_of((2 * field + part) * PART_SLOTS, 8)
                place = (2 * member + part) * LANE
                out_ref[owner, :, place : place + LANE] = results[0, pl.ds(start, PART_SLOTS), :].astype(jnp.bfloat16)
                tails.append(results[1, pl.ds(start, PART_SLOTS), :])
            place = (4 + member) * LANE
            out_ref[owner, :, place : place + LANE] = jnp.where(lane < LANE // 2, *tails).astype(jnp.bfloat16)


def edge_kernel(order_ref, *refs):
    waves = refs[:HALVES]
    chosen_ref, rest_ref, above_ref, below_ref = refs[HALVES:]
    row = lax.broadcasted_iota(jnp.int32, (NWAVE, NWAVE), 0)
    chosen_ref[...] = jnp.where(row == order_ref[...], 1.0, 0.0).astype(jnp.bfloat16)
    count = NWAVE // HALVES
    ordered = sum(
        jnp.dot(
            chosen_ref[:, half * count : (half + 1) * count],
            waves[half][...],
            preferred_element_type=jnp.float32,
        )
        for half in range(HALVES)
    )
    turned = ordered.T.astype(jnp.bfloat16)
    rest = BAND - LANE
    for part in range(4):
        start = part * (rest + 2 * RANK)
        rest_ref[part * rest : (part + 1) * rest] = turned[start : start + rest]
        above_ref[part * RANK : (part + 1) * RANK] = turned[start + rest : start + rest + RANK]
        below_ref[part * RANK : (part + 1) * RANK] = turned[start + rest + RANK : start + rest + 2 * RANK]


def order_kernel(chosen_ref, *refs):
    waves, out_ref = refs[:HALVES], refs[HALVES]
    count = NWAVE // HALVES
    ordered = sum(
        jnp.dot(
            chosen_ref[:, half * count : (half + 1) * count],
            waves[half][...],
            preferred_element_type=jnp.float32,
        )
        for half in range(HALVES)
    )
    out_ref[...] = ordered.T.astype(jnp.bfloat16)


def synthesis_kernel(main_ref, rest_ref, above_ref, below_ref, expand_ref, table_ref, out_ref, left):
    @pl.when(pl.program_id(0) == 0)
    def _():
        rest = BAND - LANE
        for field in range(2):
            for part in range(2):
                which = 2 * field + part
                edges = slice(which * RANK, (which + 1) * RANK)
                added = jnp.dot(
                    expand_ref[...],
                    jnp.concatenate([above_ref[edges], below_ref[edges]], axis=0),
                    preferred_element_type=jnp.float32,
                )
                lanes = slice(part * NWAVE, (part + 1) * NWAVE)
                own = main_ref[which * LANE : (which + 1) * LANE].astype(jnp.float32)
                left[field * BAND : field * BAND + LANE, lanes] = (own + added[:LANE]).astype(jnp.bfloat16)
                own = rest_ref[which * rest : (which + 1) * rest].astype(jnp.float32)
                left[field * BAND + LANE : (field + 1) * BAND, lanes] = (own + added[LANE:]).astype(jnp.bfloat16)

    sums = jnp.dot(left[...], table_ref[...], preferred_element_type=jnp.float32)
    out_ref[0] = sums[:BAND].astype(jnp.bfloat16)
    out_ref[1] = sums[BAND:].astype(jnp.bfloat16)


def along_z(step):
    return [(4 * x + z, 4 * x + (z + step) % 4) for x in range(4) for z in range(4)]


def along_x(step):
    return [(4 * x + z, 4 * ((x + step) % 4) + z) for x in range(4) for z in range(4)]


def neighbour(step):
    return [(band, band + step) for band in range(BANDS) if 0 <= band + step < BANDS]


SMEM = pl.BlockSpec(memory_space=pltpu.SMEM)
VMEM = pl.BlockSpec(memory_space=pltpu.VMEM)
ANY = pl.BlockSpec(memory_space=pl.ANY)
SMALL = pltpu.CompilerParams(vmem_limit_bytes=SMALL_BYTES)
LARGE = pltpu.CompilerParams(vmem_limit_bytes=LARGE_BYTES)


def bf16(*shape):
    return jax.ShapeDtypeStruct(shape, jnp.bfloat16)


def make_on_device(table, matrices, expand):
    def on_device(spectra, legendre, wave_order, writer_order):
        halves = pl.pallas_call(
            pack_kernel,
            out_shape=[bf16(2 * PART_PAIRS, BLOCKS * LANE)] * HALVES,
            in_specs=[SMEM, VMEM],
            out_specs=[VMEM] * HALVES,
            scratch_shapes=[
                pltpu.VMEM((5, SLOTS, LANE), jnp.float32),
                pltpu.VMEM((PAIRS, LANE), jnp.int32),
                pltpu.VMEM((PAIRS, LANE), jnp.int32),
                pltpu.VMEM((HALVES, 2 * PART_PAIRS, BLOCKS * LANE), jnp.float32),
            ],
            name="pack",
        )(wave_order, spectra)
        order = wave_order.reshape(OWNERS, HALVES, PART_SLOTS).swapaxes(0, 1).reshape(1, NWAVE)

        axes = ((along_z, along_x), (along_x, along_z))
        gathered = halves
        for stage in range(2):
            arrived = [
                [values] + [lax.ppermute(values, "lat", axes[half][stage](step)) for step in (1, 3, 2)]
                for half, values in enumerate(gathered)
            ]
            gathered = lax.optimization_barrier([jnp.stack(blocks) for blocks in arrived]) if stage == 0 else arrived

        waves = []
        for half in range(HALVES):
            lifted = pl.pallas_call(
                lambda *refs, half=half: legendre_kernel(half, *refs),
                out_shape=bf16(OWNERS, PART_SLOTS, WIDTH),
                in_specs=[SMEM, SMEM] + [ANY] * 6,
                out_specs=VMEM,
                scratch_shapes=[
                    pltpu.VMEM((PART_PAIRS, BAND, BLOCKS * LANE), jnp.bfloat16),
                    pltpu.VMEM((4, 4, 2 * PART_PAIRS, BLOCKS * LANE), jnp.bfloat16),
                    pltpu.VMEM((BLOCKS, 2 * FIELDS * PART_PAIRS, LANE), jnp.float32),
                    pltpu.VMEM((2, 2 * FIELDS * PART_SLOTS, LANE), jnp.float32),
                    pltpu.VMEM((2, 2 * FIELDS * PART_SLOTS, LANE), jnp.float32),
                    pltpu.VMEM((BAND, 2 * LANE), jnp.bfloat16),
                    pltpu.SemaphoreType.DMA((PART_PAIRS,)),
                    pltpu.SemaphoreType.DMA((4,)),
                    pltpu.SemaphoreType.DMA,
                ],
                compiler_params=SMALL,
                cost_estimate=pl.CostEstimate(flops=400_000_000, bytes_accessed=8_000_000, transcendentals=0),
                name=f"legendre{half}",
            )(wave_order, writer_order, *gathered[half], legendre, matrices)
            if half + 1 < HALVES:
                lifted, gathered[half + 1] = lax.optimization_barrier((lifted, gathered[half + 1]))
            received = lax.all_to_all(lifted, "wave", split_axis=0, concat_axis=0, tiled=True)
            waves.append(received.reshape(OWNERS * PART_SLOTS, WIDTH))

        main, rest = 4 * LANE, 4 * (BAND - LANE)
        count = NWAVE // HALVES
        chosen, tail, above, below = pl.pallas_call(
            edge_kernel,
            grid=(1,),
            out_shape=[bf16(NWAVE, NWAVE), bf16(rest, NWAVE), bf16(4 * RANK, NWAVE), bf16(4 * RANK, NWAVE)],
            in_specs=[pl.BlockSpec((1, NWAVE), lambda i: (0, 0))]
            + [pl.BlockSpec((count, WIDTH - main), lambda i: (0, main // (WIDTH - main)))] * HALVES,
            out_specs=[VMEM] * 4,
            compiler_params=SMALL,
            name="edges",
        )(order, *waves)
        above = lax.ppermute(above, "lat", neighbour(-1))
        below = lax.ppermute(below, "lat", neighbour(1))
        ordered = pl.pallas_call(
            order_kernel,
            grid=(1,),
            out_shape=bf16(main, NWAVE),
            in_specs=[pl.BlockSpec((NWAVE, NWAVE), lambda i: (0, 0))]
            + [pl.BlockSpec((count, main), lambda i: (0, 0))] * HALVES,
            out_specs=VMEM,
            compiler_params=SMALL,
            cost_estimate=pl.CostEstimate(flops=800_000_000, bytes_accessed=4_000_000, transcendentals=0),
            name="order",
        )(chosen, *waves)
        return pl.pallas_call(
            synthesis_kernel,
            grid=(NLON // TILE,),
            out_shape=bf16(2, BAND, NLON),
            in_specs=[VMEM] * 5 + [pl.BlockSpec((2 * NWAVE, TILE), lambda j: (0, j))],
            out_specs=pl.BlockSpec((2, BAND, TILE), lambda j: (0, 0, j)),
            scratch_shapes=[pltpu.VMEM((2 * BAND, 2 * NWAVE), jnp.bfloat16)],
            compiler_params=LARGE,
            cost_estimate=pl.CostEstimate(flops=4_400_000_000, bytes_accessed=18_000_000, transcendentals=0),
            name="synthesis",
        )(ordered, tail, above, below, expand, table)

    return on_device


def solution(mesh):
    table = longitude_matrix()
    matrices, expand = latitude_matrices()
    return jax.shard_map(
        make_on_device(jnp.asarray(table), jnp.asarray(matrices), jnp.asarray(expand)),
        mesh=mesh,
        in_specs=(P("lat", None, "wave", None), P("wave", "lat", None), P(), P()),
        out_specs=P("wave", "lat", None),
        check_vma=False,
    )
```

```python
import math

import jax
import jax.numpy as jnp
import ml_dtypes
import numpy as np
from jax import lax
from jax.experimental import pallas as pl
from jax.experimental.pallas import tpu as pltpu
from jax.sharding import PartitionSpec as P

NLAT = 2560
NLON = 5120
NWAVE = 640
WL = 5
BANDS = 16
OWNERS = 8
BAND = NLAT // BANDS
SLOTS = NWAVE // OWNERS
PAIRS = SLOTS // 2
FIELDS = 16
BLOCKS = 6
LANE = 128
HALVES = 2
PART_PAIRS = PAIRS // HALVES
PART_SLOTS = SLOTS // HALVES
RANK = 16
WIDTH = 4 * LANE + 4 * (BAND - LANE + 2 * RANK)
TILE = 256
STEPS = NLON // 2 // TILE
GROUP = 4
SMALL_BYTES = 16 * 2**20
FETCH_BYTES = int(45.5 * 2**20)
LARGE_BYTES = int(50 * 2**20)

LIFT_ALPHA = -1.586134342059924
LIFT_BETA = -0.052980118572961
LIFT_GAMMA = 0.882911075530934
LIFT_DELTA = 0.443506852043971
LIFT_KAPPA = 1.149604398860241


def analyze(values, levels, mode_name):
    if levels == 0:
        return values
    widths = [(4, 4)] + [(0, 0)] * (values.ndim - 1)
    extended = np.pad(values, widths, mode=mode_name)
    even, odd = extended[0::2], extended[1::2]
    first_d = odd[:-1] + LIFT_ALPHA * (even[:-1] + even[1:])
    first_s = even[1:-1] + LIFT_BETA * (first_d[:-1] + first_d[1:])
    second_d = first_d[1:-1] + LIFT_GAMMA * (first_s[:-1] + first_s[1:])
    second_s = first_s[1:-1] + LIFT_DELTA * (second_d[:-1] + second_d[1:])
    result = np.empty_like(values)
    result[0::2] = analyze(second_s * LIFT_KAPPA, levels - 1, mode_name)
    result[1::2] = second_d[1:] / LIFT_KAPPA
    return result


def longitude_matrices():
    waves = np.arange(NWAVE)
    phase = waves[:, None] * np.arange(NLON)[None, :] % NLON
    angle = phase * (2.0 * math.pi / NLON)
    weight = np.where(waves == 0, 1.0, 2.0)[:, None] / math.sqrt(2.0 * NWAVE)
    table = np.concatenate([weight * np.cos(angle), -weight * np.sin(angle)], axis=0)
    table = table.astype(np.float32).astype(ml_dtypes.bfloat16).astype(np.float64)
    lifted = analyze(table.T, WL, "wrap").T
    half = lifted[:, : NLON // 2].reshape(2 * NWAVE, STEPS, TILE).swapaxes(0, 1)
    middle = np.zeros((NWAVE, LANE))
    middle[:, 0] = lifted[:NWAVE, NLON // 2]
    return [values.astype(np.float32).astype(ml_dtypes.bfloat16) for values in (half, middle)]


def latitude_matrices():
    whole = analyze(np.eye(NLAT), WL, "reflect")

    def block(row_band, column_band):
        return whole[row_band * BAND : (row_band + 1) * BAND, column_band * BAND : (column_band + 1) * BAND]

    assert all(np.abs(block(band - 1, band) - block(6, 7)).max() < 1e-12 for band in range(1, BANDS))
    assert all(np.abs(block(band, band - 1) - block(8, 7)).max() < 1e-12 for band in range(1, BANDS))
    inner = whole[:, 7 * BAND : 8 * BAND]
    assert np.abs(inner[: 6 * BAND]).max() == 0 and np.abs(inner[9 * BAND :]).max() == 0
    assert all(np.abs(block(band, band) - block(7, 7)).max() < 1e-12 for band in range(1, BANDS - 1))
    expand = np.zeros((BAND, 2 * RANK))
    project = np.zeros((BAND, 2 * RANK))
    for side, part in enumerate((block(6, 7), block(8, 7))):
        left, sizes, right = np.linalg.svd(part)
        rank = int((sizes > 1e-12).sum())
        assert rank <= RANK
        expand[:, side * RANK : side * RANK + rank] = left[:, :rank] * sizes[:rank]
        project[:, side * RANK : side * RANK + rank] = right[:rank].T
    out = np.zeros((3, BAND, 2 * LANE))
    for variant, band in enumerate((0, 7, BANDS - 1)):
        own = block(band, band).T
        tail = np.concatenate([own[:, LANE:], project], axis=1)
        out[variant] = np.concatenate([own[:, :LANE], tail, tail], axis=1)
    return (
        out.astype(np.float32).astype(ml_dtypes.bfloat16),
        expand.astype(np.float32).astype(ml_dtypes.bfloat16),
    )


def pack_kernel(order_ref, spectra_ref, order_any, writer_any, matrix_any, *refs):
    outs, (order_out, writer_out, matrix_out) = refs[:HALVES], refs[HALVES : HALVES + 3]
    wide, low, high, packed, sems = refs[HALVES + 3 :]
    band = lax.axis_index("lat")
    variant = jnp.where(band == 0, 0, jnp.where(band == BANDS - 1, 2, 1))
    copies = [
        pltpu.make_async_copy(order_any, order_out, sems.at[0]),
        pltpu.make_async_copy(writer_any, writer_out, sems.at[1]),
        pltpu.make_async_copy(matrix_any.at[variant], matrix_out, sems.at[2]),
    ]
    for copy in copies:
        copy.start()
    first = lax.axis_index("wave") * SLOTS
    for pair in range(PAIRS):
        low[pl.ds(pair, 1), :] = jnp.full((1, LANE), order_ref[first + 2 * pair], jnp.int32)
        high[pl.ds(pair, 1), :] = jnp.full((1, LANE), order_ref[first + 2 * pair + 1], jnp.int32)
    waves_a, waves_b = low[...], high[...]
    lane = lax.broadcasted_iota(jnp.int32, (PAIRS, LANE), 1)
    zero = jnp.zeros((PAIRS, LANE), jnp.float32)
    for part in range(2):
        firsts, seconds = [], []
        for block in range(5):
            wide[block] = spectra_ref[0, part, :, block * LANE : (block + 1) * LANE].astype(jnp.float32)
            values = wide[block, pl.ds(0, PAIRS, stride=2), :]
            firsts.append(jnp.where(lane + block * LANE >= waves_a, values, zero))
            values = wide[block, pl.ds(1, PAIRS, stride=2), :]
            seconds.append(jnp.where(lane + block * LANE >= waves_b, values, zero))
        for block in range(BLOCKS):
            taken = firsts[block - 1] if block else zero
            for cut in range(block, 5):
                inside = (waves_a >= cut * LANE) & (waves_a < (cut + 1) * LANE)
                taken = jnp.where(inside, seconds[4 - cut + block], taken)
            for half in range(HALVES):
                packed[half, pl.ds(part * PART_PAIRS, PART_PAIRS), block * LANE : (block + 1) * LANE] = taken[
                    half * PART_PAIRS : (half + 1) * PART_PAIRS
                ]
    for half in range(HALVES):
        outs[half][...] = packed[half].astype(jnp.bfloat16)
    for copy in copies:
        copy.wait()


def fetch_kernel(order_ref, legendre_ref, *refs):
    outs, sems = refs[:HALVES], refs[HALVES]
    first = lax.axis_index("wave") * SLOTS
    for half in range(HALVES):

        def fetch(member, carry, half=half):
            pair = half * PART_PAIRS + member
            block = order_ref[first + 2 * pair] // LANE
            for cut in range(5):

                @pl.when(block == cut)
                def _():
                    pltpu.make_async_copy(
                        legendre_ref.at[2 * pair + 1, :, pl.ds((4 - cut) * LANE, (cut + 1) * LANE)],
                        outs[half].at[member, :, pl.ds(0, (cut + 1) * LANE)],
                        sems.at[half],
                    ).start()
                    pltpu.make_async_copy(
                        legendre_ref.at[2 * pair, :, pl.ds(cut * LANE, (5 - cut) * LANE)],
                        outs[half].at[member, :, pl.ds((cut + 1) * LANE, (5 - cut) * LANE)],
                        sems.at[half],
                    ).start()

            return carry

        lax.fori_loop(0, PART_PAIRS, fetch, 0)
    for half in range(HALVES):
        pltpu.make_async_copy(outs[half], outs[half], sems.at[half]).wait()


def legendre_kernel(half, order_ref, writer_ref, *refs):
    parts = refs[:4]
    held, matrix, out_ref = refs[4:7]
    spread, rows, results = refs[7:]
    base = half * PART_PAIRS
    first = lax.axis_index("wave") * SLOTS + 2 * base
    band = lax.axis_index("lat")
    band_x, band_z = band // 4, lax.rem(band, 4)
    steps = (0, 3, 1, 2)
    for outer in range(4):
        for inner in range(4):
            along_x, along_z = (outer, inner) if half == 0 else (inner, outer)
            field = 4 * lax.rem(band_x + steps[along_x], 4) + lax.rem(band_z + steps[along_z], 4)
            start = pl.multiple_of(field * 2 * PART_PAIRS, 8)
            for block in range(BLOCKS):
                values = parts[outer][inner, :, block * LANE : (block + 1) * LANE]
                spread[block, pl.ds(start, 2 * PART_PAIRS), :] = values.astype(jnp.float32)

    def contract(group, carry):
        for member in range(GROUP):
            pair = group * GROUP + member
            wave = order_ref[first + 2 * pair]
            lower, upper = [], []
            for block in range(BLOCKS):
                values = spread[block, pl.ds(pair, 2 * FIELDS, stride=PART_PAIRS), :].astype(jnp.bfloat16)
                from_a = wave < block * LANE
                lower.append(jnp.where(from_a, values, jnp.zeros_like(values)))
                upper.append(jnp.where(from_a, jnp.zeros_like(values), values))
            left = jnp.concatenate(
                [jnp.concatenate(lower, axis=1), jnp.concatenate(upper, axis=1)], axis=0
            )
            sums = lax.dot_general(
                left, held[pair], (((1,), (1,)), ((), ())), preferred_element_type=jnp.float32
            )
            for which in range(2):
                piece = sums[which * 2 * FIELDS : (which + 1) * 2 * FIELDS]
                where = pl.ds(2 * pair + which, 2 * FIELDS, stride=PART_SLOTS)
                rows[0, where, :] = piece[:, :LANE]
                rows[1, where, : BAND - LANE] = piece[:, LANE:]
        return carry

    lax.fori_loop(0, PART_PAIRS // GROUP, contract, 0)

    chunk = 2 * FIELDS * PART_SLOTS // 4
    for index in range(4):
        picked = slice(index * chunk, (index + 1) * chunk)
        left = jnp.concatenate([rows[0, picked, :], rows[1, picked, : BAND - LANE]], axis=1).astype(jnp.bfloat16)
        sums = jnp.dot(left, matrix[...], preferred_element_type=jnp.float32)
        results[0, picked, :] = sums[:, :LANE]
        results[1, picked, :] = sums[:, LANE:]

    lane = lax.broadcasted_iota(jnp.int32, (PART_SLOTS, LANE), 1)
    for owner in range(OWNERS):
        for member in range(2):
            field = writer_ref[2 * owner + member]
            tails = []
            for part in range(2):
                start = pl.multiple_of((2 * field + part) * PART_SLOTS, 8)
                place = (2 * member + part) * LANE
                out_ref[owner, :, place : place + LANE] = results[0, pl.ds(start, PART_SLOTS), :].astype(jnp.bfloat16)
                tails.append(results[1, pl.ds(start, PART_SLOTS), :])
            place = (4 + member) * LANE
            out_ref[owner, :, place : place + LANE] = jnp.where(lane < LANE // 2, *tails).astype(jnp.bfloat16)


def edge_kernel(order_ref, *refs):
    waves = refs[:HALVES]
    chosen_ref, rest_ref, above_ref, below_ref = refs[HALVES:]
    row = lax.broadcasted_iota(jnp.int32, (NWAVE, NWAVE), 0)
    chosen_ref[...] = jnp.where(row == order_ref[...], 1.0, 0.0).astype(jnp.bfloat16)
    count = NWAVE // HALVES
    ordered = sum(
        jnp.dot(
            chosen_ref[:, half * count : (half + 1) * count],
            waves[half][...],
            preferred_element_type=jnp.float32,
        )
        for half in range(HALVES)
    )
    turned = ordered.T.astype(jnp.bfloat16)
    rest = BAND - LANE
    for part in range(4):
        start = part * (rest + 2 * RANK)
        rest_ref[part * rest : (part + 1) * rest] = turned[start : start + rest]
        above_ref[part * RANK : (part + 1) * RANK] = turned[start + rest : start + rest + RANK]
        below_ref[part * RANK : (part + 1) * RANK] = turned[start + rest + RANK : start + rest + 2 * RANK]


def order_kernel(chosen_ref, *refs):
    waves, out_ref = refs[:HALVES], refs[HALVES]
    count = NWAVE // HALVES
    ordered = sum(
        jnp.dot(
            chosen_ref[:, half * count : (half + 1) * count],
            waves[half][...],
            preferred_element_type=jnp.float32,
        )
        for half in range(HALVES)
    )
    out_ref[...] = ordered.T.astype(jnp.bfloat16)


def synthesis_kernel(main_ref, rest_ref, above_ref, below_ref, expand_ref, middle_ref, table_ref, out_ref, *refs):
    left, table, tiles, even, flip, table_sems, out_sems = refs
    tables = [pltpu.make_async_copy(table_ref.at[step], table.at[step], table_sems.at[step]) for step in range(STEPS)]
    for copy in reversed(tables):
        copy.start()
    rest = BAND - LANE
    for field in range(2):
        for part in range(2):
            which = 2 * field + part
            edges = slice(which * RANK, (which + 1) * RANK)
            added = jnp.dot(
                expand_ref[...],
                jnp.concatenate([above_ref[edges], below_ref[edges]], axis=0),
                preferred_element_type=jnp.float32,
            )
            own = main_ref[which * LANE : (which + 1) * LANE].astype(jnp.float32)
            left[part, field * BAND : field * BAND + LANE] = (own + added[:LANE]).astype(jnp.bfloat16)
            own = rest_ref[which * rest : (which + 1) * rest].astype(jnp.float32)
            left[part, field * BAND + LANE : (field + 1) * BAND] = (own + added[LANE:]).astype(jnp.bfloat16)
    total = lax.broadcasted_iota(jnp.int32, (TILE, TILE), 0) + lax.broadcasted_iota(jnp.int32, (TILE, TILE), 1)
    flip[...] = jnp.where(total == TILE, 1.0, 0.0).astype(jnp.bfloat16)
    even[...] = jnp.dot(left[0], middle_ref[...], preferred_element_type=jnp.float32)

    def place(tile, where):
        return [
            pltpu.make_async_copy(
                tiles.at[tile, field],
                out_ref.at[field, :, pl.ds(where, TILE)],
                out_sems.at[tile, field],
            )
            for field in range(2)
        ]

    def step(count, carry):
        tile = STEPS - 1 - count
        pltpu.make_async_copy(table_ref.at[tile], table.at[tile], table_sems.at[tile]).wait()
        cosine = jnp.dot(left[0], table[tile, :NWAVE], preferred_element_type=jnp.float32)
        sine = jnp.dot(left[1], table[tile, NWAVE:], preferred_element_type=jnp.float32)
        front = (cosine + sine).astype(jnp.bfloat16)
        back = cosine - sine
        turned = jnp.dot(back.astype(jnp.bfloat16), flip[...], preferred_element_type=jnp.float32)
        lane = lax.broadcasted_iota(jnp.int32, (2 * BAND, LANE), 1)
        mirror = 2 * STEPS - 1 - tile
        head = jnp.where(lane == 0, even[...], turned[:, :LANE]).astype(jnp.bfloat16)
        tail = turned[:, LANE:].astype(jnp.bfloat16)
        even[...] = back[:, :LANE]
        for field in range(2):
            rows = slice(field * BAND, (field + 1) * BAND)
            tiles[tile, field] = front[rows]
            tiles[mirror, field, :, :LANE] = head[rows]
            tiles[mirror, field, :, LANE:] = tail[rows]
        for which in (tile, mirror):
            for copy in place(which, pl.multiple_of(which * TILE, TILE)):
                copy.start()
        return carry

    lax.fori_loop(0, STEPS, step, 0)
    for tile in range(2 * STEPS):
        for copy in place(tile, tile * TILE):
            copy.wait()


def along_z(step):
    return [(4 * x + z, 4 * x + (z + step) % 4) for x in range(4) for z in range(4)]


def along_x(step):
    return [(4 * x + z, 4 * ((x + step) % 4) + z) for x in range(4) for z in range(4)]


def neighbour(step):
    return [(band, band + step) for band in range(BANDS) if 0 <= band + step < BANDS]


SMEM = pl.BlockSpec(memory_space=pltpu.SMEM)
VMEM = pl.BlockSpec(memory_space=pltpu.VMEM)
ANY = pl.BlockSpec(memory_space=pl.ANY)
FETCH = pltpu.CompilerParams(vmem_limit_bytes=FETCH_BYTES)
SMALL = pltpu.CompilerParams(vmem_limit_bytes=SMALL_BYTES)
LARGE = pltpu.CompilerParams(vmem_limit_bytes=LARGE_BYTES)


def bf16(*shape):
    return jax.ShapeDtypeStruct(shape, jnp.bfloat16)


def make_on_device(table, middle, matrices, expand):
    def on_device(spectra, legendre, wave_order, writer_order):
        *halves, orders, writers, matrix = pl.pallas_call(
            pack_kernel,
            out_shape=[bf16(2 * PART_PAIRS, BLOCKS * LANE)] * HALVES
            + [
                jax.ShapeDtypeStruct((NWAVE,), jnp.int32),
                jax.ShapeDtypeStruct((FIELDS,), jnp.int32),
                bf16(BAND, 2 * LANE),
            ],
            in_specs=[SMEM, VMEM, ANY, ANY, ANY],
            out_specs=[VMEM] * HALVES + [ANY] * 3,
            scratch_shapes=[
                pltpu.VMEM((5, SLOTS, LANE), jnp.float32),
                pltpu.VMEM((PAIRS, LANE), jnp.int32),
                pltpu.VMEM((PAIRS, LANE), jnp.int32),
                pltpu.VMEM((HALVES, 2 * PART_PAIRS, BLOCKS * LANE), jnp.float32),
                pltpu.SemaphoreType.DMA((3,)),
            ],
            name="pack",
        )(wave_order, spectra, wave_order, writer_order, matrices)
        order = wave_order.reshape(OWNERS, HALVES, PART_SLOTS).swapaxes(0, 1).reshape(1, NWAVE)
        held = pl.pallas_call(
            fetch_kernel,
            out_shape=[bf16(PART_PAIRS, BAND, BLOCKS * LANE)] * HALVES,
            in_specs=[SMEM, ANY],
            out_specs=[VMEM] * HALVES,
            scratch_shapes=[pltpu.SemaphoreType.DMA((HALVES,))],
            compiler_params=FETCH,
            cost_estimate=pl.CostEstimate(flops=0, bytes_accessed=14_000_000, transcendentals=0),
            name="fetch",
        )(orders, legendre)

        axes = ((along_z, along_x), (along_x, along_z))
        gathered = halves
        for stage in range(2):
            arrived = [
                [values] + [lax.ppermute(values, "lat", axes[half][stage](step)) for step in (1, 3, 2)]
                for half, values in enumerate(gathered)
            ]
            if stage == 0:
                gathered, held = lax.optimization_barrier(([jnp.stack(blocks) for blocks in arrived], held))
            else:
                gathered = arrived

        waves = []
        for half in range(HALVES):
            lifted = pl.pallas_call(
                lambda *refs, half=half: legendre_kernel(half, *refs),
                out_shape=bf16(OWNERS, PART_SLOTS, WIDTH),
                in_specs=[SMEM, SMEM] + [VMEM] * 6,
                out_specs=VMEM,
                scratch_shapes=[
                    pltpu.VMEM((BLOCKS, 2 * FIELDS * PART_PAIRS, LANE), jnp.float32),
                    pltpu.VMEM((2, 2 * FIELDS * PART_SLOTS, LANE), jnp.float32),
                    pltpu.VMEM((2, 2 * FIELDS * PART_SLOTS, LANE), jnp.float32),
                ],
                compiler_params=SMALL,
                cost_estimate=pl.CostEstimate(flops=400_000_000, bytes_accessed=8_000_000, transcendentals=0),
                name=f"legendre{half}",
            )(orders, writers, *gathered[half], held[half], matrix)
            if half + 1 < HALVES:
                lifted, gathered[half + 1] = lax.optimization_barrier((lifted, gathered[half + 1]))
            if waves:
                lifted, waves[-1] = lax.optimization_barrier((lifted, waves[-1]))
            received = lax.all_to_all(lifted, "wave", split_axis=0, concat_axis=0, tiled=True)
            waves.append(received.reshape(OWNERS * PART_SLOTS, WIDTH))

        main, rest = 4 * LANE, 4 * (BAND - LANE)
        count = NWAVE // HALVES
        chosen, tail, above, below = pl.pallas_call(
            edge_kernel,
            grid=(1,),
            out_shape=[bf16(NWAVE, NWAVE), bf16(rest, NWAVE), bf16(4 * RANK, NWAVE), bf16(4 * RANK, NWAVE)],
            in_specs=[pl.BlockSpec((1, NWAVE), lambda i: (0, 0))]
            + [pl.BlockSpec((count, WIDTH - main), lambda i: (0, main // (WIDTH - main)))] * HALVES,
            out_specs=[VMEM] * 4,
            compiler_params=SMALL,
            name="edges",
        )(order, *waves)
        above = lax.ppermute(above, "lat", neighbour(-1))
        below = lax.ppermute(below, "lat", neighbour(1))
        ordered = pl.pallas_call(
            order_kernel,
            grid=(1,),
            out_shape=bf16(main, NWAVE),
            in_specs=[pl.BlockSpec((NWAVE, NWAVE), lambda i: (0, 0))]
            + [pl.BlockSpec((count, main), lambda i: (0, 0))] * HALVES,
            out_specs=VMEM,
            compiler_params=SMALL,
            cost_estimate=pl.CostEstimate(flops=800_000_000, bytes_accessed=4_000_000, transcendentals=0),
            name="order",
        )(chosen, *waves)
        return pl.pallas_call(
            synthesis_kernel,
            out_shape=bf16(2, BAND, NLON),
            in_specs=[VMEM] * 6 + [ANY],
            out_specs=ANY,
            scratch_shapes=[
                pltpu.VMEM((2, 2 * BAND, NWAVE), jnp.bfloat16),
                pltpu.VMEM((STEPS, 2 * NWAVE, TILE), jnp.bfloat16),
                pltpu.VMEM((2 * STEPS, 2, BAND, TILE), jnp.bfloat16),
                pltpu.VMEM((2 * BAND, LANE), jnp.float32),
                pltpu.VMEM((TILE, TILE), jnp.bfloat16),
                pltpu.SemaphoreType.DMA((STEPS,)),
                pltpu.SemaphoreType.DMA((2 * STEPS, 2)),
            ],
            compiler_params=LARGE,
            cost_estimate=pl.CostEstimate(flops=2_400_000_000, bytes_accessed=11_000_000, transcendentals=0),
            name="synthesis",
        )(ordered, tail, above, below, expand, middle, table)

    return on_device


def solution(mesh):
    constants = [*longitude_matrices(), *latitude_matrices()]
    return jax.shard_map(
        make_on_device(*[jnp.asarray(values) for values in constants]),
        mesh=mesh,
        in_specs=(P("lat", None, "wave", None), P("wave", "lat", None), P(), P()),
        out_specs=P("wave", "lat", None),
        check_vma=False,
    )
```

```python
import math

import jax
import jax.numpy as jnp
import ml_dtypes
import numpy as np
from jax import lax
from jax.experimental import pallas as pl
from jax.experimental.pallas import tpu as pltpu
from jax.sharding import PartitionSpec as P

NLAT = 2560
NLON = 5120
NWAVE = 640
WL = 5
BANDS = 16
OWNERS = 8
BAND = NLAT // BANDS
SLOTS = NWAVE // OWNERS
PAIRS = SLOTS // 2
FIELDS = 16
BLOCKS = 6
LANE = 128
HALVES = 2
PART_PAIRS = PAIRS // HALVES
PART_SLOTS = SLOTS // HALVES
RANK = 16
WIDTH = 4 * LANE + 4 * (BAND - LANE + 2 * RANK)
TILE = 256
STEPS = NLON // 2 // TILE
GROUP = 4
SMALL_BYTES = 16 * 2**20
FETCH_BYTES = 44 * 2**20
LARGE_BYTES = 50 * 2**20

LIFT_ALPHA = -1.586134342059924
LIFT_BETA = -0.052980118572961
LIFT_GAMMA = 0.882911075530934
LIFT_DELTA = 0.443506852043971
LIFT_KAPPA = 1.149604398860241


def analyze(values, levels, mode_name):
    if levels == 0:
        return values
    widths = [(4, 4)] + [(0, 0)] * (values.ndim - 1)
    extended = np.pad(values, widths, mode=mode_name)
    even, odd = extended[0::2], extended[1::2]
    first_d = odd[:-1] + LIFT_ALPHA * (even[:-1] + even[1:])
    first_s = even[1:-1] + LIFT_BETA * (first_d[:-1] + first_d[1:])
    second_d = first_d[1:-1] + LIFT_GAMMA * (first_s[:-1] + first_s[1:])
    second_s = first_s[1:-1] + LIFT_DELTA * (second_d[:-1] + second_d[1:])
    result = np.empty_like(values)
    result[0::2] = analyze(second_s * LIFT_KAPPA, levels - 1, mode_name)
    result[1::2] = second_d[1:] / LIFT_KAPPA
    return result


def longitude_matrices():
    waves = np.arange(NWAVE)
    phase = waves[:, None] * np.arange(NLON)[None, :] % NLON
    angle = phase * (2.0 * math.pi / NLON)
    weight = np.where(waves == 0, 1.0, 2.0)[:, None] / math.sqrt(2.0 * NWAVE)
    table = np.concatenate([weight * np.cos(angle), -weight * np.sin(angle)], axis=0)
    table = table.astype(np.float32).astype(ml_dtypes.bfloat16).astype(np.float64)
    lifted = analyze(table.T, WL, "wrap").T
    half = lifted[:, : NLON // 2].reshape(2 * NWAVE, STEPS, TILE).swapaxes(0, 1)
    middle = np.zeros((NWAVE, LANE))
    middle[:, 0] = lifted[:NWAVE, NLON // 2]
    return [values.astype(np.float32).astype(ml_dtypes.bfloat16) for values in (half, middle)]


def latitude_matrices():
    whole = analyze(np.eye(NLAT), WL, "reflect")

    def block(row_band, column_band):
        return whole[row_band * BAND : (row_band + 1) * BAND, column_band * BAND : (column_band + 1) * BAND]

    assert all(np.abs(block(band - 1, band) - block(6, 7)).max() < 1e-12 for band in range(1, BANDS))
    assert all(np.abs(block(band, band - 1) - block(8, 7)).max() < 1e-12 for band in range(1, BANDS))
    inner = whole[:, 7 * BAND : 8 * BAND]
    assert np.abs(inner[: 6 * BAND]).max() == 0 and np.abs(inner[9 * BAND :]).max() == 0
    assert all(np.abs(block(band, band) - block(7, 7)).max() < 1e-12 for band in range(1, BANDS - 1))
    expand = np.zeros((BAND, 2 * RANK))
    project = np.zeros((BAND, 2 * RANK))
    for side, part in enumerate((block(6, 7), block(8, 7))):
        left, sizes, right = np.linalg.svd(part)
        rank = int((sizes > 1e-12).sum())
        assert rank <= RANK
        expand[:, side * RANK : side * RANK + rank] = left[:, :rank] * sizes[:rank]
        project[:, side * RANK : side * RANK + rank] = right[:rank].T
    out = np.zeros((3, BAND, 2 * LANE))
    for variant, band in enumerate((0, 7, BANDS - 1)):
        own = block(band, band).T
        tail = np.concatenate([own[:, LANE:], project], axis=1)
        out[variant] = np.concatenate([own[:, :LANE], tail, tail], axis=1)
    return (
        out.astype(np.float32).astype(ml_dtypes.bfloat16),
        expand.astype(np.float32).astype(ml_dtypes.bfloat16),
    )


def pack_kernel(order_ref, spectra_ref, *refs):
    outs, (wide, low, high, packed) = refs[:HALVES], refs[HALVES:]
    first = lax.axis_index("wave") * SLOTS
    for pair in range(PAIRS):
        low[pl.ds(pair, 1), :] = jnp.full((1, LANE), order_ref[first + 2 * pair], jnp.int32)
        high[pl.ds(pair, 1), :] = jnp.full((1, LANE), order_ref[first + 2 * pair + 1], jnp.int32)
    waves_a, waves_b = low[...], high[...]
    lane = lax.broadcasted_iota(jnp.int32, (PAIRS, LANE), 1)
    for part in range(2):
        for block in range(5):
            wide[block] = spectra_ref[0, part, :, block * LANE : (block + 1) * LANE].astype(jnp.float32)
        for block in range(BLOCKS):
            taken = jnp.zeros((PAIRS, LANE), jnp.float32)
            if block <= 4:
                values = wide[4 - block, pl.ds(1, PAIRS, stride=2), :]
                taken = jnp.where(lane + (4 - block) * LANE >= waves_b, values, taken)
            if block >= 1:
                values = wide[block - 1, pl.ds(0, PAIRS, stride=2), :]
                values = jnp.where(lane + (block - 1) * LANE >= waves_a, values, jnp.zeros_like(values))
                taken = jnp.where(waves_a < block * LANE, values, taken)
            for half in range(HALVES):
                packed[half, pl.ds(part * PART_PAIRS, PART_PAIRS), block * LANE : (block + 1) * LANE] = taken[
                    half * PART_PAIRS : (half + 1) * PART_PAIRS
                ]
    for half in range(HALVES):
        outs[half][...] = packed[half].astype(jnp.bfloat16)


def fetch_kernel(order_ref, writer_ref, matrix_ref, legendre_ref, order_out, writer_out, matrix_out, held_out, sems):
    band = lax.axis_index("lat")
    variant = jnp.where(band == 0, 0, jnp.where(band == BANDS - 1, 2, 1))
    copies = [
        pltpu.make_async_copy(legendre_ref.at[pl.ds(0, PART_SLOTS)], held_out, sems.at[0]),
        pltpu.make_async_copy(order_ref, order_out, sems.at[1]),
        pltpu.make_async_copy(writer_ref, writer_out, sems.at[2]),
        pltpu.make_async_copy(matrix_ref.at[variant], matrix_out, sems.at[3]),
    ]
    for copy in copies:
        copy.start()
    for copy in copies:
        copy.wait()


def legendre_kernel(half, order_ref, writer_ref, *refs):
    parts = refs[:4]
    legendre_ref, matrix, out_ref = refs[4:7]
    spread, rows, results = refs[7:10]
    held, copies = legendre_ref, []
    if half:
        held, sems = refs[10:]
        for index in range(2):
            some = PART_SLOTS // 2
            source = legendre_ref.at[pl.ds(half * PART_SLOTS + index * some, some)]
            copies.append(pltpu.make_async_copy(source, held.at[pl.ds(index * some, some)], sems.at[index]))
            copies[-1].start()
    base = half * PART_PAIRS
    first = lax.axis_index("wave") * SLOTS + 2 * base
    band = lax.axis_index("lat")
    band_x, band_z = band // 4, lax.rem(band, 4)
    steps = (0, 3, 1, 2)
    for outer in range(4):
        for inner in range(4):
            along_x, along_z = (outer, inner) if half == 0 else (inner, outer)
            field = 4 * lax.rem(band_x + steps[along_x], 4) + lax.rem(band_z + steps[along_z], 4)
            start = pl.multiple_of(field * 2 * PART_PAIRS, 8)
            for block in range(BLOCKS):
                values = parts[outer][inner, :, block * LANE : (block + 1) * LANE]
                spread[block, pl.ds(start, 2 * PART_PAIRS), :] = values.astype(jnp.float32)

    def contract(group, carry):
        for member in range(GROUP):
            pair = group * GROUP + member
            wave = order_ref[first + 2 * pair]
            lower, upper, values_of_n = [], [], []
            for block in range(BLOCKS):
                values = spread[block, pl.ds(pair, 2 * FIELDS, stride=PART_PAIRS), :].astype(jnp.bfloat16)
                from_a = wave < block * LANE
                slot = 2 * pair + jnp.where(from_a, 0, 1)
                source = pl.multiple_of(jnp.where(from_a, block - 1, 4 - block) * LANE, LANE)
                values_of_n.append(held[slot, :, pl.ds(source, LANE)])
                lower.append(jnp.where(from_a, values, jnp.zeros_like(values)))
                upper.append(jnp.where(from_a, jnp.zeros_like(values), values))
            left = jnp.concatenate(
                [jnp.concatenate(lower, axis=1), jnp.concatenate(upper, axis=1)], axis=0
            )
            sums = lax.dot_general(
                left, jnp.concatenate(values_of_n, axis=1), (((1,), (1,)), ((), ())), preferred_element_type=jnp.float32
            )
            for which in range(2):
                piece = sums[which * 2 * FIELDS : (which + 1) * 2 * FIELDS]
                where = pl.ds(2 * pair + which, 2 * FIELDS, stride=PART_SLOTS)
                rows[0, where, :] = piece[:, :LANE]
                rows[1, where, : BAND - LANE] = piece[:, LANE:]
        return carry

    for copy in copies:
        copy.wait()
    lax.fori_loop(0, PART_PAIRS // GROUP, contract, 0)

    chunk = 2 * FIELDS * PART_SLOTS // 4
    for index in range(4):
        picked = slice(index * chunk, (index + 1) * chunk)
        left = jnp.concatenate([rows[0, picked, :], rows[1, picked, : BAND - LANE]], axis=1).astype(jnp.bfloat16)
        sums = jnp.dot(left, matrix[...], preferred_element_type=jnp.float32)
        results[0, picked, :] = sums[:, :LANE]
        results[1, picked, :] = sums[:, LANE:]

    lane = lax.broadcasted_iota(jnp.int32, (PART_SLOTS, LANE), 1)
    for owner in range(OWNERS):
        for member in range(2):
            field = writer_ref[2 * owner + member]
            tails = []
            for part in range(2):
                start = pl.multiple_of((2 * field + part) * PART_SLOTS, 8)
                place = (2 * member + part) * LANE
                out_ref[owner, :, place : place + LANE] = results[0, pl.ds(start, PART_SLOTS), :].astype(jnp.bfloat16)
                tails.append(results[1, pl.ds(start, PART_SLOTS), :])
            place = (4 + member) * LANE
            out_ref[owner, :, place : place + LANE] = jnp.where(lane < LANE // 2, *tails).astype(jnp.bfloat16)


def edge_kernel(order_ref, *refs):
    waves = refs[:HALVES]
    chosen_ref, rest_ref, above_ref, below_ref = refs[HALVES:]
    row = lax.broadcasted_iota(jnp.int32, (NWAVE, NWAVE), 0)
    chosen_ref[...] = jnp.where(row == order_ref[...], 1.0, 0.0).astype(jnp.bfloat16)
    count = NWAVE // HALVES
    ordered = sum(
        jnp.dot(
            chosen_ref[:, half * count : (half + 1) * count],
            waves[half][...],
            preferred_element_type=jnp.float32,
        )
        for half in range(HALVES)
    )
    turned = ordered.T.astype(jnp.bfloat16)
    rest = BAND - LANE
    for part in range(4):
        start = part * (rest + 2 * RANK)
        rest_ref[part * rest : (part + 1) * rest] = turned[start : start + rest]
        above_ref[part * RANK : (part + 1) * RANK] = turned[start + rest : start + rest + RANK]
        below_ref[part * RANK : (part + 1) * RANK] = turned[start + rest + RANK : start + rest + 2 * RANK]


def order_kernel(chosen_ref, *refs):
    waves, out_ref = refs[:HALVES], refs[HALVES]
    count = NWAVE // HALVES
    ordered = sum(
        jnp.dot(
            chosen_ref[:, half * count : (half + 1) * count],
            waves[half][...],
            preferred_element_type=jnp.float32,
        )
        for half in range(HALVES)
    )
    out_ref[...] = ordered.T.astype(jnp.bfloat16)


def synthesis_kernel(main_ref, rest_ref, above_ref, below_ref, expand_ref, middle_ref, table_ref, out_ref, *refs):
    left, table, tiles, even, flip, table_sems, out_sems = refs
    tables = [pltpu.make_async_copy(table_ref.at[step], table.at[step], table_sems.at[step]) for step in range(STEPS)]
    for copy in reversed(tables):
        copy.start()
    rest = BAND - LANE
    for field in range(2):
        for part in range(2):
            which = 2 * field + part
            edges = slice(which * RANK, (which + 1) * RANK)
            added = jnp.dot(
                expand_ref[...],
                jnp.concatenate([above_ref[edges], below_ref[edges]], axis=0),
                preferred_element_type=jnp.float32,
            )
            own = main_ref[which * LANE : (which + 1) * LANE].astype(jnp.float32)
            left[part, field * BAND : field * BAND + LANE] = (own + added[:LANE]).astype(jnp.bfloat16)
            own = rest_ref[which * rest : (which + 1) * rest].astype(jnp.float32)
            left[part, field * BAND + LANE : (field + 1) * BAND] = (own + added[LANE:]).astype(jnp.bfloat16)
    total = lax.broadcasted_iota(jnp.int32, (TILE, TILE), 0) + lax.broadcasted_iota(jnp.int32, (TILE, TILE), 1)
    flip[...] = jnp.where(total == TILE, 1.0, 0.0).astype(jnp.bfloat16)
    even[...] = jnp.dot(left[0], middle_ref[...], preferred_element_type=jnp.float32)

    def place(tile, where):
        return [
            pltpu.make_async_copy(
                tiles.at[tile, field],
                out_ref.at[field, :, pl.ds(where, TILE)],
                out_sems.at[tile, field],
            )
            for field in range(2)
        ]

    def step(count, carry):
        tile = STEPS - 1 - count
        pltpu.make_async_copy(table_ref.at[tile], table.at[tile], table_sems.at[tile]).wait()
        cosine = jnp.dot(left[0], table[tile, :NWAVE], preferred_element_type=jnp.float32)
        sine = jnp.dot(left[1], table[tile, NWAVE:], preferred_element_type=jnp.float32)
        front = (cosine + sine).astype(jnp.bfloat16)
        back = cosine - sine
        turned = jnp.dot(back.astype(jnp.bfloat16), flip[...], preferred_element_type=jnp.float32)
        lane = lax.broadcasted_iota(jnp.int32, (2 * BAND, LANE), 1)
        mirror = 2 * STEPS - 1 - tile
        head = jnp.where(lane == 0, even[...], turned[:, :LANE]).astype(jnp.bfloat16)
        tail = turned[:, LANE:].astype(jnp.bfloat16)
        even[...] = back[:, :LANE]
        for field in range(2):
            rows = slice(field * BAND, (field + 1) * BAND)
            tiles[tile, field] = front[rows]
            tiles[mirror, field, :, :LANE] = head[rows]
            tiles[mirror, field, :, LANE:] = tail[rows]
        for which in (tile, mirror):
            for copy in place(which, pl.multiple_of(which * TILE, TILE)):
                copy.start()
        return carry

    lax.fori_loop(0, STEPS, step, 0)
    for tile in range(2 * STEPS):
        for copy in place(tile, tile * TILE):
            copy.wait()


def along_z(step):
    return [(4 * x + z, 4 * x + (z + step) % 4) for x in range(4) for z in range(4)]


def along_x(step):
    return [(4 * x + z, 4 * ((x + step) % 4) + z) for x in range(4) for z in range(4)]


def neighbour(step):
    return [(band, band + step) for band in range(BANDS) if 0 <= band + step < BANDS]


SMEM = pl.BlockSpec(memory_space=pltpu.SMEM)
VMEM = pl.BlockSpec(memory_space=pltpu.VMEM)
ANY = pl.BlockSpec(memory_space=pl.ANY)
FETCH = pltpu.CompilerParams(vmem_limit_bytes=FETCH_BYTES)
SMALL = pltpu.CompilerParams(vmem_limit_bytes=SMALL_BYTES)
LARGE = pltpu.CompilerParams(vmem_limit_bytes=LARGE_BYTES)


def bf16(*shape):
    return jax.ShapeDtypeStruct(shape, jnp.bfloat16)


def make_on_device(table, middle, matrices, expand):
    def on_device(spectra, legendre, wave_order, writer_order):
        halves = pl.pallas_call(
            pack_kernel,
            out_shape=[bf16(2 * PART_PAIRS, BLOCKS * LANE)] * HALVES,
            in_specs=[SMEM, VMEM],
            out_specs=[VMEM] * HALVES,
            scratch_shapes=[
                pltpu.VMEM((5, SLOTS, LANE), jnp.float32),
                pltpu.VMEM((PAIRS, LANE), jnp.int32),
                pltpu.VMEM((PAIRS, LANE), jnp.int32),
                pltpu.VMEM((HALVES, 2 * PART_PAIRS, BLOCKS * LANE), jnp.float32),
            ],
            name="pack",
        )(wave_order, spectra)
        order = wave_order.reshape(OWNERS, HALVES, PART_SLOTS).swapaxes(0, 1).reshape(1, NWAVE)

        axes = ((along_z, along_x), (along_x, along_z))
        gathered = halves
        for stage in range(2):
            arrived = [
                [values] + [lax.ppermute(values, "lat", axes[half][stage](step)) for step in (1, 3, 2)]
                for half, values in enumerate(gathered)
            ]
            gathered = arrived
            if stage == 0:
                gathered, legendre = lax.optimization_barrier(([jnp.stack(blocks) for blocks in arrived], legendre))

        orders, writers, matrix, held = pl.pallas_call(
            fetch_kernel,
            out_shape=[
                jax.ShapeDtypeStruct((NWAVE,), jnp.int32),
                jax.ShapeDtypeStruct((FIELDS,), jnp.int32),
                bf16(BAND, 2 * LANE),
                bf16(PART_SLOTS, BAND, NWAVE),
            ],
            in_specs=[ANY] * 4,
            out_specs=[ANY] * 3 + [VMEM],
            scratch_shapes=[pltpu.SemaphoreType.DMA((4,))],
            compiler_params=FETCH,
            cost_estimate=pl.CostEstimate(flops=0, bytes_accessed=14_000_000, transcendentals=0),
            name="fetch",
        )(wave_order, writer_order, matrices, legendre)

        waves = []
        for half in range(HALVES):
            lifted = pl.pallas_call(
                lambda *refs, half=half: legendre_kernel(half, *refs),
                out_shape=bf16(OWNERS, PART_SLOTS, WIDTH),
                in_specs=[SMEM, SMEM] + [VMEM] * 4 + [ANY if half else VMEM, VMEM],
                out_specs=VMEM,
                scratch_shapes=[
                    pltpu.VMEM((BLOCKS, 2 * FIELDS * PART_PAIRS, LANE), jnp.float32),
                    pltpu.VMEM((2, 2 * FIELDS * PART_SLOTS, LANE), jnp.float32),
                    pltpu.VMEM((2, 2 * FIELDS * PART_SLOTS, LANE), jnp.float32),
                ]
                + [pltpu.VMEM((PART_SLOTS, BAND, NWAVE), jnp.bfloat16), pltpu.SemaphoreType.DMA((2,))] * half,
                compiler_params=FETCH if half else SMALL,
                cost_estimate=pl.CostEstimate(flops=400_000_000, bytes_accessed=8_000_000, transcendentals=0),
                name=f"legendre{half}",
            )(orders, writers, *gathered[half], legendre if half else held, matrix)
            if half + 1 < HALVES:
                lifted, gathered[half + 1] = lax.optimization_barrier((lifted, gathered[half + 1]))
            if waves:
                lifted, waves[-1] = lax.optimization_barrier((lifted, waves[-1]))
            received = lax.all_to_all(lifted, "wave", split_axis=0, concat_axis=0, tiled=True)
            waves.append(received.reshape(OWNERS * PART_SLOTS, WIDTH))

        main, rest = 4 * LANE, 4 * (BAND - LANE)
        count = NWAVE // HALVES
        chosen, tail, above, below = pl.pallas_call(
            edge_kernel,
            grid=(1,),
            out_shape=[bf16(NWAVE, NWAVE), bf16(rest, NWAVE), bf16(4 * RANK, NWAVE), bf16(4 * RANK, NWAVE)],
            in_specs=[pl.BlockSpec((1, NWAVE), lambda i: (0, 0))]
            + [pl.BlockSpec((count, WIDTH - main), lambda i: (0, main // (WIDTH - main)))] * HALVES,
            out_specs=[VMEM] * 4,
            compiler_params=SMALL,
            name="edges",
        )(order, *waves)
        above = lax.ppermute(above, "lat", neighbour(-1))
        below = lax.ppermute(below, "lat", neighbour(1))
        ordered = pl.pallas_call(
            order_kernel,
            grid=(1,),
            out_shape=bf16(main, NWAVE),
            in_specs=[pl.BlockSpec((NWAVE, NWAVE), lambda i: (0, 0))]
            + [pl.BlockSpec((count, main), lambda i: (0, 0))] * HALVES,
            out_specs=VMEM,
            compiler_params=SMALL,
            cost_estimate=pl.CostEstimate(flops=800_000_000, bytes_accessed=4_000_000, transcendentals=0),
            name="order",
        )(chosen, *waves)
        return pl.pallas_call(
            synthesis_kernel,
            out_shape=bf16(2, BAND, NLON),
            in_specs=[VMEM] * 6 + [ANY],
            out_specs=ANY,
            scratch_shapes=[
                pltpu.VMEM((2, 2 * BAND, NWAVE), jnp.bfloat16),
                pltpu.VMEM((STEPS, 2 * NWAVE, TILE), jnp.bfloat16),
                pltpu.VMEM((2 * STEPS, 2, BAND, TILE), jnp.bfloat16),
                pltpu.VMEM((2 * BAND, LANE), jnp.float32),
                pltpu.VMEM((TILE, TILE), jnp.bfloat16),
                pltpu.SemaphoreType.DMA((STEPS,)),
                pltpu.SemaphoreType.DMA((2 * STEPS, 2)),
            ],
            compiler_params=LARGE,
            cost_estimate=pl.CostEstimate(flops=2_400_000_000, bytes_accessed=11_000_000, transcendentals=0),
            name="synthesis",
        )(ordered, tail, above, below, expand, middle, table)

    return on_device


def solution(mesh):
    constants = [*longitude_matrices(), *latitude_matrices()]
    return jax.shard_map(
        make_on_device(*[jnp.asarray(values) for values in constants]),
        mesh=mesh,
        in_specs=(P("lat", None, "wave", None), P("wave", "lat", None), P(), P()),
        out_specs=P("wave", "lat", None),
        check_vma=False,
    )
```

```python
import math

import jax
import jax.numpy as jnp
import ml_dtypes
import numpy as np
from jax import lax
from jax.experimental import pallas as pl
from jax.experimental.pallas import tpu as pltpu
from jax.sharding import PartitionSpec as P

NLAT = 2560
NLON = 5120
NWAVE = 640
WL = 5
BANDS = 16
OWNERS = 8
BAND = NLAT // BANDS
SLOTS = NWAVE // OWNERS
PAIRS = SLOTS // 2
FIELDS = 16
BLOCKS = 6
LANE = 128
HALVES = 2
PART_PAIRS = PAIRS // HALVES
PART_SLOTS = SLOTS // HALVES
RANK = 16
WIDTH = 4 * LANE + 4 * (BAND - LANE + 2 * RANK)
TILE = 256
STEPS = NLON // 2 // TILE
GROUP = 4
SMALL_BYTES = 16 * 2**20
MIDDLE_BYTES = 40 * 2**20
FETCH_BYTES = 44 * 2**20
LARGE_BYTES = 50 * 2**20

LIFT_ALPHA = -1.586134342059924
LIFT_BETA = -0.052980118572961
LIFT_GAMMA = 0.882911075530934
LIFT_DELTA = 0.443506852043971
LIFT_KAPPA = 1.149604398860241


def analyze(values, levels, mode_name):
    if levels == 0:
        return values
    widths = [(4, 4)] + [(0, 0)] * (values.ndim - 1)
    extended = np.pad(values, widths, mode=mode_name)
    even, odd = extended[0::2], extended[1::2]
    first_d = odd[:-1] + LIFT_ALPHA * (even[:-1] + even[1:])
    first_s = even[1:-1] + LIFT_BETA * (first_d[:-1] + first_d[1:])
    second_d = first_d[1:-1] + LIFT_GAMMA * (first_s[:-1] + first_s[1:])
    second_s = first_s[1:-1] + LIFT_DELTA * (second_d[:-1] + second_d[1:])
    result = np.empty_like(values)
    result[0::2] = analyze(second_s * LIFT_KAPPA, levels - 1, mode_name)
    result[1::2] = second_d[1:] / LIFT_KAPPA
    return result


def longitude_matrices():
    waves = np.arange(NWAVE)
    phase = waves[:, None] * np.arange(NLON)[None, :] % NLON
    angle = phase * (2.0 * math.pi / NLON)
    weight = np.where(waves == 0, 1.0, 2.0)[:, None] / math.sqrt(2.0 * NWAVE)
    table = np.concatenate([weight * np.cos(angle), -weight * np.sin(angle)], axis=0)
    table = table.astype(np.float32).astype(ml_dtypes.bfloat16).astype(np.float64)
    lifted = analyze(table.T, WL, "wrap").T
    half = lifted[:, : NLON // 2].reshape(2 * NWAVE, STEPS, TILE).swapaxes(0, 1)
    middle = np.zeros((NWAVE, LANE))
    middle[:, 0] = lifted[:NWAVE, NLON // 2]
    return [values.astype(np.float32).astype(ml_dtypes.bfloat16) for values in (half, middle)]


def latitude_matrices():
    whole = analyze(np.eye(NLAT), WL, "reflect")

    def block(row_band, column_band):
        return whole[row_band * BAND : (row_band + 1) * BAND, column_band * BAND : (column_band + 1) * BAND]

    assert all(np.abs(block(band - 1, band) - block(6, 7)).max() < 1e-12 for band in range(1, BANDS))
    assert all(np.abs(block(band, band - 1) - block(8, 7)).max() < 1e-12 for band in range(1, BANDS))
    inner = whole[:, 7 * BAND : 8 * BAND]
    assert np.abs(inner[: 6 * BAND]).max() == 0 and np.abs(inner[9 * BAND :]).max() == 0
    assert all(np.abs(block(band, band) - block(7, 7)).max() < 1e-12 for band in range(1, BANDS - 1))
    expand = np.zeros((BAND, 2 * RANK))
    project = np.zeros((BAND, 2 * RANK))
    for side, part in enumerate((block(6, 7), block(8, 7))):
        left, sizes, right = np.linalg.svd(part)
        rank = int((sizes > 1e-12).sum())
        assert rank <= RANK
        expand[:, side * RANK : side * RANK + rank] = left[:, :rank] * sizes[:rank]
        project[:, side * RANK : side * RANK + rank] = right[:rank].T
    out = np.zeros((3, BAND, 2 * LANE))
    for variant, band in enumerate((0, 7, BANDS - 1)):
        own = block(band, band).T
        tail = np.concatenate([own[:, LANE:], project], axis=1)
        out[variant] = np.concatenate([own[:, :LANE], tail, tail], axis=1)
    return (
        out.astype(np.float32).astype(ml_dtypes.bfloat16),
        expand.astype(np.float32).astype(ml_dtypes.bfloat16),
    )


def pack_kernel(order_ref, spectra_ref, *refs):
    outs, (wide, low, high, packed) = refs[:HALVES], refs[HALVES:]
    first = lax.axis_index("wave") * SLOTS
    for pair in range(PAIRS):
        low[pl.ds(pair, 1), :] = jnp.full((1, LANE), order_ref[first + 2 * pair], jnp.int32)
        high[pl.ds(pair, 1), :] = jnp.full((1, LANE), order_ref[first + 2 * pair + 1], jnp.int32)
    waves_a, waves_b = low[...], high[...]
    lane = lax.broadcasted_iota(jnp.int32, (PAIRS, LANE), 1)
    for part in range(2):
        for block in range(5):
            wide[block] = spectra_ref[0, part, :, block * LANE : (block + 1) * LANE].astype(jnp.float32)
        for block in range(BLOCKS):
            taken = jnp.zeros((PAIRS, LANE), jnp.float32)
            if block <= 4:
                values = wide[4 - block, pl.ds(1, PAIRS, stride=2), :]
                taken = jnp.where(lane + (4 - block) * LANE >= waves_b, values, taken)
            if block >= 1:
                values = wide[block - 1, pl.ds(0, PAIRS, stride=2), :]
                values = jnp.where(lane + (block - 1) * LANE >= waves_a, values, jnp.zeros_like(values))
                taken = jnp.where(waves_a < block * LANE, values, taken)
            for half in range(HALVES):
                packed[half, pl.ds(part * PART_PAIRS, PART_PAIRS), block * LANE : (block + 1) * LANE] = taken[
                    half * PART_PAIRS : (half + 1) * PART_PAIRS
                ]
    for half in range(HALVES):
        outs[half][...] = packed[half].astype(jnp.bfloat16)


def fetch_kernel(order_ref, writer_ref, matrix_ref, legendre_ref, order_out, writer_out, matrix_out, held_out, sems):
    band = lax.axis_index("lat")
    variant = jnp.where(band == 0, 0, jnp.where(band == BANDS - 1, 2, 1))
    copies = [
        pltpu.make_async_copy(legendre_ref.at[pl.ds(0, PART_SLOTS)], held_out, sems.at[0]),
        pltpu.make_async_copy(order_ref, order_out, sems.at[1]),
        pltpu.make_async_copy(writer_ref, writer_out, sems.at[2]),
        pltpu.make_async_copy(matrix_ref.at[variant], matrix_out, sems.at[3]),
    ]
    for copy in copies:
        copy.start()
    for copy in copies:
        copy.wait()


def legendre_kernel(order_ref, writer_ref, *refs):
    parts = refs[: 4 * HALVES]
    near_ref, legendre_ref, matrix, out_ref = refs[4 * HALVES : 4 * HALVES + 4]
    spread, rows, results, rest, sems = refs[4 * HALVES + 4 :]
    held = (near_ref, rest)
    some = PART_SLOTS // 2
    copies = [
        pltpu.make_async_copy(
            legendre_ref.at[pl.ds(PART_SLOTS + index * some, some)], rest.at[pl.ds(index * some, some)], sems.at[index]
        )
        for index in range(2)
    ]
    for copy in copies:
        copy.start()
    first = lax.axis_index("wave") * SLOTS
    band = lax.axis_index("lat")
    band_x, band_z = band // 4, lax.rem(band, 4)
    steps = (0, 3, 1, 2)
    for half in range(HALVES):
        for outer in range(4):
            for inner in range(4):
                along_x, along_z = (outer, inner) if half == 0 else (inner, outer)
                field = 4 * lax.rem(band_x + steps[along_x], 4) + lax.rem(band_z + steps[along_z], 4)
                start = pl.multiple_of(field * 2 * PART_PAIRS, 8)
                for block in range(BLOCKS):
                    values = parts[4 * half + outer][inner, :, block * LANE : (block + 1) * LANE]
                    spread[block, pl.ds(start, 2 * PART_PAIRS), :] = values.astype(jnp.float32)

        def contract(group, carry, half=half):
            for member in range(GROUP):
                pair = group * GROUP + member
                wave = order_ref[first + half * PART_SLOTS + 2 * pair]
                lower, upper, values_of_n = [], [], []
                for block in range(BLOCKS):
                    values = spread[block, pl.ds(pair, 2 * FIELDS, stride=PART_PAIRS), :].astype(jnp.bfloat16)
                    from_a = wave < block * LANE
                    slot = 2 * pair + jnp.where(from_a, 0, 1)
                    source = pl.multiple_of(jnp.where(from_a, block - 1, 4 - block) * LANE, LANE)
                    values_of_n.append(held[half][slot, :, pl.ds(source, LANE)])
                    lower.append(jnp.where(from_a, values, jnp.zeros_like(values)))
                    upper.append(jnp.where(from_a, jnp.zeros_like(values), values))
                left = jnp.concatenate(
                    [jnp.concatenate(lower, axis=1), jnp.concatenate(upper, axis=1)], axis=0
                )
                sums = lax.dot_general(
                    left,
                    jnp.concatenate(values_of_n, axis=1),
                    (((1,), (1,)), ((), ())),
                    preferred_element_type=jnp.float32,
                )
                for which in range(2):
                    piece = sums[which * 2 * FIELDS : (which + 1) * 2 * FIELDS]
                    where = pl.ds(half * PART_SLOTS + 2 * pair + which, 2 * FIELDS, stride=SLOTS)
                    rows[0, where, :] = piece[:, :LANE]
                    rows[1, where, : BAND - LANE] = piece[:, LANE:]
            return carry

        if half:
            for copy in copies:
                copy.wait()
        lax.fori_loop(0, PART_PAIRS // GROUP, contract, 0)

    chunk = 2 * FIELDS * SLOTS // 8
    for index in range(8):
        picked = slice(index * chunk, (index + 1) * chunk)
        left = jnp.concatenate([rows[0, picked, :], rows[1, picked, : BAND - LANE]], axis=1).astype(jnp.bfloat16)
        sums = jnp.dot(left, matrix[...], preferred_element_type=jnp.float32)
        results[0, picked, :] = sums[:, :LANE]
        results[1, picked, :] = sums[:, LANE:]

    lane = lax.broadcasted_iota(jnp.int32, (SLOTS, LANE), 1)
    for owner in range(OWNERS):
        for member in range(2):
            field = writer_ref[2 * owner + member]
            tails = []
            for part in range(2):
                start = pl.multiple_of((2 * field + part) * SLOTS, 8)
                place = (2 * member + part) * LANE
                out_ref[owner, :, place : place + LANE] = results[0, pl.ds(start, SLOTS), :].astype(jnp.bfloat16)
                tails.append(results[1, pl.ds(start, SLOTS), :])
            place = (4 + member) * LANE
            out_ref[owner, :, place : place + LANE] = jnp.where(lane < LANE // 2, *tails).astype(jnp.bfloat16)


def edge_kernel(order_ref, waves_ref, chosen_ref, rest_ref, above_ref, below_ref):
    row = lax.broadcasted_iota(jnp.int32, (NWAVE, NWAVE), 0)
    chosen_ref[...] = jnp.where(row == order_ref[...], 1.0, 0.0).astype(jnp.bfloat16)
    ordered = jnp.dot(chosen_ref[...], waves_ref[...], preferred_element_type=jnp.float32)
    turned = ordered.T.astype(jnp.bfloat16)
    rest = BAND - LANE
    for part in range(4):
        start = part * (rest + 2 * RANK)
        rest_ref[part * rest : (part + 1) * rest] = turned[start : start + rest]
        above_ref[part * RANK : (part + 1) * RANK] = turned[start + rest : start + rest + RANK]
        below_ref[part * RANK : (part + 1) * RANK] = turned[start + rest + RANK : start + rest + 2 * RANK]


def order_kernel(chosen_ref, waves_ref, out_ref):
    ordered = jnp.dot(chosen_ref[...], waves_ref[...], preferred_element_type=jnp.float32)
    out_ref[...] = ordered.T.astype(jnp.bfloat16)


def synthesis_kernel(main_ref, rest_ref, above_ref, below_ref, expand_ref, middle_ref, table_ref, out_ref, *refs):
    left, table, tiles, even, flip, table_sems, out_sems = refs
    tables = [pltpu.make_async_copy(table_ref.at[step], table.at[step], table_sems.at[step]) for step in range(STEPS)]
    for copy in reversed(tables):
        copy.start()
    rest = BAND - LANE
    for field in range(2):
        for part in range(2):
            which = 2 * field + part
            edges = slice(which * RANK, (which + 1) * RANK)
            added = jnp.dot(
                expand_ref[...],
                jnp.concatenate([above_ref[edges], below_ref[edges]], axis=0),
                preferred_element_type=jnp.float32,
            )
            own = main_ref[which * LANE : (which + 1) * LANE].astype(jnp.float32)
            left[part, field * BAND : field * BAND + LANE] = (own + added[:LANE]).astype(jnp.bfloat16)
            own = rest_ref[which * rest : (which + 1) * rest].astype(jnp.float32)
            left[part, field * BAND + LANE : (field + 1) * BAND] = (own + added[LANE:]).astype(jnp.bfloat16)
    total = lax.broadcasted_iota(jnp.int32, (TILE, TILE), 0) + lax.broadcasted_iota(jnp.int32, (TILE, TILE), 1)
    flip[...] = jnp.where(total == TILE, 1.0, 0.0).astype(jnp.bfloat16)
    even[...] = jnp.dot(left[0], middle_ref[...], preferred_element_type=jnp.float32)

    def place(tile, where):
        return [
            pltpu.make_async_copy(
                tiles.at[tile, field],
                out_ref.at[field, :, pl.ds(where, TILE)],
                out_sems.at[tile, field],
            )
            for field in range(2)
        ]

    def step(count, carry):
        tile = STEPS - 1 - count
        pltpu.make_async_copy(table_ref.at[tile], table.at[tile], table_sems.at[tile]).wait()
        cosine = jnp.dot(left[0], table[tile, :NWAVE], preferred_element_type=jnp.float32)
        sine = jnp.dot(left[1], table[tile, NWAVE:], preferred_element_type=jnp.float32)
        front = (cosine + sine).astype(jnp.bfloat16)
        back = cosine - sine
        turned = jnp.dot(back.astype(jnp.bfloat16), flip[...], preferred_element_type=jnp.float32)
        lane = lax.broadcasted_iota(jnp.int32, (2 * BAND, LANE), 1)
        mirror = 2 * STEPS - 1 - tile
        head = jnp.where(lane == 0, even[...], turned[:, :LANE]).astype(jnp.bfloat16)
        tail = turned[:, LANE:].astype(jnp.bfloat16)
        even[...] = back[:, :LANE]
        for field in range(2):
            rows = slice(field * BAND, (field + 1) * BAND)
            tiles[tile, field] = front[rows]
            tiles[mirror, field, :, :LANE] = head[rows]
            tiles[mirror, field, :, LANE:] = tail[rows]
        for which in (tile, mirror):
            for copy in place(which, pl.multiple_of(which * TILE, TILE)):
                copy.start()
        return carry

    lax.fori_loop(0, STEPS, step, 0)
    for tile in range(2 * STEPS):
        for copy in place(tile, tile * TILE):
            copy.wait()


def along_z(step):
    return [(4 * x + z, 4 * x + (z + step) % 4) for x in range(4) for z in range(4)]


def along_x(step):
    return [(4 * x + z, 4 * ((x + step) % 4) + z) for x in range(4) for z in range(4)]


def neighbour(step):
    return [(band, band + step) for band in range(BANDS) if 0 <= band + step < BANDS]


SMEM = pl.BlockSpec(memory_space=pltpu.SMEM)
VMEM = pl.BlockSpec(memory_space=pltpu.VMEM)
ANY = pl.BlockSpec(memory_space=pl.ANY)
FETCH = pltpu.CompilerParams(vmem_limit_bytes=FETCH_BYTES)
MIDDLE = pltpu.CompilerParams(vmem_limit_bytes=MIDDLE_BYTES)
SMALL = pltpu.CompilerParams(vmem_limit_bytes=SMALL_BYTES)
LARGE = pltpu.CompilerParams(vmem_limit_bytes=LARGE_BYTES)


def bf16(*shape):
    return jax.ShapeDtypeStruct(shape, jnp.bfloat16)


def make_on_device(table, middle, matrices, expand):
    def on_device(spectra, legendre, wave_order, writer_order):
        halves = pl.pallas_call(
            pack_kernel,
            out_shape=[bf16(2 * PART_PAIRS, BLOCKS * LANE)] * HALVES,
            in_specs=[SMEM, VMEM],
            out_specs=[VMEM] * HALVES,
            scratch_shapes=[
                pltpu.VMEM((5, SLOTS, LANE), jnp.float32),
                pltpu.VMEM((PAIRS, LANE), jnp.int32),
                pltpu.VMEM((PAIRS, LANE), jnp.int32),
                pltpu.VMEM((HALVES, 2 * PART_PAIRS, BLOCKS * LANE), jnp.float32),
            ],
            name="pack",
        )(wave_order, spectra)

        axes = ((along_z, along_x), (along_x, along_z))
        firsts = []
        for half, values in enumerate(halves):
            sent = [lax.ppermute(values, "lat", axes[half][0](step)) for step in (1, 3, 2)]
            firsts.append(jnp.stack([values] + sent))
        firsts, legendre = lax.optimization_barrier((firsts, legendre))
        orders, writers, matrix, near = pl.pallas_call(
            fetch_kernel,
            out_shape=[
                jax.ShapeDtypeStruct((NWAVE,), jnp.int32),
                jax.ShapeDtypeStruct((FIELDS,), jnp.int32),
                bf16(BAND, 2 * LANE),
                bf16(PART_SLOTS, BAND, NWAVE),
            ],
            in_specs=[ANY] * 4,
            out_specs=[ANY] * 3 + [VMEM],
            scratch_shapes=[pltpu.SemaphoreType.DMA((4,))],
            compiler_params=FETCH,
            cost_estimate=pl.CostEstimate(flops=0, bytes_accessed=14_000_000, transcendentals=0),
            name="fetch",
        )(wave_order, writer_order, matrices, legendre)
        parts, opposites = [], []
        for half, values in enumerate(firsts):
            along = axes[half][1]
            before, after = [lax.ppermute(values, "lat", along(step)) for step in (1, 3)]
            parts.append([values, before, after])
            opposites.append(before)
        opposites, near = lax.optimization_barrier((opposites, near))
        for half in range(HALVES):
            parts[half].append(lax.ppermute(opposites[half], "lat", axes[half][1](1)))

        lifted = pl.pallas_call(
            legendre_kernel,
            out_shape=bf16(OWNERS, SLOTS, WIDTH),
            in_specs=[SMEM, SMEM] + [VMEM] * (4 * HALVES) + [VMEM, ANY, VMEM],
            out_specs=VMEM,
            scratch_shapes=[
                pltpu.VMEM((BLOCKS, 2 * FIELDS * PART_PAIRS, LANE), jnp.float32),
                pltpu.VMEM((2, 2 * FIELDS * SLOTS, LANE), jnp.float32),
                pltpu.VMEM((2, 2 * FIELDS * SLOTS, LANE), jnp.float32),
                pltpu.VMEM((PART_SLOTS, BAND, NWAVE), jnp.bfloat16),
                pltpu.SemaphoreType.DMA((2,)),
            ],
            compiler_params=MIDDLE,
            cost_estimate=pl.CostEstimate(flops=800_000_000, bytes_accessed=16_000_000, transcendentals=0),
            name="legendre",
        )(orders, writers, *parts[0], *parts[1], near, legendre, matrix)
        waves = lax.all_to_all(lifted, "wave", split_axis=0, concat_axis=0, tiled=True).reshape(NWAVE, WIDTH)

        main, rest = 4 * LANE, 4 * (BAND - LANE)
        chosen, tail, above, below = pl.pallas_call(
            edge_kernel,
            grid=(1,),
            out_shape=[bf16(NWAVE, NWAVE), bf16(rest, NWAVE), bf16(4 * RANK, NWAVE), bf16(4 * RANK, NWAVE)],
            in_specs=[pl.BlockSpec((1, NWAVE), lambda i: (0, 0))]
            + [pl.BlockSpec((NWAVE, WIDTH - main), lambda i: (0, main // (WIDTH - main)))],
            out_specs=[VMEM] * 4,
            compiler_params=SMALL,
            name="edges",
        )(wave_order.reshape(1, NWAVE), waves)
        above = lax.ppermute(above, "lat", neighbour(-1))
        below = lax.ppermute(below, "lat", neighbour(1))
        ordered = pl.pallas_call(
            order_kernel,
            grid=(1,),
            out_shape=bf16(main, NWAVE),
            in_specs=[pl.BlockSpec((NWAVE, NWAVE), lambda i: (0, 0))]
            + [pl.BlockSpec((NWAVE, main), lambda i: (0, 0))],
            out_specs=VMEM,
            compiler_params=SMALL,
            cost_estimate=pl.CostEstimate(flops=800_000_000, bytes_accessed=4_000_000, transcendentals=0),
            name="order",
        )(chosen, waves)
        return pl.pallas_call(
            synthesis_kernel,
            out_shape=bf16(2, BAND, NLON),
            in_specs=[VMEM] * 6 + [ANY],
            out_specs=ANY,
            scratch_shapes=[
                pltpu.VMEM((2, 2 * BAND, NWAVE), jnp.bfloat16),
                pltpu.VMEM((STEPS, 2 * NWAVE, TILE), jnp.bfloat16),
                pltpu.VMEM((2 * STEPS, 2, BAND, TILE), jnp.bfloat16),
                pltpu.VMEM((2 * BAND, LANE), jnp.float32),
                pltpu.VMEM((TILE, TILE), jnp.bfloat16),
                pltpu.SemaphoreType.DMA((STEPS,)),
                pltpu.SemaphoreType.DMA((2 * STEPS, 2)),
            ],
            compiler_params=LARGE,
            cost_estimate=pl.CostEstimate(flops=2_400_000_000, bytes_accessed=11_000_000, transcendentals=0),
            name="synthesis",
        )(ordered, tail, above, below, expand, middle, table)

    return on_device


def solution(mesh):
    constants = [*longitude_matrices(), *latitude_matrices()]
    return jax.shard_map(
        make_on_device(*[jnp.asarray(values) for values in constants]),
        mesh=mesh,
        in_specs=(P("lat", None, "wave", None), P("wave", "lat", None), P(), P()),
        out_specs=P("wave", "lat", None),
        check_vma=False,
    )
```

```python
import math

import jax
import jax.numpy as jnp
import ml_dtypes
import numpy as np
from jax import lax
from jax.experimental import pallas as pl
from jax.experimental.pallas import tpu as pltpu
from jax.sharding import PartitionSpec as P

NLAT = 2560
NLON = 5120
NWAVE = 640
WL = 5
BANDS = 16
OWNERS = 8
BAND = NLAT // BANDS
SLOTS = NWAVE // OWNERS
PAIRS = SLOTS // 2
FIELDS = 16
BLOCKS = 6
LANE = 128
HALVES = 2
PART_PAIRS = PAIRS // HALVES
PART_SLOTS = SLOTS // HALVES
RANK = 16
WIDTH = 4 * LANE + 4 * (BAND - LANE + 2 * RANK)
TILE = 256
STEPS = NLON // 2 // TILE
GROUP = 4
SMALL_BYTES = 16 * 2**20
MIDDLE_BYTES = 40 * 2**20
FETCH_BYTES = 44 * 2**20
LARGE_BYTES = 50 * 2**20

LIFT_ALPHA = -1.586134342059924
LIFT_BETA = -0.052980118572961
LIFT_GAMMA = 0.882911075530934
LIFT_DELTA = 0.443506852043971
LIFT_KAPPA = 1.149604398860241


def analyze(values, levels, mode_name):
    if levels == 0:
        return values
    widths = [(4, 4)] + [(0, 0)] * (values.ndim - 1)
    extended = np.pad(values, widths, mode=mode_name)
    even, odd = extended[0::2], extended[1::2]
    first_d = odd[:-1] + LIFT_ALPHA * (even[:-1] + even[1:])
    first_s = even[1:-1] + LIFT_BETA * (first_d[:-1] + first_d[1:])
    second_d = first_d[1:-1] + LIFT_GAMMA * (first_s[:-1] + first_s[1:])
    second_s = first_s[1:-1] + LIFT_DELTA * (second_d[:-1] + second_d[1:])
    result = np.empty_like(values)
    result[0::2] = analyze(second_s * LIFT_KAPPA, levels - 1, mode_name)
    result[1::2] = second_d[1:] / LIFT_KAPPA
    return result


def longitude_matrices():
    waves = np.arange(NWAVE)
    phase = waves[:, None] * np.arange(NLON)[None, :] % NLON
    angle = phase * (2.0 * math.pi / NLON)
    weight = np.where(waves == 0, 1.0, 2.0)[:, None] / math.sqrt(2.0 * NWAVE)
    table = np.concatenate([weight * np.cos(angle), -weight * np.sin(angle)], axis=0)
    table = table.astype(np.float32).astype(ml_dtypes.bfloat16).astype(np.float64)
    lifted = analyze(table.T, WL, "wrap").T
    half = lifted[:, : NLON // 2].reshape(2 * NWAVE, STEPS, TILE).swapaxes(0, 1)
    middle = np.zeros((NWAVE, LANE))
    middle[:, 0] = lifted[:NWAVE, NLON // 2]
    return [values.astype(np.float32).astype(ml_dtypes.bfloat16) for values in (half, middle)]


def latitude_matrices():
    whole = analyze(np.eye(NLAT), WL, "reflect")

    def block(row_band, column_band):
        return whole[row_band * BAND : (row_band + 1) * BAND, column_band * BAND : (column_band + 1) * BAND]

    assert all(np.abs(block(band - 1, band) - block(6, 7)).max() < 1e-12 for band in range(1, BANDS))
    assert all(np.abs(block(band, band - 1) - block(8, 7)).max() < 1e-12 for band in range(1, BANDS))
    inner = whole[:, 7 * BAND : 8 * BAND]
    assert np.abs(inner[: 6 * BAND]).max() == 0 and np.abs(inner[9 * BAND :]).max() == 0
    assert all(np.abs(block(band, band) - block(7, 7)).max() < 1e-12 for band in range(1, BANDS - 1))
    expand = np.zeros((BAND, 2 * RANK))
    project = np.zeros((BAND, 2 * RANK))
    for side, part in enumerate((block(6, 7), block(8, 7))):
        left, sizes, right = np.linalg.svd(part)
        rank = int((sizes > 1e-12).sum())
        assert rank <= RANK
        expand[:, side * RANK : side * RANK + rank] = left[:, :rank] * sizes[:rank]
        project[:, side * RANK : side * RANK + rank] = right[:rank].T
    out = np.zeros((3, BAND, 2 * LANE))
    for variant, band in enumerate((0, 7, BANDS - 1)):
        own = block(band, band).T
        tail = np.concatenate([own[:, LANE:], project], axis=1)
        out[variant] = np.concatenate([own[:, :LANE], tail, tail], axis=1)
    return (
        out.astype(np.float32).astype(ml_dtypes.bfloat16),
        expand.astype(np.float32).astype(ml_dtypes.bfloat16),
    )


def pack_kernel(order_ref, spectra_ref, *refs):
    outs, (wide, low, high, packed) = refs[:HALVES], refs[HALVES:]
    first = lax.axis_index("wave") * SLOTS
    for pair in range(PAIRS):
        low[pl.ds(pair, 1), :] = jnp.full((1, LANE), order_ref[first + 2 * pair], jnp.int32)
        high[pl.ds(pair, 1), :] = jnp.full((1, LANE), order_ref[first + 2 * pair + 1], jnp.int32)
    waves_a, waves_b = low[...], high[...]
    lane = lax.broadcasted_iota(jnp.int32, (PAIRS, LANE), 1)
    for part in range(2):
        for block in range(5):
            wide[block] = spectra_ref[0, part, :, block * LANE : (block + 1) * LANE].astype(jnp.float32)
        for block in range(BLOCKS):
            taken = jnp.zeros((PAIRS, LANE), jnp.float32)
            if block <= 4:
                values = wide[4 - block, pl.ds(1, PAIRS, stride=2), :]
                taken = jnp.where(lane + (4 - block) * LANE >= waves_b, values, taken)
            if block >= 1:
                values = wide[block - 1, pl.ds(0, PAIRS, stride=2), :]
                values = jnp.where(lane + (block - 1) * LANE >= waves_a, values, jnp.zeros_like(values))
                taken = jnp.where(waves_a < block * LANE, values, taken)
            for half in range(HALVES):
                packed[half, pl.ds(part * PART_PAIRS, PART_PAIRS), block * LANE : (block + 1) * LANE] = taken[
                    half * PART_PAIRS : (half + 1) * PART_PAIRS
                ]
    for half in range(HALVES):
        outs[half][...] = packed[half].astype(jnp.bfloat16)


def fetch_kernel(order_ref, writer_ref, matrix_ref, legendre_ref, order_out, writer_out, matrix_out, held_out, sems):
    band = lax.axis_index("lat")
    variant = jnp.where(band == 0, 0, jnp.where(band == BANDS - 1, 2, 1))
    copies = [
        pltpu.make_async_copy(legendre_ref.at[pl.ds(0, PART_SLOTS)], held_out, sems.at[0]),
        pltpu.make_async_copy(order_ref, order_out, sems.at[1]),
        pltpu.make_async_copy(writer_ref, writer_out, sems.at[2]),
        pltpu.make_async_copy(matrix_ref.at[variant], matrix_out, sems.at[3]),
    ]
    for copy in copies:
        copy.start()
    for copy in copies:
        copy.wait()


def legendre_kernel(order_ref, writer_ref, *refs):
    parts = refs[: 4 * HALVES]
    near_ref, legendre_ref, matrix, out_ref, tail_ref = refs[4 * HALVES : 4 * HALVES + 5]
    spread, rows, results, rest, sems = refs[4 * HALVES + 5 :]
    held = (near_ref, rest)
    some = PART_SLOTS // 2
    copies = [
        pltpu.make_async_copy(
            legendre_ref.at[pl.ds(PART_SLOTS + index * some, some)], rest.at[pl.ds(index * some, some)], sems.at[index]
        )
        for index in range(2)
    ]
    for copy in copies:
        copy.start()
    first = lax.axis_index("wave") * SLOTS
    band = lax.axis_index("lat")
    band_x, band_z = band // 4, lax.rem(band, 4)
    steps = (0, 3, 1, 2)
    for half in range(HALVES):
        for outer in range(4):
            for inner in range(4):
                along_x, along_z = (outer, inner) if half == 0 else (inner, outer)
                field = 4 * lax.rem(band_x + steps[along_x], 4) + lax.rem(band_z + steps[along_z], 4)
                start = pl.multiple_of(field * 2 * PART_PAIRS, 8)
                for block in range(BLOCKS):
                    values = parts[4 * half + outer][inner, :, block * LANE : (block + 1) * LANE]
                    spread[block, pl.ds(start, 2 * PART_PAIRS), :] = values.astype(jnp.float32)

        def contract(group, carry, half=half):
            for member in range(GROUP):
                pair = group * GROUP + member
                wave = order_ref[first + half * PART_SLOTS + 2 * pair]
                lower, upper, values_of_n = [], [], []
                for block in range(BLOCKS):
                    values = spread[block, pl.ds(pair, 2 * FIELDS, stride=PART_PAIRS), :].astype(jnp.bfloat16)
                    from_a = wave < block * LANE
                    slot = 2 * pair + jnp.where(from_a, 0, 1)
                    source = pl.multiple_of(jnp.where(from_a, block - 1, 4 - block) * LANE, LANE)
                    values_of_n.append(held[half][slot, :, pl.ds(source, LANE)])
                    lower.append(jnp.where(from_a, values, jnp.zeros_like(values)))
                    upper.append(jnp.where(from_a, jnp.zeros_like(values), values))
                left = jnp.concatenate(
                    [jnp.concatenate(lower, axis=1), jnp.concatenate(upper, axis=1)], axis=0
                )
                sums = lax.dot_general(
                    left,
                    jnp.concatenate(values_of_n, axis=1),
                    (((1,), (1,)), ((), ())),
                    preferred_element_type=jnp.float32,
                )
                for which in range(2):
                    piece = sums[which * 2 * FIELDS : (which + 1) * 2 * FIELDS]
                    where = pl.ds(half * PART_SLOTS + 2 * pair + which, 2 * FIELDS, stride=SLOTS)
                    rows[0, where, :] = piece[:, :LANE]
                    rows[1, where, : BAND - LANE] = piece[:, LANE:]
            return carry

        if half:
            for copy in copies:
                copy.wait()
        lax.fori_loop(0, PART_PAIRS // GROUP, contract, 0)

    chunk = 2 * FIELDS * SLOTS // 8
    for index in range(8):
        picked = slice(index * chunk, (index + 1) * chunk)
        left = jnp.concatenate([rows[0, picked, :], rows[1, picked, : BAND - LANE]], axis=1).astype(jnp.bfloat16)
        sums = jnp.dot(left, matrix[...], preferred_element_type=jnp.float32)
        results[0, picked, :] = sums[:, :LANE]
        results[1, picked, :] = sums[:, LANE:]

    lane = lax.broadcasted_iota(jnp.int32, (SLOTS, LANE), 1)
    for owner in range(OWNERS):
        for member in range(2):
            field = writer_ref[2 * owner + member]
            tails = []
            for part in range(2):
                start = pl.multiple_of((2 * field + part) * SLOTS, 8)
                place = (2 * member + part) * LANE
                out_ref[owner, :, place : place + LANE] = results[0, pl.ds(start, SLOTS), :].astype(jnp.bfloat16)
                tails.append(results[1, pl.ds(start, SLOTS), :])
            place = member * LANE
            tail_ref[owner, :, place : place + LANE] = jnp.where(lane < LANE // 2, *tails).astype(jnp.bfloat16)


def edge_kernel(order_ref, waves_ref, chosen_ref, rest_ref, above_ref, below_ref):
    row = lax.broadcasted_iota(jnp.int32, (NWAVE, NWAVE), 0)
    chosen_ref[...] = jnp.where(row == order_ref[...], 1.0, 0.0).astype(jnp.bfloat16)
    ordered = jnp.dot(chosen_ref[...], waves_ref[...], preferred_element_type=jnp.float32)
    turned = ordered.T.astype(jnp.bfloat16)
    rest = BAND - LANE
    for part in range(4):
        start = part * (rest + 2 * RANK)
        rest_ref[part * rest : (part + 1) * rest] = turned[start : start + rest]
        above_ref[part * RANK : (part + 1) * RANK] = turned[start + rest : start + rest + RANK]
        below_ref[part * RANK : (part + 1) * RANK] = turned[start + rest + RANK : start + rest + 2 * RANK]


def order_kernel(chosen_ref, waves_ref, out_ref):
    ordered = jnp.dot(chosen_ref[...], waves_ref[...], preferred_element_type=jnp.float32)
    out_ref[...] = ordered.T.astype(jnp.bfloat16)


def synthesis_kernel(main_ref, rest_ref, above_ref, below_ref, expand_ref, middle_ref, table_ref, out_ref, *refs):
    left, table, tiles, even, flip, table_sems, out_sems = refs
    tables = [pltpu.make_async_copy(table_ref.at[step], table.at[step], table_sems.at[step]) for step in range(STEPS)]
    for copy in reversed(tables):
        copy.start()
    rest = BAND - LANE
    for field in range(2):
        for part in range(2):
            which = 2 * field + part
            edges = slice(which * RANK, (which + 1) * RANK)
            added = jnp.dot(
                expand_ref[...],
                jnp.concatenate([above_ref[edges], below_ref[edges]], axis=0),
                preferred_element_type=jnp.float32,
            )
            own = main_ref[which * LANE : (which + 1) * LANE].astype(jnp.float32)
            left[part, field * BAND : field * BAND + LANE] = (own + added[:LANE]).astype(jnp.bfloat16)
            own = rest_ref[which * rest : (which + 1) * rest].astype(jnp.float32)
            left[part, field * BAND + LANE : (field + 1) * BAND] = (own + added[LANE:]).astype(jnp.bfloat16)
    total = lax.broadcasted_iota(jnp.int32, (TILE, TILE), 0) + lax.broadcasted_iota(jnp.int32, (TILE, TILE), 1)
    flip[...] = jnp.where(total == TILE, 1.0, 0.0).astype(jnp.bfloat16)
    even[...] = jnp.dot(left[0], middle_ref[...], preferred_element_type=jnp.float32)

    def place(tile, where):
        return [
            pltpu.make_async_copy(
                tiles.at[tile, field],
                out_ref.at[field, :, pl.ds(where, TILE)],
                out_sems.at[tile, field],
            )
            for field in range(2)
        ]

    def step(count, carry):
        tile = STEPS - 1 - count
        pltpu.make_async_copy(table_ref.at[tile], table.at[tile], table_sems.at[tile]).wait()
        cosine = jnp.dot(left[0], table[tile, :NWAVE], preferred_element_type=jnp.float32)
        sine = jnp.dot(left[1], table[tile, NWAVE:], preferred_element_type=jnp.float32)
        front = (cosine + sine).astype(jnp.bfloat16)
        back = cosine - sine
        turned = jnp.dot(back.astype(jnp.bfloat16), flip[...], preferred_element_type=jnp.float32)
        lane = lax.broadcasted_iota(jnp.int32, (2 * BAND, LANE), 1)
        mirror = 2 * STEPS - 1 - tile
        head = jnp.where(lane == 0, even[...], turned[:, :LANE]).astype(jnp.bfloat16)
        tail = turned[:, LANE:].astype(jnp.bfloat16)
        even[...] = back[:, :LANE]
        for field in range(2):
            rows = slice(field * BAND, (field + 1) * BAND)
            tiles[tile, field] = front[rows]
            tiles[mirror, field, :, :LANE] = head[rows]
            tiles[mirror, field, :, LANE:] = tail[rows]
        for which in (tile, mirror):
            for copy in place(which, pl.multiple_of(which * TILE, TILE)):
                copy.start()
        return carry

    lax.fori_loop(0, STEPS, step, 0)
    for tile in range(2 * STEPS):
        for copy in place(tile, tile * TILE):
            copy.wait()


def along_z(step):
    return [(4 * x + z, 4 * x + (z + step) % 4) for x in range(4) for z in range(4)]


def along_x(step):
    return [(4 * x + z, 4 * ((x + step) % 4) + z) for x in range(4) for z in range(4)]


def neighbour(step):
    return [(band, band + step) for band in range(BANDS) if 0 <= band + step < BANDS]


SMEM = pl.BlockSpec(memory_space=pltpu.SMEM)
VMEM = pl.BlockSpec(memory_space=pltpu.VMEM)
ANY = pl.BlockSpec(memory_space=pl.ANY)
FETCH = pltpu.CompilerParams(vmem_limit_bytes=FETCH_BYTES)
MIDDLE = pltpu.CompilerParams(vmem_limit_bytes=MIDDLE_BYTES)
SMALL = pltpu.CompilerParams(vmem_limit_bytes=SMALL_BYTES)
LARGE = pltpu.CompilerParams(vmem_limit_bytes=LARGE_BYTES)


def bf16(*shape):
    return jax.ShapeDtypeStruct(shape, jnp.bfloat16)


def make_on_device(table, middle, matrices, expand):
    def on_device(spectra, legendre, wave_order, writer_order):
        halves = pl.pallas_call(
            pack_kernel,
            out_shape=[bf16(2 * PART_PAIRS, BLOCKS * LANE)] * HALVES,
            in_specs=[SMEM, VMEM],
            out_specs=[VMEM] * HALVES,
            scratch_shapes=[
                pltpu.VMEM((5, SLOTS, LANE), jnp.float32),
                pltpu.VMEM((PAIRS, LANE), jnp.int32),
                pltpu.VMEM((PAIRS, LANE), jnp.int32),
                pltpu.VMEM((HALVES, 2 * PART_PAIRS, BLOCKS * LANE), jnp.float32),
            ],
            name="pack",
        )(wave_order, spectra)

        axes = ((along_z, along_x), (along_x, along_z))
        firsts = []
        for half, values in enumerate(halves):
            sent = [lax.ppermute(values, "lat", axes[half][0](step)) for step in (1, 3, 2)]
            firsts.append(jnp.stack([values] + sent))
        firsts, legendre = lax.optimization_barrier((firsts, legendre))
        orders, writers, matrix, near = pl.pallas_call(
            fetch_kernel,
            out_shape=[
                jax.ShapeDtypeStruct((NWAVE,), jnp.int32),
                jax.ShapeDtypeStruct((FIELDS,), jnp.int32),
                bf16(BAND, 2 * LANE),
                bf16(PART_SLOTS, BAND, NWAVE),
            ],
            in_specs=[ANY] * 4,
            out_specs=[ANY] * 3 + [VMEM],
            scratch_shapes=[pltpu.SemaphoreType.DMA((4,))],
            compiler_params=FETCH,
            cost_estimate=pl.CostEstimate(flops=0, bytes_accessed=14_000_000, transcendentals=0),
            name="fetch",
        )(wave_order, writer_order, matrices, legendre)
        parts, opposites = [], []
        for half, values in enumerate(firsts):
            along = axes[half][1]
            before, after = [lax.ppermute(values, "lat", along(step)) for step in (1, 3)]
            parts.append([values, before, after])
            opposites.append(before)
        opposites, near = lax.optimization_barrier((opposites, near))
        for half in range(HALVES):
            parts[half].append(lax.ppermute(opposites[half], "lat", axes[half][1](1)))

        lifted, tails = pl.pallas_call(
            legendre_kernel,
            out_shape=[bf16(OWNERS, SLOTS, 4 * LANE), bf16(OWNERS, SLOTS, WIDTH - 4 * LANE)],
            in_specs=[SMEM, SMEM] + [VMEM] * (4 * HALVES) + [VMEM, ANY, VMEM],
            out_specs=[VMEM] * 2,
            scratch_shapes=[
                pltpu.VMEM((BLOCKS, 2 * FIELDS * PART_PAIRS, LANE), jnp.float32),
                pltpu.VMEM((2, 2 * FIELDS * SLOTS, LANE), jnp.float32),
                pltpu.VMEM((2, 2 * FIELDS * SLOTS, LANE), jnp.float32),
                pltpu.VMEM((PART_SLOTS, BAND, NWAVE), jnp.bfloat16),
                pltpu.SemaphoreType.DMA((2,)),
            ],
            compiler_params=MIDDLE,
            cost_estimate=pl.CostEstimate(flops=800_000_000, bytes_accessed=16_000_000, transcendentals=0),
            name="legendre",
        )(orders, writers, *parts[0], *parts[1], near, legendre, matrix)
        edges = lax.all_to_all(tails, "wave", split_axis=0, concat_axis=0, tiled=True)
        waves = lax.all_to_all(lifted, "wave", split_axis=0, concat_axis=0, tiled=True)

        main, rest = 4 * LANE, 4 * (BAND - LANE)
        chosen, tail, above, below = pl.pallas_call(
            edge_kernel,
            grid=(1,),
            out_shape=[bf16(NWAVE, NWAVE), bf16(rest, NWAVE), bf16(4 * RANK, NWAVE), bf16(4 * RANK, NWAVE)],
            in_specs=[pl.BlockSpec((1, NWAVE), lambda i: (0, 0))]
            + [pl.BlockSpec((NWAVE, WIDTH - main), lambda i: (0, 0))],
            out_specs=[VMEM] * 4,
            compiler_params=SMALL,
            name="edges",
        )(wave_order.reshape(1, NWAVE), edges.reshape(NWAVE, WIDTH - main))
        above = lax.ppermute(above, "lat", neighbour(-1))
        below = lax.ppermute(below, "lat", neighbour(1))
        ordered = pl.pallas_call(
            order_kernel,
            grid=(1,),
            out_shape=bf16(main, NWAVE),
            in_specs=[pl.BlockSpec((NWAVE, NWAVE), lambda i: (0, 0))]
            + [pl.BlockSpec((NWAVE, main), lambda i: (0, 0))],
            out_specs=VMEM,
            compiler_params=SMALL,
            cost_estimate=pl.CostEstimate(flops=800_000_000, bytes_accessed=4_000_000, transcendentals=0),
            name="order",
        )(chosen, waves.reshape(NWAVE, main))
        return pl.pallas_call(
            synthesis_kernel,
            out_shape=bf16(2, BAND, NLON),
            in_specs=[VMEM] * 6 + [ANY],
            out_specs=ANY,
            scratch_shapes=[
                pltpu.VMEM((2, 2 * BAND, NWAVE), jnp.bfloat16),
                pltpu.VMEM((STEPS, 2 * NWAVE, TILE), jnp.bfloat16),
                pltpu.VMEM((2 * STEPS, 2, BAND, TILE), jnp.bfloat16),
                pltpu.VMEM((2 * BAND, LANE), jnp.float32),
                pltpu.VMEM((TILE, TILE), jnp.bfloat16),
                pltpu.SemaphoreType.DMA((STEPS,)),
                pltpu.SemaphoreType.DMA((2 * STEPS, 2)),
            ],
            compiler_params=LARGE,
            cost_estimate=pl.CostEstimate(flops=2_400_000_000, bytes_accessed=11_000_000, transcendentals=0),
            name="synthesis",
        )(ordered, tail, above, below, expand, middle, table)

    return on_device


def solution(mesh):
    constants = [*longitude_matrices(), *latitude_matrices()]
    return jax.shard_map(
        make_on_device(*[jnp.asarray(values) for values in constants]),
        mesh=mesh,
        in_specs=(P("lat", None, "wave", None), P("wave", "lat", None), P(), P()),
        out_specs=P("wave", "lat", None),
        check_vma=False,
    )
```

```python
import math

import jax
import jax.numpy as jnp
import ml_dtypes
import numpy as np
from jax import lax
from jax.experimental import pallas as pl
from jax.experimental.pallas import tpu as pltpu
from jax.sharding import PartitionSpec as P

NLAT = 2560
NLON = 5120
NWAVE = 640
WL = 5
BANDS = 16
OWNERS = 8
BAND = NLAT // BANDS
SLOTS = NWAVE // OWNERS
PAIRS = SLOTS // 2
FIELDS = 16
BLOCKS = 6
LANE = 128
HALVES = 2
PART_PAIRS = PAIRS // HALVES
PART_SLOTS = SLOTS // HALVES
RANK = 16
WIDTH = 4 * LANE + 4 * (BAND - LANE + 2 * RANK)
TILE = 256
STEPS = NLON // 4 // TILE
GROUP = 4
SMALL_BYTES = 16 * 2**20
MIDDLE_BYTES = 40 * 2**20
FETCH_BYTES = 44 * 2**20
LARGE_BYTES = 50 * 2**20

LIFT_ALPHA = -1.586134342059924
LIFT_BETA = -0.052980118572961
LIFT_GAMMA = 0.882911075530934
LIFT_DELTA = 0.443506852043971
LIFT_KAPPA = 1.149604398860241


def analyze(values, levels, mode_name):
    if levels == 0:
        return values
    widths = [(4, 4)] + [(0, 0)] * (values.ndim - 1)
    extended = np.pad(values, widths, mode=mode_name)
    even, odd = extended[0::2], extended[1::2]
    first_d = odd[:-1] + LIFT_ALPHA * (even[:-1] + even[1:])
    first_s = even[1:-1] + LIFT_BETA * (first_d[:-1] + first_d[1:])
    second_d = first_d[1:-1] + LIFT_GAMMA * (first_s[:-1] + first_s[1:])
    second_s = first_s[1:-1] + LIFT_DELTA * (second_d[:-1] + second_d[1:])
    result = np.empty_like(values)
    result[0::2] = analyze(second_s * LIFT_KAPPA, levels - 1, mode_name)
    result[1::2] = second_d[1:] / LIFT_KAPPA
    return result


def longitude_matrices():
    waves = np.concatenate([np.arange(0, NWAVE, 2), np.arange(1, NWAVE, 2)])
    phase = waves[:, None] * np.arange(NLON)[None, :] % NLON
    angle = phase * (2.0 * math.pi / NLON)
    weight = np.where(waves == 0, 1.0, 2.0)[:, None] / math.sqrt(2.0 * NWAVE)
    table = np.concatenate([weight * np.cos(angle), -weight * np.sin(angle)], axis=0)
    table = table.astype(np.float32).astype(ml_dtypes.bfloat16).astype(np.float64)
    cosine, sine = analyze(table.T, WL, "wrap").T.reshape(2, NWAVE, NLON)
    half = NWAVE // 2
    both = np.stack([np.concatenate([cosine[:half], sine[half:]]), np.concatenate([sine[:half], cosine[half:]])])
    quarter = both[:, :, : NLON // 4].reshape(2, NWAVE, STEPS, TILE).transpose(2, 0, 1, 3)
    middle = np.zeros((2, NWAVE, LANE))
    middle[:, :, 0] = both[:, :, NLON // 4]
    return [values.astype(np.float32).astype(ml_dtypes.bfloat16) for values in (quarter, middle)]


def latitude_matrices():
    whole = analyze(np.eye(NLAT), WL, "reflect")

    def block(row_band, column_band):
        return whole[row_band * BAND : (row_band + 1) * BAND, column_band * BAND : (column_band + 1) * BAND]

    assert all(np.abs(block(band - 1, band) - block(6, 7)).max() < 1e-12 for band in range(1, BANDS))
    assert all(np.abs(block(band, band - 1) - block(8, 7)).max() < 1e-12 for band in range(1, BANDS))
    inner = whole[:, 7 * BAND : 8 * BAND]
    assert np.abs(inner[: 6 * BAND]).max() == 0 and np.abs(inner[9 * BAND :]).max() == 0
    assert all(np.abs(block(band, band) - block(7, 7)).max() < 1e-12 for band in range(1, BANDS - 1))
    expand = np.zeros((BAND, 2 * RANK))
    project = np.zeros((BAND, 2 * RANK))
    for side, part in enumerate((block(6, 7), block(8, 7))):
        left, sizes, right = np.linalg.svd(part)
        rank = int((sizes > 1e-12).sum())
        assert rank <= RANK
        expand[:, side * RANK : side * RANK + rank] = left[:, :rank] * sizes[:rank]
        project[:, side * RANK : side * RANK + rank] = right[:rank].T
    out = np.zeros((3, BAND, 2 * LANE))
    for variant, band in enumerate((0, 7, BANDS - 1)):
        own = block(band, band).T
        tail = np.concatenate([own[:, LANE:], project], axis=1)
        out[variant] = np.concatenate([own[:, :LANE], tail, tail], axis=1)
    return (
        out.astype(np.float32).astype(ml_dtypes.bfloat16),
        expand.astype(np.float32).astype(ml_dtypes.bfloat16),
    )


def pack_kernel(order_ref, spectra_ref, *refs):
    out_ref, wide, low, high = refs
    first = lax.axis_index("wave") * SLOTS
    for pair in range(PAIRS):
        low[pl.ds(pair, 1), :] = jnp.full((1, LANE), order_ref[first + 2 * pair], jnp.int32)
        high[pl.ds(pair, 1), :] = jnp.full((1, LANE), order_ref[first + 2 * pair + 1], jnp.int32)
    waves_a, waves_b = low[...], high[...]
    lane = lax.broadcasted_iota(jnp.int32, (PAIRS, LANE), 1)
    rows = []
    for part in range(2):
        packed = []
        for block in range(5):
            wide[block] = spectra_ref[0, part, :, block * LANE : (block + 1) * LANE].astype(jnp.float32)
        for block in range(BLOCKS):
            taken = jnp.zeros((PAIRS, LANE), jnp.float32)
            if block <= 4:
                values = wide[4 - block, pl.ds(1, PAIRS, stride=2), :]
                taken = jnp.where(lane + (4 - block) * LANE >= waves_b, values, taken)
            if block >= 1:
                values = wide[block - 1, pl.ds(0, PAIRS, stride=2), :]
                values = jnp.where(lane + (block - 1) * LANE >= waves_a, values, jnp.zeros_like(values))
                taken = jnp.where(waves_a < block * LANE, values, taken)
            packed.append(taken)
        rows.append(jnp.concatenate(packed, axis=1))
    out_ref[...] = jnp.concatenate(rows, axis=0).astype(jnp.bfloat16)


def fetch_kernel(order_ref, writer_ref, matrix_ref, legendre_ref, order_out, writer_out, matrix_out, held_out, sems):
    band = lax.axis_index("lat")
    variant = jnp.where(band == 0, 0, jnp.where(band == BANDS - 1, 2, 1))
    copies = [
        pltpu.make_async_copy(legendre_ref.at[pl.ds(0, PART_SLOTS)], held_out, sems.at[0]),
        pltpu.make_async_copy(order_ref, order_out, sems.at[1]),
        pltpu.make_async_copy(writer_ref, writer_out, sems.at[2]),
        pltpu.make_async_copy(matrix_ref.at[variant], matrix_out, sems.at[3]),
    ]
    for copy in copies:
        copy.start()
    for copy in copies:
        copy.wait()


def legendre_kernel(order_ref, writer_ref, *refs):
    parts = refs[:8]
    near_ref, legendre_ref, matrix, out_ref, tail_ref = refs[8:13]
    spread, rows, results, rest, sems = refs[13:]
    held = (near_ref, rest)
    some = PART_SLOTS // 2
    copies = [
        pltpu.make_async_copy(
            legendre_ref.at[pl.ds(PART_SLOTS + index * some, some)], rest.at[pl.ds(index * some, some)], sems.at[index]
        )
        for index in range(2)
    ]
    for copy in copies:
        copy.start()
    first = lax.axis_index("wave") * SLOTS
    band = lax.axis_index("lat")
    band_x, band_z = band // 4, lax.rem(band, 4)
    steps = (0, 3, 1, 2)
    for outer in range(4):
        for inner in range(4):
            field = 4 * lax.rem(band_x + steps[outer], 4) + lax.rem(band_z + steps[inner], 4)
            start = pl.multiple_of(field * 2 * PAIRS, 16)
            for block in range(BLOCKS):
                values = parts[2 * outer + inner // 2][inner % 2, :, block * LANE : (block + 1) * LANE]
                spread[block, pl.ds(start, 2 * PAIRS), :] = values.astype(jnp.float32)

    for half in range(HALVES):

        def contract(group, carry, half=half):
            for member in range(GROUP):
                pair = group * GROUP + member
                wave = order_ref[first + half * PART_SLOTS + 2 * pair]
                lower, upper, values_of_n = [], [], []
                for block in range(BLOCKS):
                    values = spread[block, pl.ds(half * PART_PAIRS + pair, 2 * FIELDS, stride=PAIRS), :].astype(jnp.bfloat16)
                    from_a = wave < block * LANE
                    slot = 2 * pair + jnp.where(from_a, 0, 1)
                    source = pl.multiple_of(jnp.where(from_a, block - 1, 4 - block) * LANE, LANE)
                    values_of_n.append(held[half][slot, :, pl.ds(source, LANE)])
                    lower.append(jnp.where(from_a, values, jnp.zeros_like(values)))
                    upper.append(jnp.where(from_a, jnp.zeros_like(values), values))
                left = jnp.concatenate(
                    [jnp.concatenate(lower, axis=1), jnp.concatenate(upper, axis=1)], axis=0
                )
                sums = lax.dot_general(
                    left,
                    jnp.concatenate(values_of_n, axis=1),
                    (((1,), (1,)), ((), ())),
                    preferred_element_type=jnp.float32,
                )
                for which in range(2):
                    piece = sums[which * 2 * FIELDS : (which + 1) * 2 * FIELDS]
                    where = pl.ds(half * PART_SLOTS + 2 * pair + which, 2 * FIELDS, stride=SLOTS)
                    rows[0, where, :] = piece[:, :LANE]
                    rows[1, where, : BAND - LANE] = piece[:, LANE:]
            return carry

        if half:
            for copy in copies:
                copy.wait()
        lax.fori_loop(0, PART_PAIRS // GROUP, contract, 0)

    chunk = 2 * FIELDS * SLOTS // 8
    for index in range(8):
        picked = slice(index * chunk, (index + 1) * chunk)
        left = jnp.concatenate([rows[0, picked, :], rows[1, picked, : BAND - LANE]], axis=1).astype(jnp.bfloat16)
        sums = jnp.dot(left, matrix[...], preferred_element_type=jnp.float32)
        results[0, picked, :] = sums[:, :LANE]
        results[1, picked, :] = sums[:, LANE:]

    lane = lax.broadcasted_iota(jnp.int32, (SLOTS, LANE), 1)
    for owner in range(OWNERS):
        for member in range(2):
            field = writer_ref[2 * owner + member]
            tails = []
            for part in range(2):
                start = pl.multiple_of((2 * field + part) * SLOTS, 8)
                place = (2 * member + part) * LANE
                out_ref[owner, :, place : place + LANE] = results[0, pl.ds(start, SLOTS), :].astype(jnp.bfloat16)
                tails.append(results[1, pl.ds(start, SLOTS), :])
            place = member * LANE
            tail_ref[owner, :, place : place + LANE] = jnp.where(lane < LANE // 2, *tails).astype(jnp.bfloat16)


def edge_kernel(order_ref, waves_ref, chosen_ref, rest_ref, above_ref, below_ref):
    row = lax.broadcasted_iota(jnp.int32, (NWAVE, NWAVE), 0)
    wave = jnp.where(row < NWAVE // 2, 2 * row, 2 * row + 1 - NWAVE)
    chosen_ref[...] = jnp.where(wave == order_ref[...], 1.0, 0.0).astype(jnp.bfloat16)
    ordered = jnp.dot(chosen_ref[...], waves_ref[...], preferred_element_type=jnp.float32)
    turned = ordered.T.astype(jnp.bfloat16)
    rest = BAND - LANE
    for part in range(4):
        start = part * (rest + 2 * RANK)
        rest_ref[part * rest : (part + 1) * rest] = turned[start : start + rest]
        above_ref[part * RANK : (part + 1) * RANK] = turned[start + rest : start + rest + RANK]
        below_ref[part * RANK : (part + 1) * RANK] = turned[start + rest + RANK : start + rest + 2 * RANK]


def order_kernel(chosen_ref, waves_ref, out_ref):
    ordered = jnp.dot(chosen_ref[...], waves_ref[...], preferred_element_type=jnp.float32)
    out_ref[...] = ordered.T.astype(jnp.bfloat16)


def synthesis_kernel(main_ref, rest_ref, above_ref, below_ref, expand_ref, middle_ref, table_ref, out_ref, *refs):
    left, table, tiles, ends, flip, table_sems, out_sems = refs
    tables = [pltpu.make_async_copy(table_ref.at[step], table.at[step], table_sems.at[step]) for step in range(STEPS)]
    for copy in reversed(tables):
        copy.start()
    rest = BAND - LANE
    rows = 2 * BAND
    low = lax.broadcasted_iota(jnp.int32, (BAND, NWAVE), 1) < NWAVE // 2
    for field in range(2):
        summed = []
        for part in range(2):
            which = 2 * field + part
            edges = slice(which * RANK, (which + 1) * RANK)
            added = jnp.dot(
                expand_ref[...],
                jnp.concatenate([above_ref[edges], below_ref[edges]], axis=0),
                preferred_element_type=jnp.float32,
            )
            own = [main_ref[which * LANE : (which + 1) * LANE], rest_ref[which * rest : (which + 1) * rest]]
            summed.append(jnp.concatenate(own, axis=0).astype(jnp.float32) + added)
        cosine, sine = summed
        for turned, value in enumerate((sine, -sine)):
            picked = slice(turned * rows + field * BAND, turned * rows + (field + 1) * BAND)
            left[0, picked] = jnp.where(low, cosine, value).astype(jnp.bfloat16)
            left[1, picked] = jnp.where(low, value, cosine).astype(jnp.bfloat16)
    total = lax.broadcasted_iota(jnp.int32, (TILE, TILE), 0) + lax.broadcasted_iota(jnp.int32, (TILE, TILE), 1)
    flip[...] = jnp.where(total == TILE, 1.0, 0.0).astype(jnp.bfloat16)

    def products(first, second):
        a = jnp.dot(left[0], first, preferred_element_type=jnp.float32)
        b = jnp.dot(left[1], second, preferred_element_type=jnp.float32)
        return a[:rows] + b[:rows], a[:rows] - b[:rows], a[rows:] - b[rows:], a[rows:] + b[rows:]

    _, ends[0], _, ends[1] = products(middle_ref[0], middle_ref[1])

    def place(tile, where):
        return [
            pltpu.make_async_copy(
                tiles.at[tile, field],
                out_ref.at[field, :, pl.ds(where, TILE)],
                out_sems.at[tile, field],
            )
            for field in range(2)
        ]

    lane = lax.broadcasted_iota(jnp.int32, (rows, LANE), 1)
    for tile in reversed(range(STEPS)):
        tables[tile].wait()
        east, back, south, west = products(table[tile, 0], table[tile, 1])
        written = [(tile, east), (2 * STEPS + tile, south)]
        for which, (values, target) in enumerate(((back, 2 * STEPS - 1 - tile), (west, 4 * STEPS - 1 - tile))):
            turned = jnp.dot(values.astype(jnp.bfloat16), flip[...], preferred_element_type=jnp.float32)
            head = jnp.where(lane == 0, ends[which], turned[:, :LANE])
            ends[which] = values[:, :LANE]
            written.append((target, jnp.concatenate([head, turned[:, LANE:]], axis=1)))
        for target, values in written:
            for field in range(2):
                tiles[target, field] = values[field * BAND : (field + 1) * BAND].astype(jnp.bfloat16)
            for copy in place(target, target * TILE):
                copy.start()
    for tile in range(4 * STEPS):
        for copy in place(tile, tile * TILE):
            copy.wait()


def along_z(step):
    return [(4 * x + z, 4 * x + (z + step) % 4) for x in range(4) for z in range(4)]


def along_x(step):
    return [(4 * x + z, 4 * ((x + step) % 4) + z) for x in range(4) for z in range(4)]


def neighbour(step):
    return [(band, band + step) for band in range(BANDS) if 0 <= band + step < BANDS]


SMEM = pl.BlockSpec(memory_space=pltpu.SMEM)
VMEM = pl.BlockSpec(memory_space=pltpu.VMEM)
ANY = pl.BlockSpec(memory_space=pl.ANY)
FETCH = pltpu.CompilerParams(vmem_limit_bytes=FETCH_BYTES)
MIDDLE = pltpu.CompilerParams(vmem_limit_bytes=MIDDLE_BYTES)
SMALL = pltpu.CompilerParams(vmem_limit_bytes=SMALL_BYTES)
LARGE = pltpu.CompilerParams(vmem_limit_bytes=LARGE_BYTES)


def bf16(*shape):
    return jax.ShapeDtypeStruct(shape, jnp.bfloat16)


def make_on_device(table, middle, matrices, expand):
    def on_device(spectra, legendre, wave_order, writer_order):
        packed = pl.pallas_call(
            pack_kernel,
            out_shape=bf16(2 * PAIRS, BLOCKS * LANE),
            in_specs=[SMEM, VMEM],
            out_specs=VMEM,
            scratch_shapes=[
                pltpu.VMEM((5, SLOTS, LANE), jnp.float32),
                pltpu.VMEM((PAIRS, LANE), jnp.int32),
                pltpu.VMEM((PAIRS, LANE), jnp.int32),
            ],
            name="pack",
        )(wave_order, spectra)

        below_z, above_z, across_z = [lax.ppermute(packed, "lat", along_z(step)) for step in (1, 3, 2)]
        firsts = [jnp.stack([packed, below_z]), jnp.stack([above_z, across_z])]
        firsts, legendre = lax.optimization_barrier((firsts, legendre))
        orders, writers, matrix, near = pl.pallas_call(
            fetch_kernel,
            out_shape=[
                jax.ShapeDtypeStruct((NWAVE,), jnp.int32),
                jax.ShapeDtypeStruct((FIELDS,), jnp.int32),
                bf16(BAND, 2 * LANE),
                bf16(PART_SLOTS, BAND, NWAVE),
            ],
            in_specs=[ANY] * 4,
            out_specs=[ANY] * 3 + [VMEM],
            scratch_shapes=[pltpu.SemaphoreType.DMA((4,))],
            compiler_params=FETCH,
            cost_estimate=pl.CostEstimate(flops=0, bytes_accessed=14_000_000, transcendentals=0),
            name="fetch",
        )(wave_order, writer_order, matrices, legendre)
        before = [lax.ppermute(values, "lat", along_x(1)) for values in firsts]
        after = [lax.ppermute(values, "lat", along_x(3)) for values in firsts]
        relayed, near = lax.optimization_barrier(((before[0], after[1]), near))
        opposite = [lax.ppermute(relayed[0], "lat", along_x(1)), lax.ppermute(relayed[1], "lat", along_x(3))]

        lifted, tails = pl.pallas_call(
            legendre_kernel,
            out_shape=[bf16(OWNERS, SLOTS, 4 * LANE), bf16(OWNERS, SLOTS, WIDTH - 4 * LANE)],
            in_specs=[SMEM, SMEM] + [VMEM] * 8 + [VMEM, ANY, VMEM],
            out_specs=[VMEM] * 2,
            scratch_shapes=[
                pltpu.VMEM((BLOCKS, 2 * FIELDS * PAIRS, LANE), jnp.float32),
                pltpu.VMEM((2, 2 * FIELDS * SLOTS, LANE), jnp.float32),
                pltpu.VMEM((2, 2 * FIELDS * SLOTS, LANE), jnp.float32),
                pltpu.VMEM((PART_SLOTS, BAND, NWAVE), jnp.bfloat16),
                pltpu.SemaphoreType.DMA((2,)),
            ],
            compiler_params=MIDDLE,
            cost_estimate=pl.CostEstimate(flops=800_000_000, bytes_accessed=16_000_000, transcendentals=0),
            name="legendre",
        )(orders, writers, *firsts, *before, *after, *opposite, near, legendre, matrix)
        edges = lax.all_to_all(tails, "wave", split_axis=0, concat_axis=0, tiled=True)
        waves = lax.all_to_all(lifted, "wave", split_axis=0, concat_axis=0, tiled=True)

        main, rest = 4 * LANE, 4 * (BAND - LANE)
        chosen, tail, above, below = pl.pallas_call(
            edge_kernel,
            grid=(1,),
            out_shape=[bf16(NWAVE, NWAVE), bf16(rest, NWAVE), bf16(4 * RANK, NWAVE), bf16(4 * RANK, NWAVE)],
            in_specs=[pl.BlockSpec((1, NWAVE), lambda i: (0, 0))]
            + [pl.BlockSpec((NWAVE, WIDTH - main), lambda i: (0, 0))],
            out_specs=[VMEM] * 4,
            compiler_params=SMALL,
            name="edges",
        )(wave_order.reshape(1, NWAVE), edges.reshape(NWAVE, WIDTH - main))
        above = lax.ppermute(above, "lat", neighbour(-1))
        below = lax.ppermute(below, "lat", neighbour(1))
        ordered = pl.pallas_call(
            order_kernel,
            grid=(1,),
            out_shape=bf16(main, NWAVE),
            in_specs=[pl.BlockSpec((NWAVE, NWAVE), lambda i: (0, 0))]
            + [pl.BlockSpec((NWAVE, main), lambda i: (0, 0))],
            out_specs=VMEM,
            compiler_params=SMALL,
            cost_estimate=pl.CostEstimate(flops=800_000_000, bytes_accessed=4_000_000, transcendentals=0),
            name="order",
        )(chosen, waves.reshape(NWAVE, main))
        return pl.pallas_call(
            synthesis_kernel,
            out_shape=bf16(2, BAND, NLON),
            in_specs=[VMEM] * 6 + [ANY],
            out_specs=ANY,
            scratch_shapes=[
                pltpu.VMEM((2, 4 * BAND, NWAVE), jnp.bfloat16),
                pltpu.VMEM((STEPS, 2, NWAVE, TILE), jnp.bfloat16),
                pltpu.VMEM((4 * STEPS, 2, BAND, TILE), jnp.bfloat16),
                pltpu.VMEM((2, 2 * BAND, LANE), jnp.float32),
                pltpu.VMEM((TILE, TILE), jnp.bfloat16),
                pltpu.SemaphoreType.DMA((STEPS,)),
                pltpu.SemaphoreType.DMA((4 * STEPS, 2)),
            ],
            compiler_params=LARGE,
            cost_estimate=pl.CostEstimate(flops=2_400_000_000, bytes_accessed=11_000_000, transcendentals=0),
            name="synthesis",
        )(ordered, tail, above, below, expand, middle, table)

    return on_device


def solution(mesh):
    constants = [*longitude_matrices(), *latitude_matrices()]
    return jax.shard_map(
        make_on_device(*[jnp.asarray(values) for values in constants]),
        mesh=mesh,
        in_specs=(P("lat", None, "wave", None), P("wave", "lat", None), P(), P()),
        out_specs=P("wave", "lat", None),
        check_vma=False,
    )
```

```python
import math

import jax
import jax.numpy as jnp
import ml_dtypes
import numpy as np
from jax import lax
from jax.experimental import pallas as pl
from jax.experimental.pallas import tpu as pltpu
from jax.sharding import PartitionSpec as P

NLAT = 2560
NLON = 5120
NWAVE = 640
WL = 5
BANDS = 16
OWNERS = 8
BAND = NLAT // BANDS
SLOTS = NWAVE // OWNERS
PAIRS = SLOTS // 2
FIELDS = 16
BLOCKS = 6
LANE = 128
HALVES = 2
PART_PAIRS = PAIRS // HALVES
PART_SLOTS = SLOTS // HALVES
RANK = 16
WIDTH = 4 * LANE + 4 * (BAND - LANE + 2 * RANK)
TILE = 256
STEPS = NLON // 4 // TILE
GROUP = 10
SMALL_BYTES = 16 * 2**20
MIDDLE_BYTES = 40 * 2**20
FETCH_BYTES = 44 * 2**20
LARGE_BYTES = 50 * 2**20

LIFT_ALPHA = -1.586134342059924
LIFT_BETA = -0.052980118572961
LIFT_GAMMA = 0.882911075530934
LIFT_DELTA = 0.443506852043971
LIFT_KAPPA = 1.149604398860241


def analyze(values, levels, mode_name):
    if levels == 0:
        return values
    widths = [(4, 4)] + [(0, 0)] * (values.ndim - 1)
    extended = np.pad(values, widths, mode=mode_name)
    even, odd = extended[0::2], extended[1::2]
    first_d = odd[:-1] + LIFT_ALPHA * (even[:-1] + even[1:])
    first_s = even[1:-1] + LIFT_BETA * (first_d[:-1] + first_d[1:])
    second_d = first_d[1:-1] + LIFT_GAMMA * (first_s[:-1] + first_s[1:])
    second_s = first_s[1:-1] + LIFT_DELTA * (second_d[:-1] + second_d[1:])
    result = np.empty_like(values)
    result[0::2] = analyze(second_s * LIFT_KAPPA, levels - 1, mode_name)
    result[1::2] = second_d[1:] / LIFT_KAPPA
    return result


def longitude_matrices():
    waves = np.concatenate([np.arange(0, NWAVE, 2), np.arange(1, NWAVE, 2)])
    phase = waves[:, None] * np.arange(NLON)[None, :] % NLON
    angle = phase * (2.0 * math.pi / NLON)
    weight = np.where(waves == 0, 1.0, 2.0)[:, None] / math.sqrt(2.0 * NWAVE)
    table = np.concatenate([weight * np.cos(angle), -weight * np.sin(angle)], axis=0)
    table = table.astype(np.float32).astype(ml_dtypes.bfloat16).astype(np.float64)
    cosine, sine = analyze(table.T, WL, "wrap").T.reshape(2, NWAVE, NLON)
    half = NWAVE // 2
    both = np.stack([np.concatenate([cosine[:half], sine[half:]]), np.concatenate([sine[:half], cosine[half:]])])
    quarter = both[:, :, : NLON // 4].reshape(2, NWAVE, STEPS, TILE).transpose(2, 0, 1, 3)
    middle = np.zeros((2, NWAVE, LANE))
    middle[:, :, 0] = both[:, :, NLON // 4]
    return [values.astype(np.float32).astype(ml_dtypes.bfloat16) for values in (quarter, middle)]


def latitude_matrices():
    whole = analyze(np.eye(NLAT), WL, "reflect")

    def block(row_band, column_band):
        return whole[row_band * BAND : (row_band + 1) * BAND, column_band * BAND : (column_band + 1) * BAND]

    assert all(np.abs(block(band - 1, band) - block(6, 7)).max() < 1e-12 for band in range(1, BANDS))
    assert all(np.abs(block(band, band - 1) - block(8, 7)).max() < 1e-12 for band in range(1, BANDS))
    inner = whole[:, 7 * BAND : 8 * BAND]
    assert np.abs(inner[: 6 * BAND]).max() == 0 and np.abs(inner[9 * BAND :]).max() == 0
    assert all(np.abs(block(band, band) - block(7, 7)).max() < 1e-12 for band in range(1, BANDS - 1))
    expand = np.zeros((BAND, 2 * RANK))
    project = np.zeros((BAND, 2 * RANK))
    for side, part in enumerate((block(6, 7), block(8, 7))):
        left, sizes, right = np.linalg.svd(part)
        rank = int((sizes > 1e-12).sum())
        assert rank <= RANK
        expand[:, side * RANK : side * RANK + rank] = left[:, :rank] * sizes[:rank]
        project[:, side * RANK : side * RANK + rank] = right[:rank].T
    out = np.zeros((3, BAND, 2 * LANE))
    for variant, band in enumerate((0, 7, BANDS - 1)):
        own = block(band, band).T
        tail = np.concatenate([own[:, LANE:], project], axis=1)
        out[variant] = np.concatenate([own[:, :LANE], tail, tail], axis=1)
    return (
        out.astype(np.float32).astype(ml_dtypes.bfloat16),
        expand.astype(np.float32).astype(ml_dtypes.bfloat16),
    )


def pack_kernel(order_ref, spectra_ref, *refs):
    out_ref, wide, low, high = refs
    first = lax.axis_index("wave") * SLOTS
    for pair in range(PAIRS):
        low[pl.ds(pair, 1), :] = jnp.full((1, LANE), order_ref[first + 2 * pair], jnp.int32)
        high[pl.ds(pair, 1), :] = jnp.full((1, LANE), order_ref[first + 2 * pair + 1], jnp.int32)
    waves_a, waves_b = low[...], high[...]
    lane = lax.broadcasted_iota(jnp.int32, (PAIRS, LANE), 1)
    rows = []
    for part in range(2):
        packed = []
        for block in range(5):
            wide[block] = spectra_ref[0, part, :, block * LANE : (block + 1) * LANE].astype(jnp.float32)
        for block in range(BLOCKS):
            taken = jnp.zeros((PAIRS, LANE), jnp.float32)
            if block <= 4:
                values = wide[4 - block, pl.ds(1, PAIRS, stride=2), :]
                taken = jnp.where(lane + (4 - block) * LANE >= waves_b, values, taken)
            if block >= 1:
                values = wide[block - 1, pl.ds(0, PAIRS, stride=2), :]
                values = jnp.where(lane + (block - 1) * LANE >= waves_a, values, jnp.zeros_like(values))
                taken = jnp.where(waves_a < block * LANE, values, taken)
            packed.append(taken)
        rows.append(jnp.concatenate(packed, axis=1))
    out_ref[...] = jnp.concatenate(rows, axis=0).astype(jnp.bfloat16)


def hand_kernel(order_ref, writer_ref, matrix_ref, order_out, writer_out, matrix_out, sems):
    band = lax.axis_index("lat")
    variant = jnp.where(band == 0, 0, jnp.where(band == BANDS - 1, 2, 1))
    copies = [
        pltpu.make_async_copy(order_ref, order_out, sems.at[0]),
        pltpu.make_async_copy(writer_ref, writer_out, sems.at[1]),
        pltpu.make_async_copy(matrix_ref.at[variant], matrix_out, sems.at[2]),
    ]
    for copy in copies:
        copy.start()
    for copy in copies:
        copy.wait()


def fetch_kernel(legendre_ref, held_out, sem):
    copy = pltpu.make_async_copy(legendre_ref.at[pl.ds(0, PART_SLOTS)], held_out, sem)
    copy.start()
    copy.wait()


def legendre_kernel(order_ref, writer_ref, *refs):
    parts = refs[:8]
    near_ref, legendre_ref, matrix, out_ref, tail_ref = refs[8:13]
    spread, rows, results, rest, sems = refs[13:]
    held = (near_ref, rest)
    some = PART_SLOTS // 2
    copies = [
        pltpu.make_async_copy(
            legendre_ref.at[pl.ds(PART_SLOTS + index * some, some)], rest.at[pl.ds(index * some, some)], sems.at[index]
        )
        for index in range(2)
    ]
    for copy in copies:
        copy.start()
    first = lax.axis_index("wave") * SLOTS
    band = lax.axis_index("lat")
    band_x, band_z = band // 4, lax.rem(band, 4)
    steps = (0, 3, 1, 2)
    for outer in range(4):
        for inner in range(4):
            field = 4 * lax.rem(band_x + steps[outer], 4) + lax.rem(band_z + steps[inner], 4)
            start = pl.multiple_of(field * 2 * PAIRS, 16)
            for block in range(BLOCKS):
                values = parts[2 * outer + inner // 2][inner % 2, :, block * LANE : (block + 1) * LANE]
                spread[block, pl.ds(start, 2 * PAIRS), :] = values.astype(jnp.float32)

    for half in range(HALVES):

        def contract(group, carry, half=half):
            for member in range(GROUP):
                pair = group * GROUP + member
                wave = order_ref[first + half * PART_SLOTS + 2 * pair]
                lower, upper, values_of_n = [], [], []
                for block in range(BLOCKS):
                    values = spread[block, pl.ds(half * PART_PAIRS + pair, 2 * FIELDS, stride=PAIRS), :].astype(jnp.bfloat16)
                    from_a = wave < block * LANE
                    slot = 2 * pair + jnp.where(from_a, 0, 1)
                    source = pl.multiple_of(jnp.where(from_a, block - 1, 4 - block) * LANE, LANE)
                    values_of_n.append(held[half][slot, :, pl.ds(source, LANE)])
                    lower.append(jnp.where(from_a, values, jnp.zeros_like(values)))
                    upper.append(jnp.where(from_a, jnp.zeros_like(values), values))
                left = jnp.concatenate(
                    [jnp.concatenate(lower, axis=1), jnp.concatenate(upper, axis=1)], axis=0
                )
                sums = lax.dot_general(
                    left,
                    jnp.concatenate(values_of_n, axis=1),
                    (((1,), (1,)), ((), ())),
                    preferred_element_type=jnp.float32,
                )
                for which in range(2):
                    piece = sums[which * 2 * FIELDS : (which + 1) * 2 * FIELDS]
                    where = pl.ds(half * PART_SLOTS + 2 * pair + which, 2 * FIELDS, stride=SLOTS)
                    rows[0, where, :] = piece[:, :LANE]
                    rows[1, where, : BAND - LANE] = piece[:, LANE:]
            return carry

        if half:
            for copy in copies:
                copy.wait()
        lax.fori_loop(0, PART_PAIRS // GROUP, contract, 0)

    chunk = 2 * FIELDS * SLOTS // 8
    for index in range(8):
        picked = slice(index * chunk, (index + 1) * chunk)
        left = jnp.concatenate([rows[0, picked, :], rows[1, picked, : BAND - LANE]], axis=1).astype(jnp.bfloat16)
        sums = jnp.dot(left, matrix[...], preferred_element_type=jnp.float32)
        results[0, picked, :] = sums[:, :LANE]
        results[1, picked, :] = sums[:, LANE:]

    lane = lax.broadcasted_iota(jnp.int32, (SLOTS, LANE), 1)
    for owner in range(OWNERS):
        for member in range(2):
            field = writer_ref[2 * owner + member]
            tails = []
            for part in range(2):
                start = pl.multiple_of((2 * field + part) * SLOTS, 8)
                place = (2 * member + part) * LANE
                out_ref[owner, :, place : place + LANE] = results[0, pl.ds(start, SLOTS), :].astype(jnp.bfloat16)
                tails.append(results[1, pl.ds(start, SLOTS), :])
            place = member * LANE
            tail_ref[owner, :, place : place + LANE] = jnp.where(lane < LANE // 2, *tails).astype(jnp.bfloat16)


def edge_kernel(order_ref, waves_ref, chosen_ref, rest_ref, above_ref, below_ref):
    row = lax.broadcasted_iota(jnp.int32, (NWAVE, NWAVE), 0)
    wave = jnp.where(row < NWAVE // 2, 2 * row, 2 * row + 1 - NWAVE)
    chosen_ref[...] = jnp.where(wave == order_ref[...], 1.0, 0.0).astype(jnp.bfloat16)
    ordered = jnp.dot(chosen_ref[...], waves_ref[...], preferred_element_type=jnp.float32)
    turned = ordered.T.astype(jnp.bfloat16)
    rest = BAND - LANE
    for part in range(4):
        start = part * (rest + 2 * RANK)
        rest_ref[part * rest : (part + 1) * rest] = turned[start : start + rest]
        above_ref[part * RANK : (part + 1) * RANK] = turned[start + rest : start + rest + RANK]
        below_ref[part * RANK : (part + 1) * RANK] = turned[start + rest + RANK : start + rest + 2 * RANK]


def order_kernel(chosen_ref, waves_ref, out_ref):
    ordered = jnp.dot(chosen_ref[...], waves_ref[...], preferred_element_type=jnp.float32)
    out_ref[...] = ordered.T.astype(jnp.bfloat16)


def synthesis_kernel(main_ref, rest_ref, above_ref, below_ref, expand_ref, middle_ref, table_ref, out_ref, *refs):
    left, table, tiles, ends, flip, table_sems, out_sems = refs
    tables = [pltpu.make_async_copy(table_ref.at[step], table.at[step], table_sems.at[step]) for step in range(STEPS)]
    for copy in reversed(tables):
        copy.start()
    rest = BAND - LANE
    rows = 2 * BAND
    low = lax.broadcasted_iota(jnp.int32, (BAND, NWAVE), 1) < NWAVE // 2
    for field in range(2):
        summed = []
        for part in range(2):
            which = 2 * field + part
            edges = slice(which * RANK, (which + 1) * RANK)
            added = jnp.dot(
                expand_ref[...],
                jnp.concatenate([above_ref[edges], below_ref[edges]], axis=0),
                preferred_element_type=jnp.float32,
            )
            own = [main_ref[which * LANE : (which + 1) * LANE], rest_ref[which * rest : (which + 1) * rest]]
            summed.append(jnp.concatenate(own, axis=0).astype(jnp.float32) + added)
        cosine, sine = summed
        for turned, value in enumerate((sine, -sine)):
            picked = slice(turned * rows + field * BAND, turned * rows + (field + 1) * BAND)
            left[0, picked] = jnp.where(low, cosine, value).astype(jnp.bfloat16)
            left[1, picked] = jnp.where(low, value, cosine).astype(jnp.bfloat16)
    total = lax.broadcasted_iota(jnp.int32, (TILE, TILE), 0) + lax.broadcasted_iota(jnp.int32, (TILE, TILE), 1)
    flip[...] = jnp.where(total == TILE, 1.0, 0.0).astype(jnp.bfloat16)

    def products(first, second):
        a = jnp.dot(left[0], first, preferred_element_type=jnp.float32)
        b = jnp.dot(left[1], second, preferred_element_type=jnp.float32)
        return a[:rows] + b[:rows], a[:rows] - b[:rows], a[rows:] - b[rows:], a[rows:] + b[rows:]

    _, ends[0], _, ends[1] = products(middle_ref[0], middle_ref[1])

    def place(tile, where):
        return [
            pltpu.make_async_copy(
                tiles.at[tile, field],
                out_ref.at[field, :, pl.ds(where, TILE)],
                out_sems.at[tile, field],
            )
            for field in range(2)
        ]

    lane = lax.broadcasted_iota(jnp.int32, (rows, LANE), 1)
    for tile in reversed(range(STEPS)):
        tables[tile].wait()
        east, back, south, west = products(table[tile, 0], table[tile, 1])
        written = [(tile, east), (2 * STEPS + tile, south)]
        for which, (values, target) in enumerate(((back, 2 * STEPS - 1 - tile), (west, 4 * STEPS - 1 - tile))):
            turned = jnp.dot(values.astype(jnp.bfloat16), flip[...], preferred_element_type=jnp.float32)
            head = jnp.where(lane == 0, ends[which], turned[:, :LANE])
            ends[which] = values[:, :LANE]
            written.append((target, jnp.concatenate([head, turned[:, LANE:]], axis=1)))
        for target, values in written:
            for field in range(2):
                tiles[target, field] = values[field * BAND : (field + 1) * BAND].astype(jnp.bfloat16)
            for copy in place(target, target * TILE):
                copy.start()
    for tile in range(4 * STEPS):
        for copy in place(tile, tile * TILE):
            copy.wait()


def along_z(step):
    return [(4 * x + z, 4 * x + (z + step) % 4) for x in range(4) for z in range(4)]


def along_x(step):
    return [(4 * x + z, 4 * ((x + step) % 4) + z) for x in range(4) for z in range(4)]


def neighbour(step):
    return [(band, band + step) for band in range(BANDS) if 0 <= band + step < BANDS]


SMEM = pl.BlockSpec(memory_space=pltpu.SMEM)
VMEM = pl.BlockSpec(memory_space=pltpu.VMEM)
ANY = pl.BlockSpec(memory_space=pl.ANY)
FETCH = pltpu.CompilerParams(vmem_limit_bytes=FETCH_BYTES)
MIDDLE = pltpu.CompilerParams(vmem_limit_bytes=MIDDLE_BYTES)
SMALL = pltpu.CompilerParams(vmem_limit_bytes=SMALL_BYTES)
LARGE = pltpu.CompilerParams(vmem_limit_bytes=LARGE_BYTES)


def bf16(*shape):
    return jax.ShapeDtypeStruct(shape, jnp.bfloat16)


def make_on_device(table, middle, matrices, expand):
    def on_device(spectra, legendre, wave_order, writer_order):
        packed = pl.pallas_call(
            pack_kernel,
            out_shape=bf16(2 * PAIRS, BLOCKS * LANE),
            in_specs=[SMEM, VMEM],
            out_specs=VMEM,
            scratch_shapes=[
                pltpu.VMEM((5, SLOTS, LANE), jnp.float32),
                pltpu.VMEM((PAIRS, LANE), jnp.int32),
                pltpu.VMEM((PAIRS, LANE), jnp.int32),
            ],
            name="pack",
        )(wave_order, spectra)

        below_z, above_z, across_z = [lax.ppermute(packed, "lat", along_z(step)) for step in (1, 3, 2)]
        firsts = [jnp.stack([packed, below_z]), jnp.stack([above_z, across_z])]
        small = pl.pallas_call(
            hand_kernel,
            out_shape=[
                jax.ShapeDtypeStruct((NWAVE,), jnp.int32),
                jax.ShapeDtypeStruct((FIELDS,), jnp.int32),
                bf16(BAND, 2 * LANE),
            ],
            in_specs=[ANY] * 3,
            out_specs=[ANY] * 3,
            scratch_shapes=[pltpu.SemaphoreType.DMA((3,))],
            compiler_params=FETCH,
            cost_estimate=pl.CostEstimate(flops=0, bytes_accessed=6_000_000, transcendentals=0),
            name="hand",
        )(wave_order, writer_order, matrices)
        firsts, legendre, small = lax.optimization_barrier((firsts, legendre, small))
        orders, writers, matrix = small
        near = pl.pallas_call(
            fetch_kernel,
            out_shape=bf16(PART_SLOTS, BAND, NWAVE),
            in_specs=[ANY],
            out_specs=VMEM,
            scratch_shapes=[pltpu.SemaphoreType.DMA],
            compiler_params=FETCH,
            cost_estimate=pl.CostEstimate(flops=0, bytes_accessed=14_000_000, transcendentals=0),
            name="fetch",
        )(legendre)
        before = [lax.ppermute(values, "lat", along_x(1)) for values in firsts]
        after = [lax.ppermute(values, "lat", along_x(3)) for values in firsts]
        relayed, near = lax.optimization_barrier(((before[0], after[1]), near))
        opposite = [lax.ppermute(relayed[0], "lat", along_x(1)), lax.ppermute(relayed[1], "lat", along_x(3))]

        lifted, tails = pl.pallas_call(
            legendre_kernel,
            out_shape=[bf16(OWNERS, SLOTS, 4 * LANE), bf16(OWNERS, SLOTS, WIDTH - 4 * LANE)],
            in_specs=[SMEM, SMEM] + [VMEM] * 8 + [VMEM, ANY, VMEM],
            out_specs=[VMEM] * 2,
            scratch_shapes=[
                pltpu.VMEM((BLOCKS, 2 * FIELDS * PAIRS, LANE), jnp.float32),
                pltpu.VMEM((2, 2 * FIELDS * SLOTS, LANE), jnp.float32),
                pltpu.VMEM((2, 2 * FIELDS * SLOTS, LANE), jnp.float32),
                pltpu.VMEM((PART_SLOTS, BAND, NWAVE), jnp.bfloat16),
                pltpu.SemaphoreType.DMA((2,)),
            ],
            compiler_params=MIDDLE,
            cost_estimate=pl.CostEstimate(flops=800_000_000, bytes_accessed=16_000_000, transcendentals=0),
            name="legendre",
        )(orders, writers, *firsts, *before, *after, *opposite, near, legendre, matrix)
        edges = lax.all_to_all(tails, "wave", split_axis=0, concat_axis=0, tiled=True)
        waves = lax.all_to_all(lifted, "wave", split_axis=0, concat_axis=0, tiled=True)

        main, rest = 4 * LANE, 4 * (BAND - LANE)
        chosen, tail, above, below = pl.pallas_call(
            edge_kernel,
            grid=(1,),
            out_shape=[bf16(NWAVE, NWAVE), bf16(rest, NWAVE), bf16(4 * RANK, NWAVE), bf16(4 * RANK, NWAVE)],
            in_specs=[pl.BlockSpec((1, NWAVE), lambda i: (0, 0))]
            + [pl.BlockSpec((NWAVE, WIDTH - main), lambda i: (0, 0))],
            out_specs=[VMEM] * 4,
            compiler_params=SMALL,
            name="edges",
        )(wave_order.reshape(1, NWAVE), edges.reshape(NWAVE, WIDTH - main))
        above = lax.ppermute(above, "lat", neighbour(-1))
        below = lax.ppermute(below, "lat", neighbour(1))
        ordered = pl.pallas_call(
            order_kernel,
            grid=(1,),
            out_shape=bf16(main, NWAVE),
            in_specs=[pl.BlockSpec((NWAVE, NWAVE), lambda i: (0, 0))]
            + [pl.BlockSpec((NWAVE, main), lambda i: (0, 0))],
            out_specs=VMEM,
            compiler_params=SMALL,
            cost_estimate=pl.CostEstimate(flops=800_000_000, bytes_accessed=4_000_000, transcendentals=0),
            name="order",
        )(chosen, waves.reshape(NWAVE, main))
        return pl.pallas_call(
            synthesis_kernel,
            out_shape=bf16(2, BAND, NLON),
            in_specs=[VMEM] * 6 + [ANY],
            out_specs=ANY,
            scratch_shapes=[
                pltpu.VMEM((2, 4 * BAND, NWAVE), jnp.bfloat16),
                pltpu.VMEM((STEPS, 2, NWAVE, TILE), jnp.bfloat16),
                pltpu.VMEM((4 * STEPS, 2, BAND, TILE), jnp.bfloat16),
                pltpu.VMEM((2, 2 * BAND, LANE), jnp.float32),
                pltpu.VMEM((TILE, TILE), jnp.bfloat16),
                pltpu.SemaphoreType.DMA((STEPS,)),
                pltpu.SemaphoreType.DMA((4 * STEPS, 2)),
            ],
            compiler_params=LARGE,
            cost_estimate=pl.CostEstimate(flops=2_400_000_000, bytes_accessed=11_000_000, transcendentals=0),
            name="synthesis",
        )(ordered, tail, above, below, expand, middle, table)

    return on_device


def solution(mesh):
    constants = [*longitude_matrices(), *latitude_matrices()]
    return jax.shard_map(
        make_on_device(*[jnp.asarray(values) for values in constants]),
        mesh=mesh,
        in_specs=(P("lat", None, "wave", None), P("wave", "lat", None), P(), P()),
        out_specs=P("wave", "lat", None),
        check_vma=False,
    )
```

```python
import math

import jax
import jax.numpy as jnp
import ml_dtypes
import numpy as np
from jax import lax
from jax.experimental import pallas as pl
from jax.experimental.pallas import tpu as pltpu
from jax.sharding import PartitionSpec as P

NLAT = 2560
NLON = 5120
NWAVE = 640
WL = 5
BANDS = 16
OWNERS = 8
BAND = NLAT // BANDS
SLOTS = NWAVE // OWNERS
PAIRS = SLOTS // 2
FIELDS = 16
BLOCKS = 6
LANE = 128
HALVES = 2
PART_PAIRS = PAIRS // HALVES
PART_SLOTS = SLOTS // HALVES
RANK = 16
WIDTH = 4 * LANE + 4 * (BAND - LANE + 2 * RANK)
TILE = 256
STEPS = NLON // 4 // TILE
GROUP = 10
SMALL_BYTES = 16 * 2**20
MIDDLE_BYTES = 40 * 2**20
FETCH_BYTES = 44 * 2**20
LARGE_BYTES = 50 * 2**20

LIFT_ALPHA = -1.586134342059924
LIFT_BETA = -0.052980118572961
LIFT_GAMMA = 0.882911075530934
LIFT_DELTA = 0.443506852043971
LIFT_KAPPA = 1.149604398860241


def analyze(values, levels, mode_name):
    if levels == 0:
        return values
    widths = [(4, 4)] + [(0, 0)] * (values.ndim - 1)
    extended = np.pad(values, widths, mode=mode_name)
    even, odd = extended[0::2], extended[1::2]
    first_d = odd[:-1] + LIFT_ALPHA * (even[:-1] + even[1:])
    first_s = even[1:-1] + LIFT_BETA * (first_d[:-1] + first_d[1:])
    second_d = first_d[1:-1] + LIFT_GAMMA * (first_s[:-1] + first_s[1:])
    second_s = first_s[1:-1] + LIFT_DELTA * (second_d[:-1] + second_d[1:])
    result = np.empty_like(values)
    result[0::2] = analyze(second_s * LIFT_KAPPA, levels - 1, mode_name)
    result[1::2] = second_d[1:] / LIFT_KAPPA
    return result


def longitude_matrices():
    waves = np.concatenate([np.arange(0, NWAVE, 2), np.arange(1, NWAVE, 2)])
    phase = waves[:, None] * np.arange(NLON)[None, :] % NLON
    angle = phase * (2.0 * math.pi / NLON)
    weight = np.where(waves == 0, 1.0, 2.0)[:, None] / math.sqrt(2.0 * NWAVE)
    table = np.concatenate([weight * np.cos(angle), -weight * np.sin(angle)], axis=0)
    table = table.astype(np.float32).astype(ml_dtypes.bfloat16).astype(np.float64)
    cosine, sine = analyze(table.T, WL, "wrap").T.reshape(2, NWAVE, NLON)
    half = NWAVE // 2
    both = np.stack([np.concatenate([cosine[:half], sine[half:]]), np.concatenate([sine[:half], cosine[half:]])])
    quarter = both[:, :, : NLON // 4].reshape(2, NWAVE, STEPS, TILE).transpose(2, 0, 1, 3)
    middle = np.zeros((2, NWAVE, LANE))
    middle[:, :, 0] = both[:, :, NLON // 4]
    return [values.astype(np.float32).astype(ml_dtypes.bfloat16) for values in (quarter, middle)]


def latitude_matrices():
    whole = analyze(np.eye(NLAT), WL, "reflect")

    def block(row_band, column_band):
        return whole[row_band * BAND : (row_band + 1) * BAND, column_band * BAND : (column_band + 1) * BAND]

    assert all(np.abs(block(band - 1, band) - block(6, 7)).max() < 1e-12 for band in range(1, BANDS))
    assert all(np.abs(block(band, band - 1) - block(8, 7)).max() < 1e-12 for band in range(1, BANDS))
    inner = whole[:, 7 * BAND : 8 * BAND]
    assert np.abs(inner[: 6 * BAND]).max() == 0 and np.abs(inner[9 * BAND :]).max() == 0
    assert all(np.abs(block(band, band) - block(7, 7)).max() < 1e-12 for band in range(1, BANDS - 1))
    expand = np.zeros((BAND, 2 * RANK))
    project = np.zeros((BAND, 2 * RANK))
    for side, part in enumerate((block(6, 7), block(8, 7))):
        left, sizes, right = np.linalg.svd(part)
        rank = int((sizes > 1e-12).sum())
        assert rank <= RANK
        expand[:, side * RANK : side * RANK + rank] = left[:, :rank] * sizes[:rank]
        project[:, side * RANK : side * RANK + rank] = right[:rank].T
    out = np.zeros((3, BAND, 2 * LANE))
    for variant, band in enumerate((0, 7, BANDS - 1)):
        own = block(band, band).T
        tail = np.concatenate([own[:, LANE:], project], axis=1)
        out[variant] = np.concatenate([own[:, :LANE], tail, tail], axis=1)
    return (
        out.astype(np.float32).astype(ml_dtypes.bfloat16),
        expand.astype(np.float32).astype(ml_dtypes.bfloat16),
    )


def pack_kernel(order_ref, spectra_ref, *refs):
    out_ref, wide, low, high = refs
    first = lax.axis_index("wave") * SLOTS
    for pair in range(PAIRS):
        low[pl.ds(pair, 1), :] = jnp.full((1, LANE), order_ref[first + 2 * pair], jnp.int32)
        high[pl.ds(pair, 1), :] = jnp.full((1, LANE), order_ref[first + 2 * pair + 1], jnp.int32)
    waves_a, waves_b = low[...], high[...]
    lane = lax.broadcasted_iota(jnp.int32, (PAIRS, LANE), 1)
    rows = []
    for part in range(2):
        packed = []
        for block in range(5):
            wide[block] = spectra_ref[0, part, :, block * LANE : (block + 1) * LANE].astype(jnp.float32)
        for block in range(BLOCKS):
            taken = jnp.zeros((PAIRS, LANE), jnp.float32)
            if block <= 4:
                values = wide[4 - block, pl.ds(1, PAIRS, stride=2), :]
                taken = jnp.where(lane + (4 - block) * LANE >= waves_b, values, taken)
            if block >= 1:
                values = wide[block - 1, pl.ds(0, PAIRS, stride=2), :]
                values = jnp.where(lane + (block - 1) * LANE >= waves_a, values, jnp.zeros_like(values))
                taken = jnp.where(waves_a < block * LANE, values, taken)
            packed.append(taken)
        rows.append(jnp.concatenate(packed, axis=1))
    out_ref[...] = jnp.concatenate(rows, axis=0).astype(jnp.bfloat16)


def hand_kernel(order_ref, writer_ref, matrix_ref, order_out, writer_out, matrix_out, sems):
    band = lax.axis_index("lat")
    variant = jnp.where(band == 0, 0, jnp.where(band == BANDS - 1, 2, 1))
    copies = [
        pltpu.make_async_copy(order_ref, order_out, sems.at[0]),
        pltpu.make_async_copy(writer_ref, writer_out, sems.at[1]),
        pltpu.make_async_copy(matrix_ref.at[variant], matrix_out, sems.at[2]),
    ]
    for copy in copies:
        copy.start()
    for copy in copies:
        copy.wait()


def fetch_kernel(legendre_ref, held_out, sem):
    copy = pltpu.make_async_copy(legendre_ref.at[pl.ds(0, PART_SLOTS)], held_out, sem)
    copy.start()
    copy.wait()


def legendre_kernel(order_ref, writer_ref, *refs):
    parts = refs[:8]
    near_ref, legendre_ref, matrix, out_ref, tail_ref = refs[8:13]
    spread, rows, results, rest, sems = refs[13:]
    held = (near_ref, rest)
    some = PART_SLOTS // 2
    copies = [
        pltpu.make_async_copy(
            legendre_ref.at[pl.ds(PART_SLOTS + index * some, some)], rest.at[pl.ds(index * some, some)], sems.at[index]
        )
        for index in range(2)
    ]
    for copy in copies:
        copy.start()
    first = lax.axis_index("wave") * SLOTS
    band = lax.axis_index("lat")
    band_x, band_z = band // 4, lax.rem(band, 4)
    steps = (0, 3, 1, 2)
    for outer in range(4):
        for inner in range(4):
            field = 4 * lax.rem(band_x + steps[outer], 4) + lax.rem(band_z + steps[inner], 4)
            start = pl.multiple_of(field * 2 * PAIRS, 16)
            for block in range(BLOCKS):
                values = parts[2 * outer + inner // 2][inner % 2, :, block * LANE : (block + 1) * LANE]
                spread[block, pl.ds(start, 2 * PAIRS), :] = values.astype(jnp.float32)

    for half in range(HALVES):

        def contract(group, carry, half=half):
            for member in range(GROUP):
                pair = group * GROUP + member
                wave = order_ref[first + half * PART_SLOTS + 2 * pair]
                lower, upper, values_of_n = [], [], []
                for block in range(BLOCKS):
                    values = spread[block, pl.ds(half * PART_PAIRS + pair, 2 * FIELDS, stride=PAIRS), :].astype(jnp.bfloat16)
                    from_a = wave < block * LANE
                    slot = 2 * pair + jnp.where(from_a, 0, 1)
                    source = pl.multiple_of(jnp.where(from_a, block - 1, 4 - block) * LANE, LANE)
                    values_of_n.append(held[half][slot, :, pl.ds(source, LANE)])
                    lower.append(jnp.where(from_a, values, jnp.zeros_like(values)))
                    upper.append(jnp.where(from_a, jnp.zeros_like(values), values))
                left = jnp.concatenate(
                    [jnp.concatenate(lower, axis=1), jnp.concatenate(upper, axis=1)], axis=0
                )
                sums = lax.dot_general(
                    left,
                    jnp.concatenate(values_of_n, axis=1),
                    (((1,), (1,)), ((), ())),
                    preferred_element_type=jnp.float32,
                )
                for which in range(2):
                    piece = sums[which * 2 * FIELDS : (which + 1) * 2 * FIELDS]
                    where = pl.ds(half * PART_SLOTS + 2 * pair + which, 2 * FIELDS, stride=SLOTS)
                    rows[0, where, :] = piece[:, :LANE]
                    rows[1, where, : BAND - LANE] = piece[:, LANE:]
            return carry

        if half:
            for copy in copies:
                copy.wait()
        lax.fori_loop(0, PART_PAIRS // GROUP, contract, 0)

    chunk = 2 * FIELDS * SLOTS // 8
    for index in range(8):
        picked = slice(index * chunk, (index + 1) * chunk)
        left = jnp.concatenate([rows[0, picked, :], rows[1, picked, : BAND - LANE]], axis=1).astype(jnp.bfloat16)
        sums = jnp.dot(left, matrix[...], preferred_element_type=jnp.float32)
        out_ref[picked, :] = sums[:, :LANE].astype(jnp.bfloat16)
        results[picked, :] = sums[:, LANE:]

    lane = lax.broadcasted_iota(jnp.int32, (SLOTS, LANE), 1)
    for owner in range(OWNERS):
        for member in range(2):
            field = writer_ref[2 * owner + member]
            tails = []
            for part in range(2):
                start = pl.multiple_of((2 * field + part) * SLOTS, 8)
                tails.append(results[pl.ds(start, SLOTS), :])
            place = member * LANE
            tail_ref[owner, :, place : place + LANE] = jnp.where(lane < LANE // 2, *tails).astype(jnp.bfloat16)


def sort_kernel(writer_ref, order_ref, rows_ref, out_ref, chosen_ref):
    row = lax.broadcasted_iota(jnp.int32, (NWAVE, NWAVE), 0)
    wave = jnp.where(row < NWAVE // 2, 2 * row, 2 * row + 1 - NWAVE)
    chosen_ref[...] = jnp.where(wave == order_ref[...], 1.0, 0.0).astype(jnp.bfloat16)
    for owner in range(OWNERS):
        for which in range(4):
            start = pl.multiple_of((2 * writer_ref[2 * owner + which // 2] + which % 2) * SLOTS, 16)
            out_ref[owner, :, which * LANE : (which + 1) * LANE] = rows_ref[pl.ds(start, SLOTS), :]


def edge_kernel(chosen_ref, waves_ref, rest_ref, above_ref, below_ref):
    ordered = jnp.dot(chosen_ref[...], waves_ref[...], preferred_element_type=jnp.float32)
    turned = ordered.T.astype(jnp.bfloat16)
    rest = BAND - LANE
    for part in range(4):
        start = part * (rest + 2 * RANK)
        rest_ref[part * rest : (part + 1) * rest] = turned[start : start + rest]
        above_ref[part * RANK : (part + 1) * RANK] = turned[start + rest : start + rest + RANK]
        below_ref[part * RANK : (part + 1) * RANK] = turned[start + rest + RANK : start + rest + 2 * RANK]


def order_kernel(chosen_ref, waves_ref, out_ref):
    ordered = jnp.dot(chosen_ref[...], waves_ref[...], preferred_element_type=jnp.float32)
    out_ref[...] = ordered.T.astype(jnp.bfloat16)


def synthesis_kernel(main_ref, rest_ref, above_ref, below_ref, expand_ref, middle_ref, table_ref, out_ref, *refs):
    left, table, tiles, ends, flip, table_sems, out_sems = refs
    tables = [pltpu.make_async_copy(table_ref.at[step], table.at[step], table_sems.at[step]) for step in range(STEPS)]
    for copy in reversed(tables):
        copy.start()
    rest = BAND - LANE
    rows = 2 * BAND
    low = lax.broadcasted_iota(jnp.int32, (BAND, NWAVE), 1) < NWAVE // 2
    for field in range(2):
        summed = []
        for part in range(2):
            which = 2 * field + part
            edges = slice(which * RANK, (which + 1) * RANK)
            added = jnp.dot(
                expand_ref[...],
                jnp.concatenate([above_ref[edges], below_ref[edges]], axis=0),
                preferred_element_type=jnp.float32,
            )
            own = [main_ref[which * LANE : (which + 1) * LANE], rest_ref[which * rest : (which + 1) * rest]]
            summed.append(jnp.concatenate(own, axis=0).astype(jnp.float32) + added)
        cosine, sine = summed
        for turned, value in enumerate((sine, -sine)):
            picked = slice(turned * rows + field * BAND, turned * rows + (field + 1) * BAND)
            left[0, picked] = jnp.where(low, cosine, value).astype(jnp.bfloat16)
            left[1, picked] = jnp.where(low, value, cosine).astype(jnp.bfloat16)
    total = lax.broadcasted_iota(jnp.int32, (TILE, TILE), 0) + lax.broadcasted_iota(jnp.int32, (TILE, TILE), 1)
    flip[...] = jnp.where(total == TILE, 1.0, 0.0).astype(jnp.bfloat16)

    def products(first, second):
        a = jnp.dot(left[0], first, preferred_element_type=jnp.float32)
        b = jnp.dot(left[1], second, preferred_element_type=jnp.float32)
        return a[:rows] + b[:rows], a[:rows] - b[:rows], a[rows:] - b[rows:], a[rows:] + b[rows:]

    _, ends[0], _, ends[1] = products(middle_ref[0], middle_ref[1])

    def place(tile, where):
        return [
            pltpu.make_async_copy(
                tiles.at[tile, field],
                out_ref.at[field, :, pl.ds(where, TILE)],
                out_sems.at[tile, field],
            )
            for field in range(2)
        ]

    lane = lax.broadcasted_iota(jnp.int32, (rows, LANE), 1)
    for tile in reversed(range(STEPS)):
        tables[tile].wait()
        east, back, south, west = products(table[tile, 0], table[tile, 1])
        written = [(tile, east), (2 * STEPS + tile, south)]
        for which, (values, target) in enumerate(((back, 2 * STEPS - 1 - tile), (west, 4 * STEPS - 1 - tile))):
            turned = jnp.dot(values.astype(jnp.bfloat16), flip[...], preferred_element_type=jnp.float32)
            head = jnp.where(lane == 0, ends[which], turned[:, :LANE])
            ends[which] = values[:, :LANE]
            written.append((target, jnp.concatenate([head, turned[:, LANE:]], axis=1)))
        for target, values in written:
            for field in range(2):
                tiles[target, field] = values[field * BAND : (field + 1) * BAND].astype(jnp.bfloat16)
            for copy in place(target, target * TILE):
                copy.start()
    for tile in range(4 * STEPS):
        for copy in place(tile, tile * TILE):
            copy.wait()


def along_z(step):
    return [(4 * x + z, 4 * x + (z + step) % 4) for x in range(4) for z in range(4)]


def along_x(step):
    return [(4 * x + z, 4 * ((x + step) % 4) + z) for x in range(4) for z in range(4)]


def neighbour(step):
    return [(band, band + step) for band in range(BANDS) if 0 <= band + step < BANDS]


SMEM = pl.BlockSpec(memory_space=pltpu.SMEM)
VMEM = pl.BlockSpec(memory_space=pltpu.VMEM)
ANY = pl.BlockSpec(memory_space=pl.ANY)
FETCH = pltpu.CompilerParams(vmem_limit_bytes=FETCH_BYTES)
MIDDLE = pltpu.CompilerParams(vmem_limit_bytes=MIDDLE_BYTES)
SMALL = pltpu.CompilerParams(vmem_limit_bytes=SMALL_BYTES)
LARGE = pltpu.CompilerParams(vmem_limit_bytes=LARGE_BYTES)


def bf16(*shape):
    return jax.ShapeDtypeStruct(shape, jnp.bfloat16)


def make_on_device(table, middle, matrices, expand):
    def on_device(spectra, legendre, wave_order, writer_order):
        packed = pl.pallas_call(
            pack_kernel,
            out_shape=bf16(2 * PAIRS, BLOCKS * LANE),
            in_specs=[SMEM, VMEM],
            out_specs=VMEM,
            scratch_shapes=[
                pltpu.VMEM((5, SLOTS, LANE), jnp.float32),
                pltpu.VMEM((PAIRS, LANE), jnp.int32),
                pltpu.VMEM((PAIRS, LANE), jnp.int32),
            ],
            name="pack",
        )(wave_order, spectra)

        below_z, above_z, across_z = [lax.ppermute(packed, "lat", along_z(step)) for step in (1, 3, 2)]
        firsts = [jnp.stack([packed, below_z]), jnp.stack([above_z, across_z])]
        small = pl.pallas_call(
            hand_kernel,
            out_shape=[
                jax.ShapeDtypeStruct((NWAVE,), jnp.int32),
                jax.ShapeDtypeStruct((FIELDS,), jnp.int32),
                bf16(BAND, 2 * LANE),
            ],
            in_specs=[ANY] * 3,
            out_specs=[ANY] * 3,
            scratch_shapes=[pltpu.SemaphoreType.DMA((3,))],
            compiler_params=FETCH,
            cost_estimate=pl.CostEstimate(flops=0, bytes_accessed=6_000_000, transcendentals=0),
            name="hand",
        )(wave_order, writer_order, matrices)
        firsts, legendre, small = lax.optimization_barrier((firsts, legendre, small))
        orders, writers, matrix = small
        near = pl.pallas_call(
            fetch_kernel,
            out_shape=bf16(PART_SLOTS, BAND, NWAVE),
            in_specs=[ANY],
            out_specs=VMEM,
            scratch_shapes=[pltpu.SemaphoreType.DMA],
            compiler_params=FETCH,
            cost_estimate=pl.CostEstimate(flops=0, bytes_accessed=14_000_000, transcendentals=0),
            name="fetch",
        )(legendre)
        before = [lax.ppermute(values, "lat", along_x(1)) for values in firsts]
        after = [lax.ppermute(values, "lat", along_x(3)) for values in firsts]
        relayed, near = lax.optimization_barrier(((before[0], after[1]), near))
        opposite = [lax.ppermute(relayed[0], "lat", along_x(1)), lax.ppermute(relayed[1], "lat", along_x(3))]

        in_order, tails = pl.pallas_call(
            legendre_kernel,
            out_shape=[bf16(2 * FIELDS * SLOTS, LANE), bf16(OWNERS, SLOTS, WIDTH - 4 * LANE)],
            in_specs=[SMEM, SMEM] + [VMEM] * 8 + [VMEM, ANY, VMEM],
            out_specs=[VMEM] * 2,
            scratch_shapes=[
                pltpu.VMEM((BLOCKS, 2 * FIELDS * PAIRS, LANE), jnp.float32),
                pltpu.VMEM((2, 2 * FIELDS * SLOTS, LANE), jnp.float32),
                pltpu.VMEM((2 * FIELDS * SLOTS, LANE), jnp.float32),
                pltpu.VMEM((PART_SLOTS, BAND, NWAVE), jnp.bfloat16),
                pltpu.SemaphoreType.DMA((2,)),
            ],
            compiler_params=MIDDLE,
            cost_estimate=pl.CostEstimate(flops=800_000_000, bytes_accessed=16_000_000, transcendentals=0),
            name="legendre",
        )(orders, writers, *firsts, *before, *after, *opposite, near, legendre, matrix)
        lifted, chosen = pl.pallas_call(
            sort_kernel,
            out_shape=[bf16(OWNERS, SLOTS, 4 * LANE), bf16(NWAVE, NWAVE)],
            in_specs=[SMEM, VMEM, VMEM],
            out_specs=[VMEM] * 2,
            compiler_params=SMALL,
            cost_estimate=pl.CostEstimate(flops=0, bytes_accessed=6_000_000, transcendentals=0),
            name="sort",
        )(writers, wave_order.reshape(1, NWAVE), in_order)
        edges = lax.all_to_all(tails, "wave", split_axis=0, concat_axis=0, tiled=True)
        waves = lax.all_to_all(lifted, "wave", split_axis=0, concat_axis=0, tiled=True)

        main, rest = 4 * LANE, 4 * (BAND - LANE)
        tail, above, below = pl.pallas_call(
            edge_kernel,
            grid=(1,),
            out_shape=[bf16(rest, NWAVE), bf16(4 * RANK, NWAVE), bf16(4 * RANK, NWAVE)],
            in_specs=[pl.BlockSpec((NWAVE, NWAVE), lambda i: (0, 0))]
            + [pl.BlockSpec((NWAVE, WIDTH - main), lambda i: (0, 0))],
            out_specs=[VMEM] * 3,
            compiler_params=SMALL,
            name="edges",
        )(chosen, edges.reshape(NWAVE, WIDTH - main))
        above = lax.ppermute(above, "lat", neighbour(-1))
        below = lax.ppermute(below, "lat", neighbour(1))
        ordered = pl.pallas_call(
            order_kernel,
            grid=(1,),
            out_shape=bf16(main, NWAVE),
            in_specs=[pl.BlockSpec((NWAVE, NWAVE), lambda i: (0, 0))]
            + [pl.BlockSpec((NWAVE, main), lambda i: (0, 0))],
            out_specs=VMEM,
            compiler_params=SMALL,
            cost_estimate=pl.CostEstimate(flops=800_000_000, bytes_accessed=4_000_000, transcendentals=0),
            name="order",
        )(chosen, waves.reshape(NWAVE, main))
        return pl.pallas_call(
            synthesis_kernel,
            out_shape=bf16(2, BAND, NLON),
            in_specs=[VMEM] * 6 + [ANY],
            out_specs=ANY,
            scratch_shapes=[
                pltpu.VMEM((2, 4 * BAND, NWAVE), jnp.bfloat16),
                pltpu.VMEM((STEPS, 2, NWAVE, TILE), jnp.bfloat16),
                pltpu.VMEM((4 * STEPS, 2, BAND, TILE), jnp.bfloat16),
                pltpu.VMEM((2, 2 * BAND, LANE), jnp.float32),
                pltpu.VMEM((TILE, TILE), jnp.bfloat16),
                pltpu.SemaphoreType.DMA((STEPS,)),
                pltpu.SemaphoreType.DMA((4 * STEPS, 2)),
            ],
            compiler_params=LARGE,
            cost_estimate=pl.CostEstimate(flops=2_400_000_000, bytes_accessed=11_000_000, transcendentals=0),
            name="synthesis",
        )(ordered, tail, above, below, expand, middle, table)

    return on_device


def solution(mesh):
    constants = [*longitude_matrices(), *latitude_matrices()]
    return jax.shard_map(
        make_on_device(*[jnp.asarray(values) for values in constants]),
        mesh=mesh,
        in_specs=(P("lat", None, "wave", None), P("wave", "lat", None), P(), P()),
        out_specs=P("wave", "lat", None),
        check_vma=False,
    )
```
